128 devices in a mesh: dp: 16 (over x, z), expert: 2 (over core), ffn: 4 (over y).
Axes of the slice: x: 4, y: 4, z: 4, core: 2. Of those that a mesh axis runs over, the one named last changes fastest.
Arguments:
- tokens: bfloat16 [256, 256, 768], P(('dp', 'expert', 'ffn')), may hold values from -6 to 6
- cotangent: bfloat16 [256, 256, 768], P(('dp', 'expert', 'ffn')), may hold values from -6 to 6
- modality: int32 [256, 256], P(('dp', 'expert', 'ffn')), may hold values from 0 to 2, as said below
- ln1_gain: bfloat16 [768], replicated, may hold values from 0.25 to 1.75
- ln1_shift: bfloat16 [768], replicated, may hold values from -1.75 to 1.75
- w_query: bfloat16 [768, 768], replicated, may hold values from -0.21875 to 0.21875
- b_query: bfloat16 [768], replicated, may hold values from -1.75 to 1.75
- w_key: bfloat16 [768, 768], replicated, may hold values from -0.21875 to 0.21875
- w_value: bfloat16 [768, 768], replicated, may hold values from -0.21875 to 0.21875
- b_value: bfloat16 [768], replicated, may hold values from -1.75 to 1.75
- w_attn_out: bfloat16 [768, 768], replicated, may hold values from -0.875 to 0.875
- b_attn_out: bfloat16 [768], replicated, may hold values from -1.75 to 1.75
- ln2_gain: bfloat16 [768], replicated, may hold values from 0.25 to 1.75
- ln2_shift: bfloat16 [768], replicated, may hold values from -1.75 to 1.75
- w_in: bfloat16 [2, 768, 3072], P('expert', None, 'ffn'), may hold values from -0.21875 to 0.21875
- b_in: bfloat16 [2, 3072], P('expert', 'ffn'), may hold values from -1.75 to 1.75
- w_out: bfloat16 [2, 3072, 768], P('expert', 'ffn'), may hold values from -0.109375 to 0.109375
- b_out: bfloat16 [2, 768], P('expert'), may hold values from -1.75 to 1.75
Outputs:
- mixed: bfloat16 [256, 256, 768], P(('dp', 'expert', 'ffn'))
- grad_tokens: bfloat16 [256, 256, 768], P(('dp', 'expert', 'ffn'))
- grad_ln1_gain: float32 [768], replicated
- grad_ln1_shift: float32 [768], replicated
- grad_w_query: float32 [768, 768], replicated
- grad_b_query: float32 [768], replicated
- grad_w_key: float32 [768, 768], replicated
- grad_w_value: float32 [768, 768], replicated
- grad_b_value: float32 [768], replicated
- grad_w_attn_out: float32 [768, 768], replicated
- grad_b_attn_out: float32 [768], replicated
- grad_ln2_gain: float32 [768], replicated
- grad_ln2_shift: float32 [768], replicated
- grad_w_in: float32 [2, 768, 3072], P('expert', None, 'ffn')
- grad_b_in: float32 [2, 3072], P('expert', 'ffn')
- grad_w_out: float32 [2, 3072, 768], P('expert', 'ffn')
- grad_b_out: float32 [2, 768], P('expert')
The draws below stay inside these ranges and needn't reach their ends.
Inputs may be any that keep to these rules, and one draw needn't show every extreme that they name: modality is 0 for an image patch, 1 for a text token, 2 for padding. An item is an image-text pair (197 patches in slots 0 to 196, then 1 to 40 text tokens), an image alone, or text alone (1 to 40 tokens from slot 0); the remaining slots are padding. One device's 2 items hold at most 394 patches, and in every draw some device holds exactly that many.
All inputs are finite; a program needn't handle non-finite values.
Results may differ from the reference program's by a relative error of at most 0.019.
Values may be sent and summed in bfloat16 or wider, within the bound.
No kernel may reach another device: no remote copies, remote signals or barrier semaphores. Data moves between devices by JAX's collectives and lax.ppermute only.
A program may use at most 192 MiB of HBM per device.

```python
import math
import jax
import jax.numpy as jnp
from jax import lax

D = 768
HEAD_DIM = 64
FF = 3072
PATCHES = 197
TEXT_MAX = 40
SEQ = 256
ITEMS_DEV = 2
ITEMS = 256


def draw_modality(key, part):
    key = jax.random.fold_in(key, 11)
    kind_key, length_key, device_key = jax.random.split(key, 3)
    item_kinds = jax.random.randint(kind_key, (ITEMS,), 0, 20)
    lengths = jax.random.randint(length_key, (ITEMS,), 1, TEXT_MAX + 1)
    devices = ITEMS // ITEMS_DEV
    chosen = jax.random.randint(device_key, (), 0, devices)
    item_index = jnp.arange(ITEMS)
    is_forced = item_index // ITEMS_DEV == chosen
    item_kinds = jnp.where(is_forced, 0, item_kinds)
    first_item = item_index == chosen * ITEMS_DEV
    lengths = jnp.where(first_item, TEXT_MAX, lengths)
    has_image = item_kinds < 17
    has_text = (item_kinds < 14) | (item_kinds >= 17)
    text_start = jnp.where(has_image, PATCHES, 0)
    text_stop = text_start + jnp.where(has_text, lengths, 0)
    position = jnp.arange(SEQ)[None, :]
    image_slot = has_image[:, None] & (position < PATCHES)
    text_slot = (position >= text_start[:, None]) & (position < text_stop[:, None])
    return jnp.where(image_slot, 0, jnp.where(text_slot, 1, 2)).astype(jnp.int32)


def block_levels(rng, extent, cuts, smallest, top_value):
    def one(dim, blocks):
        draws = jax.random.uniform(jax.random.fold_in(jax.random.fold_in(rng, 6), dim), (blocks,), jnp.float32, smallest / len(cuts), top_value / len(cuts))
        return jnp.repeat(jnp.exp(draws), extent[dim] // blocks).reshape((-1,) + (1,) * (len(extent) - dim - 1))

    loudness = one(*cuts[0])
    for cut in cuts[1:]:
        loudness = loudness * one(*cut)
    return loudness


def gaussian(own_key, shape, scale, most, cuts=(), held_as=jnp.bfloat16):
    array = jax.random.normal(own_key, shape, jnp.float32) * scale
    if len(cuts) > 0:
        array = block_levels(own_key, shape, cuts, -0.22, 0.18) * array
    return jnp.clip(array, min=-most, max=most).astype(held_as)


def setup_inputs(seed: int = 0) -> dict:
    seeds = jax.random.split(jax.random.key(seed), 19)
    tokens = gaussian(seeds[0], (ITEMS, SEQ, D), 1.0, 6.0, ((0, 128),))
    cotangent = gaussian(seeds[1], (ITEMS, SEQ, D), 1.0, 6.0, ((0, 128),))
    modality = draw_modality(jax.random.fold_in(seeds[18], 71), 0)
    ln1_gain = jnp.clip(1.0 + 0.15 * jax.random.normal(seeds[3], (D,), jnp.float32), 0.25, 1.75).astype(jnp.bfloat16)
    ln1_shift = gaussian(seeds[4], (D,), 0.3, 1.75)
    w_query = gaussian(seeds[5], (D, D), D ** -0.5, 0.21875)
    b_query = gaussian(seeds[6], (D,), 0.3, 1.75)
    w_key = gaussian(seeds[7], (D, D), D ** -0.5, 0.21875)
    w_value = gaussian(seeds[8], (D, D), D ** -0.5, 0.21875)
    b_value = gaussian(seeds[9], (D,), 0.3, 1.75)
    w_attn_out = gaussian(seeds[10], (D, D), (D // 16) ** -0.5, 0.875)
    b_attn_out = gaussian(seeds[11], (D,), 0.3, 1.75)
    ln2_gain = jnp.clip(1.0 + 0.15 * jax.random.normal(seeds[12], (D,), jnp.float32), 0.25, 1.75).astype(jnp.bfloat16)
    ln2_shift = gaussian(seeds[13], (D,), 0.3, 1.75)
    w_in = gaussian(seeds[14], (2, D, FF), D ** -0.5, 0.21875, ((0, 2), (2, 4)))
    b_in = gaussian(seeds[15], (2, FF), 0.3, 1.75, ((0, 2), (1, 4)))
    w_out = gaussian(seeds[16], (2, FF, D), FF ** -0.5, 0.109375, ((0, 2), (1, 4)))
    b_out = gaussian(seeds[17], (2, D), 0.3, 1.75, ((0, 2),))
    return dict(tokens=tokens, cotangent=cotangent, modality=modality, ln1_gain=ln1_gain, ln1_shift=ln1_shift, w_query=w_query, b_query=b_query, w_key=w_key, w_value=w_value, b_value=b_value, w_attn_out=w_attn_out, b_attn_out=b_attn_out, ln2_gain=ln2_gain, ln2_shift=ln2_shift, w_in=w_in, b_in=b_in, w_out=w_out, b_out=b_out)


@jax.custom_vjp
def low(v):
    return lax.optimization_barrier(v.astype(jnp.bfloat16)).astype(jnp.float32)

@jax.custom_vjp
def low_back(v):
    return v

def low_keep(v):
    return (low(v), None)

def low_pass(kept, grad):
    return (grad,)

def back_keep(v):
    return (v, None)

def back_low(kept, grad):
    return (low(grad),)
low.defvjp(low_keep, low_pass)
low_back.defvjp(back_keep, back_low)
highest = lax.Precision.HIGHEST
epsilon = 1e-05

def layer_norm(values, gain_vec, shift_vec):
    centre = values - lax.optimization_barrier(jnp.mean(values, axis=-1, keepdims=True))
    scaled = lax.rsqrt(lax.optimization_barrier(jnp.mean(centre * centre, axis=-1, keepdims=True)) + epsilon)
    return centre * scaled * gain_vec + shift_vec

def project(operand, matrix):
    return jnp.einsum('gsd,de->gse', operand, matrix, precision=highest)

def block_forward(params, inputs, modality):
    ln1_gain, ln1_shift, w_query, b_query, w_key, w_value, b_value, w_attn_out, b_attn_out, ln2_gain, ln2_shift, w_in, b_in, w_out, b_out = params
    group_size, length, model_width = inputs.shape
    head_shape = (group_size, length, model_width // HEAD_DIM, HEAD_DIM)
    unit_one = low(layer_norm(inputs, ln1_gain, ln1_shift))
    queries = low(low_back(project(unit_one, w_query) + b_query)).reshape(head_shape)
    keys_all = low(low_back(project(unit_one, w_key))).reshape(head_shape)
    values_all = low(low_back(project(unit_one, w_value) + b_value)).reshape(head_shape)
    raw_scores = jnp.einsum('gqhe,gkhe->ghqk', queries, keys_all, precision=highest) * HEAD_DIM ** (-0.5)
    scores = low_back(raw_scores)
    key_live = (modality < 2)[:, None, None, :]
    attn_probs = jax.nn.softmax(jnp.where(key_live, scores, -1e+30), axis=-1)
    attended = jnp.einsum('ghqk,gkhe->gqhe', low(attn_probs), values_all, precision=highest)
    attended = low(low_back(attended.reshape(group_size, length, model_width)))
    hidden_one = inputs + low_back(project(attended, w_attn_out) + b_attn_out)
    unit_two = low(low_back(layer_norm(hidden_one, ln2_gain, ln2_shift)))
    branch_two = jnp.zeros_like(hidden_one)
    for expert in range(2):
        pre_act = low_back(project(unit_two, w_in[expert]) + b_in[expert])
        activation = low(jax.nn.gelu(pre_act, approximate=False))
        result = low(low_back(project(activation, w_out[expert]) + b_out[expert]))
        branch_two = branch_two + jnp.where((modality == expert)[..., None], result, 0.0)
    return hidden_one + branch_two

def reference(tokens, cotangent, modality, ln1_gain, ln1_shift, w_query, b_query, w_key, w_value, b_value, w_attn_out, b_attn_out, ln2_gain, ln2_shift, w_in, b_in, w_out, b_out):
    params = tuple((weight.astype(jnp.float32) for weight in (ln1_gain, ln1_shift, w_query, b_query, w_key, w_value, b_value, w_attn_out, b_attn_out, ln2_gain, ln2_shift, w_in, b_in, w_out, b_out)))
    group_size = math.gcd(ITEMS, max(1, 4096 // SEQ))
    blocks = ITEMS // group_size
    token_blocks = tokens.astype(jnp.float32).reshape(blocks, group_size, SEQ, D)
    grad_blocks = cotangent.astype(jnp.float32).reshape(blocks, group_size, SEQ, D)
    modal_blocks = modality.reshape(blocks, group_size, SEQ)

    def block_step(totals, pieces):
        block_tokens, block_grad, block_modal = pieces

        def forward(weights, inputs):
            return block_forward(weights, inputs, block_modal)
        result, pullback = jax.vjp(forward, params, block_tokens)
        grad_weights, grad_inputs = pullback(block_grad)
        totals = jax.tree.map(jnp.add, totals, grad_weights)
        return (totals, (result.astype(jnp.bfloat16), grad_inputs.astype(jnp.bfloat16)))
    initial = jax.tree.map(jnp.zeros_like, params)
    totals, outputs = lax.scan(block_step, initial, (token_blocks, grad_blocks, modal_blocks))
    mixed = outputs[0].reshape(ITEMS, SEQ, D)
    grad_tokens = outputs[1].reshape(ITEMS, SEQ, D)
    return (mixed, grad_tokens, totals[0], totals[1], totals[2], totals[3], totals[4], totals[5], totals[6], totals[7], totals[8], totals[9], totals[10], totals[11], totals[12], totals[13], totals[14])
```

```python
import jax
import jax.numpy as jnp
from jax import lax
from jax.sharding import PartitionSpec as P

HEAD_DIM = 64
PATCHES = 197
VIS = 200
TXT = 40
VEC = 24

epsilon = 1e-05
root_half = 0.7071067811865476
inv_root_tau = 0.3989422804014327
AXES = ("dp", "expert", "ffn")
bf16 = jnp.bfloat16
f32 = jnp.float32


def split_index(index):
    return index // 32, index // 8 % 4, index // 4 % 2, index % 4


def join_index(x, z, core, y):
    return ((x * 4 + z) * 2 + core) * 4 + y


def send(value, where):
    pairs = []
    for index in range(128):
        target = where(*split_index(index))
        if target is not None:
            pairs.append((index, join_index(*target)))
    return lax.ppermute(value, AXES, pairs)


def swap_core(value):
    return send(value, lambda x, z, c, y: (x, z, 1 - c, y))


def swap_pair(value):
    return send(value, lambda x, z, c, y: (x, z, c, y ^ 1))


def swap_other(value):
    return send(value, lambda x, z, c, y: (x, z, c, 3 - y))


def shift(value, axes, step):
    def where(x, z, c, y):
        at = dict(x=x, z=z, y=y)
        at[axes[c]] = (at[axes[c]] + step) % 4
        return at["x"], at["z"], c, at["y"]

    return send(value, where)


def norm_forward(values, gain_vec, shift_vec):
    centre = values - jnp.mean(values, axis=-1, keepdims=True)
    scaled = lax.rsqrt(jnp.mean(centre * centre, axis=-1, keepdims=True) + epsilon)
    normal_hat = centre * scaled
    return (normal_hat * gain_vec + shift_vec, normal_hat, scaled)


def norm_backward(grad_result, normal_hat, scaled, gain_vec):
    grad_hat = grad_result * gain_vec
    inner_term = (
        grad_hat
        - jnp.mean(grad_hat, axis=-1, keepdims=True)
        - normal_hat * jnp.mean(grad_hat * normal_hat, axis=-1, keepdims=True)
    )
    return (
        scaled * inner_term,
        jnp.sum(grad_result * normal_hat, axis=0),
        jnp.sum(grad_result, axis=0),
    )


def matmul(first_op, second_op):
    return jnp.dot(first_op, second_op, preferred_element_type=f32)


def contract_rows(first_op, second_op):
    return lax.dot_general(first_op, second_op, (((0,), (0,)), ((), ())), preferred_element_type=f32)


def times_transpose(first_op, second_op):
    return lax.dot_general(first_op, second_op, (((1,), (1,)), ((), ())), preferred_element_type=f32)


def expert_rows(rows, grads, parts):
    out = 0.0
    grad_in = 0.0
    kept = []
    for first, bias, second in parts:
        pre_act = matmul(rows, first) + bias.astype(f32)
        cdf = 0.5 * (1.0 + lax.erf(pre_act * root_half))
        activation = (pre_act * cdf).astype(bf16)
        slope = cdf + pre_act * jnp.exp(-0.5 * pre_act * pre_act) * inv_root_tau
        grad_pre = (times_transpose(grads, second) * slope).astype(bf16)
        out = out + matmul(activation, second)
        grad_in = grad_in + times_transpose(grad_pre, first)
        kept.append((activation, grad_pre))
    return out, grad_in, kept


def expert_grads(rows, grads, kept):
    return [
        (contract_rows(rows, grad_pre), contract_rows(activation, grads), jnp.sum(grad_pre.astype(f32), axis=0))
        for activation, grad_pre in kept
    ]


def chunk_at(value, index):
    return lax.dynamic_index_in_dim(value, index, 0, keepdims=False)


def reduce_scatter(data, vec, axes, me):
    width = data.shape[2]
    size = data.shape[1]
    low_vec = vec.astype(bf16)
    got = []
    for step in (1, 3, 2):
        out = jnp.concatenate([chunk_at(data, (me + step) % 4).astype(bf16), low_vec], axis=0)
        got.append(shift(out, axes, step))
    total = chunk_at(data, me).astype(f32)
    for piece in got:
        total = total + piece[:size].astype(f32)
        vec = vec + piece[size:].astype(f32)
    return total, vec


def all_reduce(data, vec, axes):
    size = data.shape[0]
    whole = jnp.concatenate([data, vec], axis=0)
    low = whole.astype(bf16)
    got = [shift(low, axes, step) for step in (1, 3, 2)]
    total = whole
    for piece in got:
        total = total + piece.astype(f32)
    return total[:size], total[size:]


def gather(data, axes, me):
    got = [(0, data)] + [(step, shift(data, axes, step)) for step in (1, 3, 2)]
    whole = jnp.zeros((4,) + data.shape, data.dtype)
    for step, piece in got:
        whole = lax.dynamic_update_index_in_dim(whole, piece, (me - step) % 4, 0)
    return whole.reshape((4 * data.shape[0],) + data.shape[1:])


def body(
    tokens,
    cotangent,
    modality,
    ln1_gain,
    ln1_shift,
    w_query,
    b_query,
    w_key,
    w_value,
    b_value,
    w_attn_out,
    b_attn_out,
    ln2_gain,
    ln2_shift,
    w_in,
    b_in,
    w_out,
    b_out,
):
    item_count, length, model_width = tokens.shape
    head_count = model_width // HEAD_DIM
    row_count = item_count * length
    score_scale = HEAD_DIM ** (-0.5)
    head_shape = (item_count, length, head_count, HEAD_DIM)
    core = lax.axis_index("expert")
    at_y = lax.axis_index("ffn")
    at_x = lax.axis_index("dp") // 4
    at_z = lax.axis_index("dp") % 4

    small = lax.all_gather(jnp.concatenate([b_in, b_out], axis=0), ("expert", "ffn"), axis=0)
    bias_v0 = small[at_y, 0]
    bias_v1 = small[3 - at_y, 0]
    bias_t0 = small[4 + at_y, 0]
    bias_out_v = small[0, 1].astype(f32)
    bias_out_t = small[4, 1].astype(f32)
    far_in = send(w_in[0], lambda x, z, c, y: (x, z, 0, 3 - y) if c == 0 else None)
    far_out = send(w_out[0], lambda x, z, c, y: (x, z, 1, 3 - y) if c == 0 else None)
    near_in = swap_core(w_in[0])
    near_out = swap_core(w_out[0])
    is_first = core == 0

    has_image = (modality[:, :1] == 0)[:, :, None]

    def pack(values):
        vision = values[:, :VIS]
        text = jnp.where(has_image, values[:, PATCHES : PATCHES + TXT], values[:, :TXT])
        return jnp.concatenate([vision.reshape(-1, model_width), text.reshape(-1, model_width)], axis=0)

    def unpack(rows):
        vision = rows[: item_count * VIS].reshape(item_count, VIS, model_width)
        text = rows[item_count * VIS :].reshape(item_count, TXT, model_width)
        rest = length - PATCHES - TXT
        with_image = jnp.concatenate(
            [vision[:, :PATCHES], text, jnp.zeros((item_count, rest, model_width), rows.dtype)], axis=1
        )
        alone = jnp.concatenate([text, jnp.zeros((item_count, length - TXT, model_width), rows.dtype)], axis=1)
        whole = jnp.where(has_image, with_image, alone)
        return jnp.where((modality < 2)[:, :, None], whole, 0).reshape(row_count, model_width)

    live_vision = (modality[:, :VIS] == 0).reshape(-1, 1)
    live_text = jnp.where(
        has_image[:, :, 0], modality[:, PATCHES : PATCHES + TXT] == 1, modality[:, :TXT] == 1
    ).reshape(-1, 1)
    live_rows = jnp.concatenate([live_vision, live_text], axis=0)
    grad_own = jnp.where(live_rows, pack(cotangent), 0).astype(bf16)
    cut = item_count * VIS
    grad_mate = swap_pair(grad_own)
    grad_text = jnp.concatenate([grad_own[cut:], grad_mate[cut:]], axis=0)
    grad_text = jnp.concatenate([grad_text, swap_other(grad_text)], axis=0)

    inputs = tokens.reshape(row_count, model_width).astype(f32)
    grad_result = cotangent.reshape(row_count, model_width).astype(f32)
    key_live = (modality < 2)[:, None, None, :]
    gain_one = ln1_gain.astype(f32)
    gain_two = ln2_gain.astype(f32)
    unit_one, hat_one, scale_one = norm_forward(inputs, gain_one, ln1_shift.astype(f32))
    unit_low = unit_one.astype(bf16)
    queries = (matmul(unit_low, w_query) + b_query.astype(f32)).astype(bf16)
    keys_all = matmul(unit_low, w_key).astype(bf16)
    values_all = (matmul(unit_low, w_value) + b_value.astype(f32)).astype(bf16)
    query_heads = queries.reshape(head_shape)
    key_heads = keys_all.reshape(head_shape)
    value_heads = values_all.reshape(head_shape)
    scores = jnp.einsum("iqhe,ikhe->ihqk", query_heads, key_heads, preferred_element_type=f32) * score_scale
    masked = jnp.where(key_live, scores, -1e30)
    row_peak = jnp.max(masked, axis=-1, keepdims=True)
    log_total = row_peak + jnp.log(jnp.sum(jnp.exp(masked - row_peak), axis=-1, keepdims=True))
    attn_probs = jnp.exp(masked - log_total)
    probs_low = attn_probs.astype(bf16)
    attended = jnp.einsum("ihqk,ikhe->iqhe", probs_low, value_heads, preferred_element_type=f32)
    attended = attended.reshape(row_count, model_width).astype(bf16)
    hidden_one = inputs + matmul(attended, w_attn_out) + b_attn_out.astype(f32)
    unit_two, hat_two, scale_two = norm_forward(hidden_one, gain_two, ln2_shift.astype(f32))

    unit_own = pack(unit_two.reshape(tokens.shape).astype(bf16))
    unit_mate = swap_pair(unit_own)
    unit_text = jnp.concatenate([unit_own[cut:], unit_mate[cut:]], axis=0)
    unit_text = jnp.concatenate([unit_text, swap_other(unit_text)], axis=0)
    unit_vision = jnp.concatenate([unit_own[:cut], unit_mate[:cut]], axis=0)
    grad_vision = jnp.concatenate([grad_own[:cut], grad_mate[:cut]], axis=0)

    far_other = swap_core(jnp.where(is_first, far_in, far_out))
    vision_parts = [
        (jnp.where(is_first, w_in[0], near_in), bias_v0, jnp.where(is_first, w_out[0], near_out)),
        (jnp.where(is_first, far_in, far_other), bias_v1, jnp.where(is_first, far_other, far_out)),
    ]
    text_parts = [(jnp.where(is_first, near_in, w_in[0]), bias_t0, jnp.where(is_first, near_out, w_out[0]))]

    text_out, text_back, text_kept = expert_rows(unit_text, grad_text, text_parts)
    half_text = text_back.shape[0] // 2
    text_back = text_back[:half_text] + swap_other(text_back[half_text:].astype(bf16)).astype(f32)
    text_out = text_out[:half_text] + swap_other(text_out[half_text:].astype(bf16)).astype(f32)
    vision_out, vision_back, vision_kept = expert_rows(unit_vision, grad_vision, vision_parts)

    def return_rows(vision, text):
        cut_text = item_count * TXT
        away = jnp.concatenate([vision[cut:], text[cut_text:]], axis=0).astype(bf16)
        home = jnp.concatenate([vision[:cut], text[:cut_text]], axis=0)
        return home + swap_pair(away).astype(f32)

    grad_unit = return_rows(vision_back, text_back).astype(bf16)
    bias_rows = jnp.concatenate(
        [jnp.broadcast_to(bias_out_v, (cut, model_width)), jnp.broadcast_to(bias_out_t, (item_count * TXT, model_width))]
    )
    result = (return_rows(vision_out, text_out) + bias_rows).astype(bf16)
    mixed = (hidden_one + unpack(result).astype(f32)).astype(bf16).reshape(tokens.shape)

    ((gv0_in, gv0_out, gv0_b), (gv1_in, gv1_out, gv1_b)) = expert_grads(unit_vision, grad_vision, vision_kept)
    ((gt_in, gt_out, gt_b),) = expert_grads(unit_text, grad_text, text_kept)
    low = lambda v: v.astype(bf16)
    keep_in = jnp.where(is_first, gv0_in, gt_in) + swap_core(low(jnp.where(is_first, gt_in, gv0_in))).astype(f32)
    keep_out = jnp.where(is_first, gv0_out, gt_out) + swap_core(low(jnp.where(is_first, gt_out, gv0_out))).astype(f32)
    far_sum = jnp.where(is_first, gv1_in, gv1_out) + swap_core(low(jnp.where(is_first, gv1_out, gv1_in))).astype(f32)
    far_sum = low(far_sum)
    from_in = send(far_sum, lambda x, z, c, y: (x, z, 0, 3 - y) if c == 0 else None)
    from_out = send(far_sum, lambda x, z, c, y: (x, z, 0, 3 - y) if c == 1 else None)
    keep_in = keep_in + from_in.astype(f32)
    keep_out = keep_out + from_out.astype(f32)
    no_vec = jnp.zeros((0, model_width), f32)
    me_one = jnp.where(is_first, at_x, at_z)
    me_two = jnp.where(is_first, at_z, at_x)
    expert_sum = jnp.concatenate([keep_in, keep_out], axis=0)
    expert_sum, _ = reduce_scatter(expert_sum.reshape(4, -1, model_width), no_vec, "xz", me_one)
    expert_sum, _ = reduce_scatter(expert_sum.reshape(4, -1, model_width), no_vec, "zx", me_two)
    expert_sum = gather(low(expert_sum), "zx", me_two)
    expert_sum = gather(expert_sum, "xz", me_one).astype(f32)
    grad_w_in = expert_sum[:model_width]
    grad_w_out = expert_sum[model_width:]

    grad_unit_two = unpack(grad_unit).astype(f32)
    grad_norm_two, grad_ln2_gain, grad_ln2_shift = norm_backward(grad_unit_two, hat_two, scale_two, gain_two)
    grad_hidden = grad_result + grad_norm_two
    grad_branch = grad_hidden.astype(bf16)
    grad_b_attn_out = jnp.sum(grad_branch.astype(f32), axis=0)
    grad_w_attn_out = contract_rows(attended, grad_branch)
    grad_attended = times_transpose(grad_branch, w_attn_out).astype(bf16).reshape(head_shape)
    grad_values = jnp.einsum("ihqk,iqhe->ikhe", probs_low, grad_attended, preferred_element_type=f32)
    grad_values = grad_values.astype(bf16).reshape(row_count, model_width)
    grad_probs = jnp.einsum("iqhe,ikhe->ihqk", grad_attended, value_heads, preferred_element_type=f32)
    grad_scores = attn_probs * (grad_probs - jnp.sum(grad_probs * attn_probs, axis=-1, keepdims=True))
    grad_scores = grad_scores.astype(bf16)
    grad_queries = jnp.einsum("ihqk,ikhe->iqhe", grad_scores, key_heads, preferred_element_type=f32) * score_scale
    grad_queries = grad_queries.astype(bf16).reshape(row_count, model_width)
    grad_keys = jnp.einsum("ihqk,iqhe->ikhe", grad_scores, query_heads, preferred_element_type=f32) * score_scale
    grad_keys = grad_keys.astype(bf16).reshape(row_count, model_width)
    grad_w_query = contract_rows(unit_low, grad_queries)
    grad_b_query = jnp.sum(grad_queries.astype(f32), axis=0)
    grad_w_key = contract_rows(unit_low, grad_keys)
    grad_w_value = contract_rows(unit_low, grad_values)
    grad_b_value = jnp.sum(grad_values.astype(f32), axis=0)
    grad_unit_one = (
        times_transpose(grad_queries, w_query)
        + times_transpose(grad_keys, w_key)
        + times_transpose(grad_values, w_value)
    )
    grad_norm_one, grad_ln1_gain, grad_ln1_shift = norm_backward(grad_unit_one, hat_one, scale_one, gain_one)
    grad_tokens = (grad_hidden + grad_norm_one).astype(bf16).reshape(tokens.shape)

    bias_grads = jnp.zeros((8, model_width), f32)
    bias_grads = lax.dynamic_update_index_in_dim(bias_grads, gv0_b, at_y, 0)
    bias_grads = lax.dynamic_update_index_in_dim(bias_grads, gv1_b, 3 - at_y, 0)
    bias_grads = lax.dynamic_update_index_in_dim(bias_grads, gt_b, 4 + at_y, 0)
    grad_live = grad_own.astype(f32)
    rows = [
        grad_ln1_gain,
        grad_ln1_shift,
        grad_b_query,
        grad_b_value,
        grad_b_attn_out,
        grad_ln2_gain,
        grad_ln2_shift,
        jnp.sum(grad_live[:cut], axis=0),
        jnp.sum(grad_live[cut:], axis=0),
    ]
    vec = jnp.concatenate(
        [jnp.stack(rows), bias_grads, jnp.zeros((VEC - 8 - len(rows), model_width), f32)], axis=0
    )
    pair_one = jnp.concatenate([grad_w_query, grad_w_key], axis=0)
    pair_two = jnp.concatenate([grad_w_value, grad_w_attn_out], axis=0)
    away = jnp.where(is_first, pair_two, pair_one).astype(bf16)
    shared = jnp.where(is_first, pair_one, pair_two)
    got = swap_core(jnp.concatenate([away, vec.astype(bf16)], axis=0)).astype(f32)
    shared = shared + got[: shared.shape[0]]
    vec = vec + got[shared.shape[0] :]
    me_first = jnp.where(is_first, at_y, at_x)
    me_second = jnp.where(is_first, at_x, at_z)
    shared, vec = reduce_scatter(shared.reshape(4, -1, model_width), vec, "yx", me_first)
    shared, vec = reduce_scatter(shared.reshape(4, -1, model_width), vec, "xz", me_second)
    shared, vec = all_reduce(shared, vec, "zy")
    shared = gather(shared.astype(bf16), "xz", me_second)
    shared = gather(shared, "yx", me_first)
    other = swap_core(shared)
    first_pair = jnp.where(is_first, shared, other).astype(f32)
    second_pair = jnp.where(is_first, other, shared).astype(f32)
    grad_b_in = jnp.where(is_first, chunk_at(vec, 9 + at_y), chunk_at(vec, 13 + at_y))
    grad_b_out = jnp.where(is_first, vec[7], vec[8])
    return (
        mixed,
        grad_tokens,
        vec[0],
        vec[1],
        first_pair[:model_width],
        vec[2],
        first_pair[model_width:],
        second_pair[:model_width],
        vec[3],
        second_pair[model_width:],
        vec[4],
        vec[5],
        vec[6],
        grad_w_in[None],
        grad_b_in[None],
        grad_w_out[None],
        grad_b_out[None],
    )


def solution(mesh):
    items = P(AXES, None, None)
    expert_specs = (P("expert", None, "ffn"), P("expert", "ffn"), P("expert", "ffn", None), P("expert", None))
    return jax.shard_map(
        body,
        mesh=mesh,
        in_specs=(items, items, P(AXES, None)) + (P(),) * 11 + expert_specs,
        out_specs=(items, items) + (P(),) * 11 + expert_specs,
        check_vma=False,
    )
```

```python
import functools

import jax
import jax.numpy as jnp
from jax import lax
from jax.experimental import pallas as pl
from jax.experimental.pallas import tpu as pltpu
from jax.sharding import PartitionSpec as P

D = 768
HEAD_DIM = 64
HEADS = D // HEAD_DIM
PATCHES = 197
SEQ = 256
ITEMS = 2
ROWS = ITEMS * SEQ
TEXT_AT = 192
VIS = 208
TXT = 48
CUT = ITEMS * VIS
CUT_TXT = ITEMS * TXT
VEC = 24

epsilon = 1e-05
root_half = 0.7071067811865476
inv_root_tau = 0.3989422804014327
AXES = ("dp", "expert", "ffn")
bf16 = jnp.bfloat16
f32 = jnp.float32


def split_index(index):
    return index // 32, index // 8 % 4, index // 4 % 2, index % 4


def join_index(x, z, core, y):
    return ((x * 4 + z) * 2 + core) * 4 + y


def send(value, where):
    pairs = []
    for index in range(128):
        target = where(*split_index(index))
        if target is not None:
            pairs.append((index, join_index(*target)))
    return lax.ppermute(value, AXES, pairs)


def swap_core(value):
    return send(value, lambda x, z, c, y: (x, z, 1 - c, y))


def swap_pair(value):
    return send(value, lambda x, z, c, y: (x, z, c, y ^ 1))


def swap_other(value):
    return send(value, lambda x, z, c, y: (x, z, c, 3 - y))


def swap_far(value):
    return send(value, lambda x, z, c, y: (x, z, c, y ^ 2))


def shift(value, axes, step):
    def where(x, z, c, y):
        at = dict(x=x, z=z, y=y)
        at[axes[c]] = (at[axes[c]] + step) % 4
        return at["x"], at["z"], c, at["y"]

    return send(value, where)


def shifts(pieces, axes):
    return [shift(piece, axes, step) for piece, step in zip(pieces, (1, 3, 2))]


def tie(value, *others):
    return lax.optimization_barrier((value, others))[0]


def core_index():
    return lax.axis_index("expert")


def place(axes):
    dp = lax.axis_index("dp")
    at = dict(x=dp // 4, z=dp % 4, y=lax.axis_index("ffn"))
    return jnp.where(core_index() == 0, at[axes[0]], at[axes[1]])


def norm_forward(values, gain_vec, shift_vec):
    centre = values - jnp.mean(values, axis=-1, keepdims=True)
    scaled = lax.rsqrt(jnp.mean(centre * centre, axis=-1, keepdims=True) + epsilon)
    normal_hat = centre * scaled
    return (normal_hat * gain_vec + shift_vec, normal_hat, scaled)


def norm_backward(grad_result, normal_hat, scaled, gain_vec):
    grad_hat = grad_result * gain_vec
    inner_term = (
        grad_hat
        - jnp.mean(grad_hat, axis=-1, keepdims=True)
        - normal_hat * jnp.mean(grad_hat * normal_hat, axis=-1, keepdims=True)
    )
    return (
        scaled * inner_term,
        jnp.sum(grad_result * normal_hat, axis=0, keepdims=True),
        jnp.sum(grad_result, axis=0, keepdims=True),
    )


def matmul(first_op, second_op):
    return jnp.dot(first_op, second_op, preferred_element_type=f32)


def contract_rows(first_op, second_op):
    return lax.dot_general(first_op, second_op, (((0,), (0,)), ((), ())), preferred_element_type=f32)


def times_transpose(first_op, second_op):
    return lax.dot_general(first_op, second_op, (((1,), (1,)), ((), ())), preferred_element_type=f32)


def vector(ref):
    return ref[...].astype(f32).reshape(1, D)


def slots_of(row):
    has_image = jnp.max(jnp.where(row == 0, 1.0, 0.0), axis=1, keepdims=True)
    texts = jnp.sum(jnp.where(row == 1, 1.0, 0.0), axis=1, keepdims=True)
    start = has_image * PATCHES
    slot = lax.broadcasted_iota(jnp.int32, (SEQ, 1), 0).astype(f32)
    modal = jnp.where(slot < start, 0.0, jnp.where(slot < start + texts, 1.0, 2.0))
    return has_image > 0.5, modal


def unpack_item(vision, text, has_image, modal):
    whole = jnp.concatenate(
        [
            jnp.where(has_image, vision[:TXT], text),
            vision[TXT:TEXT_AT],
            jnp.where(modal[TEXT_AT:VIS] == 1, text[: VIS - TEXT_AT], vision[TEXT_AT:]),
            text[VIS - TEXT_AT :],
            jnp.zeros((SEQ - TEXT_AT - TXT, D), f32),
        ],
        axis=0,
    )
    return jnp.where(modal < 2, whole, 0.0)


VMEM = pl.BlockSpec(memory_space=pltpu.VMEM)
ANY = pl.BlockSpec(memory_space=pl.ANY)


def cost(micros):
    return pl.CostEstimate(flops=0, bytes_accessed=int(micros * 1e5), transcendentals=0)


def params(mebibytes):
    return pltpu.CompilerParams(vmem_limit_bytes=mebibytes * 1024 * 1024)


def call(kernel, outs, *args, scratch=(), any_from=None, micros=1.5, mebibytes=12):
    specs = [VMEM] * len(args) if any_from is None else [VMEM] * any_from + [ANY] * (len(args) - any_from)
    return pl.pallas_call(
        kernel,
        out_shape=[jax.ShapeDtypeStruct(shape, dtype) for shape, dtype in outs],
        in_specs=specs,
        out_specs=[VMEM] * len(outs),
        scratch_shapes=list(scratch),
        cost_estimate=cost(micros),
        compiler_params=params(mebibytes),
    )(*args)


def pack_kernel(grad_ref, modal_ref, out_ref, text_ref, sum_ref):
    sums = [0.0, 0.0]
    for item in range(ITEMS):
        has_image, modal = slots_of(modal_ref[item : item + 1])
        grad = grad_ref[item * SEQ : (item + 1) * SEQ].astype(f32)
        vision = jnp.where(modal[:VIS] == 0, grad[:VIS], 0.0)
        text = jnp.where(
            has_image,
            jnp.where(modal[TEXT_AT : TEXT_AT + TXT] == 1, grad[TEXT_AT : TEXT_AT + TXT], 0.0),
            jnp.where(modal[:TXT] == 1, grad[:TXT], 0.0),
        )
        out_ref[item * VIS : (item + 1) * VIS] = vision.astype(bf16)
        out_ref[CUT + item * TXT : CUT + (item + 1) * TXT] = text.astype(bf16)
        text_ref[item * TXT : (item + 1) * TXT] = text.astype(bf16)
        sums[0] += jnp.sum(vision, axis=0, keepdims=True)
        sums[1] += jnp.sum(text, axis=0, keepdims=True)
    sum_ref[...] = jnp.concatenate(sums, axis=0)


def forward_kernel(
    tok_ref, modal_ref, gain1, shift1, b_query, b_value, b_out, gain2, shift2, wq_ref, wk_ref, wv_ref, wo_ref,
    grad_text, small, q_ref, k_ref, v_ref, p_ref, att_ref, hid_ref, unit_ref, text_ref, held, sems,
):
    item = pl.program_id(0)
    copies = [pltpu.make_async_copy(ref, held.at[i], sems.at[i]) for i, ref in enumerate((wq_ref, wk_ref, wv_ref, wo_ref))]

    @pl.when(item == 0)
    def _():
        for copy in copies:
            copy.start()
        text_ref[CUT_TXT : 2 * CUT_TXT] = grad_text[...]
        text_ref[2 * CUT_TXT :] = small[...]

    x = tok_ref[...].astype(f32)
    unit, _, _ = norm_forward(x, vector(gain1), vector(shift1))
    unit = unit.astype(bf16)

    @pl.when(item == 0)
    def _():
        for copy in copies:
            copy.wait()

    q_ref[...] = ((matmul(unit, held[0]) + vector(b_query)).astype(bf16) * 0.125).astype(bf16)
    k_ref[...] = matmul(unit, held[1]).astype(bf16)
    v_ref[...] = (matmul(unit, held[2]) + vector(b_value)).astype(bf16)
    row = modal_ref[pl.ds(item, 1)]
    bias = jnp.where(row < 2, 0.0, -1e30)
    low_half = lax.broadcasted_iota(jnp.int32, (1, 128), 1) < HEAD_DIM
    for pair in range(HEADS // 2):
        lanes = slice(pair * 128, (pair + 1) * 128)
        q, k, v = q_ref[:, lanes], k_ref[:, lanes], v_ref[:, lanes]
        halves = []
        for half in range(2):
            mine = low_half if half == 0 else jnp.logical_not(low_half)
            scores = times_transpose(jnp.where(mine, q, 0).astype(bf16), k) + bias
            scores = jnp.exp(scores - jnp.max(scores, axis=-1, keepdims=True))
            probs = (scores * (1.0 / jnp.sum(scores, axis=-1, keepdims=True))).astype(bf16)
            p_ref[0, 2 * pair + half] = probs
            halves.append(matmul(probs, v))
        att_ref[:, lanes] = jnp.where(low_half, halves[0], halves[1]).astype(bf16)
    hidden = x + matmul(att_ref[...], held[3]) + vector(b_out)
    hid_ref[...] = hidden
    unit, _, _ = norm_forward(hidden, vector(gain2), vector(shift2))
    has_image, _ = slots_of(row)
    unit_ref[pl.ds(pl.multiple_of(item * VIS, 16), VIS)] = unit[:VIS].astype(bf16)
    text = jnp.where(has_image, unit[TEXT_AT : TEXT_AT + TXT], unit[:TXT]).astype(bf16)
    unit_ref[pl.ds(pl.multiple_of(CUT + item * TXT, 16), TXT)] = text
    text_ref[pl.ds(pl.multiple_of(item * TXT, 16), TXT)] = text


def forward_attention(tokens, modality, vectors, weights, grad_text, small):
    block = pl.BlockSpec((SEQ, D), lambda i: (i, 0))
    heads = pl.BlockSpec((1, HEADS, SEQ, SEQ), lambda i: (i, 0, 0, 0))
    rows = jax.ShapeDtypeStruct((ROWS, D), bf16)
    return pl.pallas_call(
        forward_kernel,
        grid=(ITEMS,),
        out_shape=[rows] * 3
        + [jax.ShapeDtypeStruct((ITEMS, HEADS, SEQ, SEQ), bf16), rows, jax.ShapeDtypeStruct((ROWS, D), f32)]
        + [rows, jax.ShapeDtypeStruct((2 * CUT_TXT + 16, D), bf16)],
        in_specs=[block] + [VMEM] * 8 + [ANY] * 4 + [VMEM] * 2,
        out_specs=[block] * 3 + [heads, block, block, VMEM, VMEM],
        scratch_shapes=[pltpu.VMEM((4, D, D), bf16), pltpu.SemaphoreType.DMA((4,))],
        cost_estimate=cost(10),
        compiler_params=params(56),
    )(tokens, modality, *vectors, *weights, grad_text, small)


def fetch(first, second, buffer, sem):
    @pl.when(core_index() == 0)
    def _():
        pltpu.make_async_copy(first, buffer, sem).start()

    @pl.when(core_index() == 1)
    def _():
        pltpu.make_async_copy(second, buffer, sem).start()


def choose_kernel(first, second, out, sem):
    fetch(first, second, out, sem)
    pltpu.make_async_copy(first, out, sem).wait()


def choose(first, second):
    return pl.pallas_call(
        choose_kernel,
        out_shape=jax.ShapeDtypeStruct((D, D), bf16),
        in_specs=[ANY] * 2,
        out_specs=ANY,
        scratch_shapes=[pltpu.SemaphoreType.DMA],
        cost_estimate=cost(1),
        compiler_params=params(8),
    )(first, second)


def row_pass(unit, grad, first, bias, second, act_ref, pre_ref, base):
    for at in range(0, D, 256):
        cols = slice(at, at + 256)
        kept = slice(base + at, base + at + 256)
        pre_act = matmul(unit, first[:, cols]) + bias[:, cols]
        cdf = 0.5 + 0.5 * lax.erf(pre_act * root_half)
        act_ref[:, kept] = (pre_act * cdf).astype(bf16)
        slope = cdf + pre_act * (jnp.exp(-0.5 * pre_act * pre_act) * inv_root_tau)
        pre_ref[:, kept] = (times_transpose(grad, second[cols, :]) * slope).astype(bf16)


def vision_kernel(
    unit_ref, grad_ref, b_in, got_a, near_small, w_in, w_out, near_in, near_out, far_in, far_out, far_swap,
    out_ref, back_ref, act_ref, pre_ref, held, sems,
):
    fetch(w_in, near_in, held.at[0], sems.at[0])
    fetch(w_out, near_out, held.at[1], sems.at[1])
    fetch(far_in, far_swap, held.at[2], sems.at[2])
    fetch(far_swap, far_out, held.at[3], sems.at[3])
    first = core_index() == 0
    own_bias = (b_in[...].astype(f32), got_a[2 * CUT_TXT : 2 * CUT_TXT + 1].astype(f32))
    unit, grad = unit_ref[:CUT], grad_ref[:CUT]
    for part in range(2):
        for slot in (2 * part, 2 * part + 1):
            pltpu.make_async_copy(w_in, held.at[slot], sems.at[slot]).wait()
        bias = jnp.where(first, own_bias[part], near_small[16 * part : 16 * part + 1].astype(f32))
        row_pass(unit, grad, held.at[2 * part], bias, held.at[2 * part + 1], act_ref, pre_ref, part * D)
    back = times_transpose(pre_ref[:, :D], held[0]) + times_transpose(pre_ref[:, D:], held[2])
    back_ref[...] = back.astype(back_ref.dtype)
    out = matmul(act_ref[:, :D], held[1]) + matmul(act_ref[:, D:], held[3])
    out_ref[...] = out.astype(out_ref.dtype)


def vision_rows(unit, grad, smalls, weights, dtype):
    outs = [((CUT, D), dtype)] * 2 + [((CUT, 2 * D), bf16)] * 2
    scratch = [pltpu.VMEM((4, D, D), bf16), pltpu.SemaphoreType.DMA((4,))]
    return call(vision_kernel, outs, unit, grad, *smalls, *weights, scratch=scratch, any_from=5, micros=3, mebibytes=28)


def text_kernel(
    own_text, unit_mate, grad_mate, got_a, got_b, b_in, near_small, w_in, w_out, near_in, near_out,
    home_ref, mate_ref, a_ref, b_ref, unit_ref, grad_ref, act_ref, pre_ref, held, sems,
):
    fetch(near_in, w_in, held.at[0], sems.at[0])
    fetch(near_out, w_out, held.at[1], sems.at[1])
    for total, mate, base in ((unit_ref, unit_mate, 0), (grad_ref, grad_mate, CUT_TXT)):
        total[:CUT_TXT] = own_text[base : base + CUT_TXT]
        total[CUT_TXT : 2 * CUT_TXT] = mate[CUT:]
        total[2 * CUT_TXT : 3 * CUT_TXT] = got_a[base : base + CUT_TXT]
        total[3 * CUT_TXT :] = got_b[base : base + CUT_TXT]
    bias = jnp.where(core_index() == 0, near_small[0:1].astype(f32), b_in[...].astype(f32))
    for slot in range(2):
        pltpu.make_async_copy(w_in, held.at[slot], sems.at[slot]).wait()
    row_pass(unit_ref[...], grad_ref[...], held.at[0], bias, held.at[1], act_ref, pre_ref, 0)
    back = times_transpose(pre_ref[...], held[0])
    out = matmul(act_ref[...], held[1])
    for piece, target in enumerate((home_ref, mate_ref, a_ref, b_ref)):
        at = slice(piece * CUT_TXT, (piece + 1) * CUT_TXT)
        target[:CUT_TXT] = back[at].astype(target.dtype)
        target[CUT_TXT:] = out[at].astype(target.dtype)


def text_rows(*args):
    outs = [((2 * CUT_TXT, D), f32)] + [((2 * CUT_TXT, D), bf16)] * 3 + [((4 * CUT_TXT, D), bf16)] * 4
    scratch = [pltpu.VMEM((2, D, D), bf16), pltpu.SemaphoreType.DMA((2,))]
    return call(text_kernel, outs, *args, scratch=scratch, any_from=7, micros=5, mebibytes=20)


def expert_grads_kernel(
    unit_own, unit_mate, grad_own, grad_mate, act_own, act_mate, pre_own, pre_mate, unit_text, grad_text, act_text, pre_text,
    keep_ref, away_ref, bias_ref, blocks, sems,
):
    def vision_in(cols):
        return contract_rows(unit_own[:CUT], pre_own[:, cols]) + contract_rows(unit_mate[:CUT], pre_mate[:, cols])

    def vision_out(cols):
        return contract_rows(act_own[:, cols], grad_own[:CUT]) + contract_rows(act_mate[:, cols], grad_mate[:CUT])

    near, far = slice(0, D), slice(D, 2 * D)
    at_first = core_index() == 0
    pending = []

    def put(index, value, kind):
        slot = len(pending) % 2
        if len(pending) >= 2:
            pending[-2].wait()
        blocks[slot] = value.astype(bf16)
        rows = pl.ds(index * D, D)
        kept = at_first if kind == 0 else jnp.logical_not(at_first)

        @pl.when(kept)
        def _():
            pltpu.make_async_copy(blocks.at[slot], keep_ref.at[rows], sems.at[slot]).start()

        @pl.when(jnp.logical_not(kept))
        def _():
            pltpu.make_async_copy(blocks.at[slot], away_ref.at[rows], sems.at[slot]).start()

        pending.append(pltpu.make_async_copy(blocks.at[slot], keep_ref.at[rows], sems.at[slot]))

    put(2, contract_rows(unit_text[...], pre_text[...]), 0)
    put(2, contract_rows(act_text[...], grad_text[...]), 1)
    put(0, vision_in(near), 0)
    put(1, vision_in(far), 0)
    put(0, vision_out(near), 1)
    put(1, vision_out(far), 1)
    at_y = lax.axis_index("ffn")
    total = lambda value: jnp.sum(value.astype(f32), axis=0, keepdims=True)
    bias_ref[...] = jnp.zeros_like(bias_ref)
    bias_ref[pl.ds(at_y, 1)] = total(pre_own[:, near]) + total(pre_mate[:, near])
    bias_ref[pl.ds(3 - at_y, 1)] = total(pre_own[:, far]) + total(pre_mate[:, far])
    bias_ref[pl.ds(4 + at_y, 1)] = total(pre_text[...])
    for copy in pending[-2:]:
        copy.wait()


def branch_kernel(
    own_ref, got_ref, home, mate, a_ref, b_ref, modal_ref, cot_ref, hid_ref, att_ref, gain_ref, wo_ref,
    hidden_ref, gatt_ref, dwo_ref, sum_ref,
):
    gain = vector(gain_ref)
    sums = [0.0, 0.0, 0.0]
    for item in range(ITEMS):
        at = slice(item * SEQ, (item + 1) * SEQ)
        vis = slice(item * VIS, (item + 1) * VIS)
        txt = slice(item * TXT, (item + 1) * TXT)
        vision = own_ref[vis] + got_ref[vis].astype(f32)
        text = home[txt] + mate[txt].astype(f32) + a_ref[txt].astype(f32) + b_ref[txt].astype(f32)
        grad_unit = unpack_item(vision, text, *slots_of(modal_ref[item : item + 1])).astype(bf16).astype(f32)
        _, hat, scaled = norm_forward(hid_ref[at], 1.0, 0.0)
        grad_norm, grad_gain, grad_shift = norm_backward(grad_unit, hat, scaled, gain)
        grad_hidden = cot_ref[at].astype(f32) + grad_norm
        hidden_ref[at] = grad_hidden
        branch = grad_hidden.astype(bf16)
        gatt_ref[at] = branch
        sums[0] += grad_gain
        sums[1] += grad_shift
        sums[2] += jnp.sum(branch.astype(f32), axis=0, keepdims=True)
    dwo_ref[...] = contract_rows(att_ref[...], gatt_ref[...]).astype(bf16)
    gatt_ref[...] = times_transpose(gatt_ref[...], wo_ref[...]).astype(bf16)
    sum_ref[...] = jnp.concatenate(sums, axis=0)


def scores_kernel(q_ref, k_ref, v_ref, p_ref, gatt_ref, gq_ref, gk_ref, gv_ref):
    low_half = lax.broadcasted_iota(jnp.int32, (1, 128), 1) < HEAD_DIM
    for pair in range(HEADS // 2):
        lanes = slice(pair * 128, (pair + 1) * 128)
        q, k, v, g = q_ref[:, lanes], k_ref[:, lanes], v_ref[:, lanes], gatt_ref[:, lanes]
        gq = gk = gv = 0.0
        for half in range(2):
            mine = low_half if half == 0 else jnp.logical_not(low_half)
            mask = lambda a: jnp.where(mine, a, 0).astype(bf16)
            low = p_ref[0, 2 * pair + half]
            probs = low.astype(f32)
            inner = times_transpose(mask(g), v) * probs
            scores = (inner - probs * jnp.sum(inner, axis=-1, keepdims=True)).astype(bf16)
            gv += contract_rows(low, mask(g))
            gq += matmul(scores, mask(k))
            gk += contract_rows(scores, mask(q))
        gq_ref[:, lanes] = (gq * 0.125).astype(bf16)
        gk_ref[:, lanes] = gk.astype(bf16)
        gv_ref[:, lanes] = gv.astype(bf16)


def backward_scores(q, k, v, p, gatt):
    block = pl.BlockSpec((SEQ, D), lambda i: (i, 0))
    heads = pl.BlockSpec((1, HEADS, SEQ, SEQ), lambda i: (i, 0, 0, 0))
    return pl.pallas_call(
        scores_kernel,
        grid=(ITEMS,),
        out_shape=[jax.ShapeDtypeStruct((ROWS, D), bf16)] * 3,
        in_specs=[block] * 3 + [heads, block],
        out_specs=[block] * 3,
        cost_estimate=cost(25),
        compiler_params=params(20),
    )(q, k, v, p, gatt)


def shared_kernel(
    tok_ref, gain1, shift1, gq_ref, gk_ref, gv_ref, wq_ref, wk_ref, wv_ref, hidden_ref, dwo_ref, sums_two, grad_live, bias_rows,
    tok_out, keep_ref, away_ref,
):
    gain = vector(gain1)
    unit, hat, scaled = norm_forward(tok_ref[...].astype(f32), gain, vector(shift1))
    low = unit.astype(bf16)
    dwq = contract_rows(low, gq_ref[...]).astype(bf16)
    dwk = contract_rows(low, gk_ref[...]).astype(bf16)
    dwv = contract_rows(low, gv_ref[...]).astype(bf16)
    back = times_transpose(gq_ref[...], wq_ref[...]) + times_transpose(gk_ref[...], wk_ref[...]) + times_transpose(gv_ref[...], wv_ref[...])
    grad_norm, grad_gain, grad_shift = norm_backward(back, hat, scaled, gain)
    tok_out[...] = (hidden_ref[...] + grad_norm).astype(bf16)
    total = lambda ref: jnp.sum(ref[...].astype(f32), axis=0, keepdims=True)
    rows = [grad_gain, grad_shift, total(gq_ref), total(gv_ref), sums_two[...], grad_live[...], bias_rows[...]]
    vec = jnp.concatenate(rows + [jnp.zeros((VEC - 17, D), f32)], axis=0).astype(bf16)

    def put(mine, other):
        mine[:D] = dwq
        mine[D : 2 * D] = dwk
        other[:D] = dwv
        other[D : 2 * D] = dwo_ref[...]
        mine[2 * D :] = vec
        other[2 * D :] = vec

    @pl.when(core_index() == 0)
    def _():
        put(keep_ref, away_ref)

    @pl.when(core_index() == 1)
    def _():
        put(away_ref, keep_ref)


def mixed_kernel(own_ref, got_ref, home, mate, a_ref, b_ref, modal_ref, hid_ref, b_out, near_small, out_ref):
    first = core_index() == 0
    mine, other = b_out[...].astype(f32), near_small[1:2].astype(f32)
    bias_vision, bias_text = jnp.where(first, mine, other), jnp.where(first, other, mine)
    for item in range(ITEMS):
        at = slice(item * SEQ, (item + 1) * SEQ)
        vis = slice(item * VIS, (item + 1) * VIS)
        txt = slice(CUT_TXT + item * TXT, CUT_TXT + (item + 1) * TXT)
        vision = own_ref[vis] + got_ref[vis].astype(f32) + bias_vision
        text = home[txt] + mate[txt].astype(f32) + a_ref[txt].astype(f32) + b_ref[txt].astype(f32) + bias_text
        rows = unpack_item(vision, text, *slots_of(modal_ref[item : item + 1])).astype(bf16).astype(f32)
        out_ref[at] = (hid_ref[at] + rows).astype(bf16)


def split_kernel(count, size, axes, *refs):
    ins, outs, total = refs[:count], refs[count:-1], refs[-1]
    extra = total.shape[0] - 4 * size
    total[...] = sum(ref[: 4 * size + extra].astype(f32) for ref in ins).astype(bf16)
    me = place(axes)
    for step, out in zip((0, 1, 3, 2), outs):
        at = pl.multiple_of(lax.rem(me + step, 4) * size, 16)
        out[:size] = total[pl.ds(at, size)]
        if extra:
            out[size:] = total[4 * size :]


def split(pieces, size, extra, axes):
    outs = [((size + extra, D), bf16)] * 4
    scratch = [pltpu.VMEM((4 * size + extra, D), bf16)]
    return call(functools.partial(split_kernel, len(pieces), size, axes), outs, *pieces, scratch=scratch)


def block_steps(size):
    first = core_index() == 0
    return jnp.where(first, 4 * size, size), jnp.where(first, size, 4 * size)


def expert_split_kernel(size, keep, got, *refs):
    outs, total = refs[:-1], refs[-1]
    total[...] = (keep[...].astype(f32) + got[...].astype(f32)).astype(bf16)
    me = place("xz")
    outer, inner = block_steps(size)
    for step, out in zip((0, 1, 3, 2), outs):
        base = lax.rem(me + step, 4) * outer
        for matrix in range(3):
            for block in range(4):
                at = pl.multiple_of(base + matrix * D + block * inner, 16)
                to = (matrix * 4 + block) * size
                out[to : to + size] = total[pl.ds(at, size)]


def expert_split_again_kernel(size, *refs):
    ins, outs, total = refs[:4], refs[4:-1], refs[-1]
    total[...] = sum(ref[...].astype(f32) for ref in ins).astype(bf16)
    me = place("zx")
    for step, out in zip((0, 1, 3, 2), outs):
        block = lax.rem(me + step, 4)
        for matrix in range(3):
            at = pl.multiple_of((matrix * 4 + block) * size, 16)
            out[matrix * size : (matrix + 1) * size] = total[pl.ds(at, size)]


def expert_sum_kernel(size, *refs):
    ins, (out, swap) = refs[:4], refs[4:]
    total = sum(ref[...].astype(f32) for ref in ins).astype(bf16)
    out[...] = total
    swap[...] = jnp.where(core_index() == 0, total[2 * size :], total[:size])


def expert_place_kernel(size, mine, from_in, from_out, other, out):
    first = core_index() == 0
    near, text, far = mine[:size].astype(f32), mine[2 * size :].astype(f32), other[...].astype(f32)
    out[:size] = (jnp.where(first, near, far) + from_in[...].astype(f32)).astype(bf16)
    out[size:] = (jnp.where(first, far, text) + from_out[...].astype(f32)).astype(bf16)


def expert_finish_kernel(size, low, w_in, w_out):
    outer, inner = block_steps(size)
    for p in range(4):
        for q in range(4):
            at = pl.multiple_of(p * outer + q * inner, 16)
            base = (p * 4 + q) * 2 * size
            w_in[pl.ds(at, size)] = low[base : base + size].astype(f32)
            w_out[pl.ds(at, size)] = low[base + size : base + 2 * size].astype(f32)


def sum_kernel(size, *refs):
    ins, outs = refs[:4], refs[4:]
    outs[0][...] = sum(ref[:size].astype(f32) for ref in ins).astype(bf16)
    if len(outs) > 1:
        outs[1][...] = sum(ref[size:].astype(f32) for ref in ins)


def join_kernel(axes, *refs):
    ins, out = refs[:4], refs[4]
    size = ins[0].shape[0]
    me = place(axes)
    for step, piece in zip((0, 1, 3, 2), ins):
        at = pl.multiple_of(lax.rem(me + 4 - step, 4) * size, 16)
        out[pl.ds(at, size)] = piece[...]


def join(piece, got, axes):
    return call(functools.partial(join_kernel, axes), [((4 * piece.shape[0], D), bf16)], piece, *got)[0]


def finish_kernel(mine, other, vec, wq, wk, wv, wo, g1, s1, bq, bv, g2, s2, bo, b_in, b_out):
    first = core_index() == 0
    for low, high, at in ((wq, wv, 0), (wk, wo, 1)):
        m, o = mine[at].astype(f32), other[at].astype(f32)
        low[...] = jnp.where(first, m, o)
        high[...] = jnp.where(first, o, m)

    @pl.when(pl.program_id(0) == 0)
    def _():
        for ref, row in ((g1, 0), (s1, 1), (bq, 2), (bv, 3), (g2, 4), (s2, 5), (bo, 6)):
            ref[...] = vec[row]
        b_in[...] = vec[pl.ds(9 + 4 * core_index() + lax.axis_index("ffn"), 1)]
        b_out[...] = vec[pl.ds(7 + core_index(), 1)]


def finish(mine, other, vec):
    steps = 4
    size = D // steps
    pair = pl.BlockSpec((2, size, D), lambda i: (0, i, 0))
    block = pl.BlockSpec((size, D), lambda i: (i, 0))
    return pl.pallas_call(
        finish_kernel,
        grid=(steps,),
        out_shape=[jax.ShapeDtypeStruct((D, D), f32)] * 4
        + [jax.ShapeDtypeStruct((D,), f32)] * 7
        + [jax.ShapeDtypeStruct((1, D), f32)] * 2,
        in_specs=[pair, pair, VMEM],
        out_specs=[block] * 4 + [VMEM] * 9,
        cost_estimate=cost(5),
        compiler_params=params(12),
    )(mine.reshape(2, D, D), other.reshape(2, D, D), vec)


def body(
    tokens,
    cotangent,
    modality,
    ln1_gain,
    ln1_shift,
    w_query,
    b_query,
    w_key,
    w_value,
    b_value,
    w_attn_out,
    b_attn_out,
    ln2_gain,
    ln2_shift,
    w_in,
    b_in,
    w_out,
    b_out,
):
    flat_tokens = tokens.reshape(ROWS, D)
    flat_cot = cotangent.reshape(ROWS, D)
    w_in, w_out = w_in[0], w_out[0]

    far_in = send(w_in, lambda x, z, c, y: (x, z, 0, 3 - y) if c == 0 else None)
    far_out = send(w_out, lambda x, z, c, y: (x, z, 1, 3 - y) if c == 0 else None)
    near_in = swap_core(w_in)
    near_out = swap_core(w_out)
    small = jnp.concatenate([b_in, b_out, jnp.zeros((14, D), bf16)], axis=0)

    grad_own, grad_text, grad_live = call(
        pack_kernel, [((ROWS, D), bf16), ((CUT_TXT, D), bf16), ((2, D), f32)], flat_cot, modality, micros=2.5
    )
    grad_mate = swap_pair(grad_own)

    vectors = (ln1_gain, ln1_shift, b_query, b_value, b_attn_out, ln2_gain, ln2_shift)
    query, key, value, probs, attended, hidden_one, unit_own, text_own = forward_attention(
        tie(flat_tokens, grad_own), modality, vectors, (w_query, w_key, w_value, w_attn_out), grad_text, small
    )
    unit_own, text_own = tie((unit_own, text_own), grad_mate, near_in, near_out)
    unit_mate = swap_pair(unit_own)
    got_a, got_b = swap_other(text_own), swap_far(text_own)
    far_in, far_out, tail = tie((far_in, far_out, got_a), unit_mate, got_b)
    far_swap = swap_core(choose(far_in, far_out))
    near_small = swap_core(jnp.concatenate([small, tail[2 * CUT_TXT :]], axis=0))

    text_weights = (w_in, w_out, near_in, near_out)
    vision_weights = text_weights + (far_in, far_out, far_swap)
    smalls = (b_in, got_a, near_small)
    mate_out, mate_back, mate_act, mate_pre = vision_rows(unit_mate, grad_mate, smalls, vision_weights, bf16)
    got_back = swap_pair(mate_back)
    text_home, text_mate, text_a, text_b, units_text, grads_text, text_act, text_pre = text_rows(
        text_own, unit_mate, grad_mate, got_a, tie(got_b, mate_back), b_in, near_small, *text_weights
    )
    texts = (text_home, swap_pair(text_mate), swap_other(text_a), swap_far(text_b))
    own_out, own_back, own_act, own_pre = vision_rows(unit_own, tie(grad_own, text_home), smalls, vision_weights, f32)

    keep, away, bias_rows = pl.pallas_call(
        expert_grads_kernel,
        out_shape=[jax.ShapeDtypeStruct((3 * D, D), bf16)] * 2 + [jax.ShapeDtypeStruct((8, D), f32)],
        in_specs=[VMEM] * 12,
        out_specs=[ANY, ANY, VMEM],
        scratch_shapes=[pltpu.VMEM((2, D, D), bf16), pltpu.SemaphoreType.DMA((2,))],
        cost_estimate=cost(1),
        compiler_params=params(28),
    )(
        unit_own, unit_mate, grad_own, grad_mate, own_act, mate_act, own_pre, mate_pre, units_text, grads_text, text_act, text_pre,
    )

    grad_hidden, grad_attended, grad_w_attn_out, sums_two = call(
        branch_kernel,
        [((ROWS, D), f32), ((ROWS, D), bf16), ((D, D), bf16), ((3, D), f32)],
        own_back, tie(got_back, keep), *texts, modality, flat_cot, hidden_one, attended, ln2_gain, w_attn_out,
        micros=100, mebibytes=20,
    )
    away_got = swap_core(tie(away, got_back, *texts))
    got_out = swap_pair(tie(mate_out, got_back))
    grad_query, grad_key, grad_value = backward_scores(query, key, value, probs, grad_attended)
    size = D // 16
    expert_pieces = call(
        functools.partial(expert_split_kernel, size),
        [((12 * size, D), bf16)] * 4,
        keep, tie(away_got, grad_query, got_out),
        scratch=[pltpu.VMEM((3 * D, D), bf16)], micros=2, mebibytes=20,
    )
    expert_got = shifts(expert_pieces[1:], "xz")
    grad_query = tie(grad_query, *expert_pieces)
    grad_tokens, shared_keep, shared_away = call(
        shared_kernel,
        [((ROWS, D), bf16)] + [((2 * D + VEC, D), bf16)] * 2,
        flat_tokens, ln1_gain, ln1_shift, grad_query, grad_key, grad_value, w_query, w_key, w_value,
        grad_hidden, grad_w_attn_out, sums_two, grad_live, bias_rows,
        micros=11, mebibytes=28,
    )

    shared_got = swap_core(tie(shared_away, expert_got[0]))
    shared_pieces = split([shared_keep, shared_got], 2 * D // 4, VEC, "yx")
    shared_got = shifts(shared_pieces[1:], "yx")
    shared_pieces = split([shared_pieces[0]] + shared_got, 2 * D // 16, VEC, "xz")
    shared_got = shifts(shared_pieces[1:], "xz")
    expert_pieces = call(
        functools.partial(expert_split_again_kernel, size),
        [((3 * size, D), bf16)] * 4,
        expert_pieces[0], *tie(expert_got, *shared_pieces),
        scratch=[pltpu.VMEM((12 * size, D), bf16)],
    )
    expert_got = shifts(expert_pieces[1:], "zx")
    (shared_total,) = call(
        functools.partial(sum_kernel, 2 * D // 16 + VEC),
        [((2 * D // 16 + VEC, D), bf16)],
        shared_pieces[0], *shared_got,
    )
    shared_last = shifts([shared_total] * 3, "zy")
    expert_sum, expert_swap = call(
        functools.partial(expert_sum_kernel, size),
        [((3 * size, D), bf16), ((size, D), bf16)],
        expert_pieces[0], *tie(expert_got, shared_total),
    )
    expert_far = expert_sum[size : 2 * size]
    from_in = send(expert_far, lambda x, z, c, y: (x, z, 0, 3 - y) if c == 0 else None)
    from_out = send(expert_far, lambda x, z, c, y: (x, z, 0, 3 - y) if c == 1 else None)
    from_core = swap_core(expert_swap)
    shared_sum, vec = call(
        functools.partial(sum_kernel, 2 * D // 16),
        [((2 * D // 16, D), bf16), ((VEC, D), f32)],
        shared_total, *tie(shared_last, expert_sum),
    )
    shared_got = shifts([shared_sum] * 3, "xz")
    (expert_sum,) = call(
        functools.partial(expert_place_kernel, size),
        [((2 * size, D), bf16)],
        tie(expert_sum, shared_sum), from_in, from_out, from_core,
    )
    expert_got = shifts([expert_sum] * 3, "zx")
    shared_sum = join(shared_sum, tie(shared_got, expert_sum), "xz")
    shared_got = shifts([shared_sum] * 3, "yx")
    expert_sum = join(tie(expert_sum, shared_sum), expert_got, "zx")
    expert_got = shifts([expert_sum] * 3, "xz")
    shared_sum = join(shared_sum, tie(shared_got, expert_sum), "yx")
    expert_sum = join(tie(expert_sum, shared_sum), expert_got, "xz")
    grad_w_in, grad_w_out = call(functools.partial(expert_finish_kernel, size), [((D, D), f32)] * 2, expert_sum, micros=3)
    outs = finish(shared_sum, swap_core(shared_sum), vec)
    d_query, d_key, d_value, d_out, d_gain1, d_shift1, d_bq, d_bv, d_gain2, d_shift2, d_bo, d_b_in, d_b_out = outs
    (mixed,) = call(
        mixed_kernel,
        [((ROWS, D), bf16)],
        own_out, got_out, *texts, modality, hidden_one, b_out, near_small,
        micros=4, mebibytes=16,
    )
    return (
        mixed.reshape(tokens.shape),
        grad_tokens.reshape(tokens.shape),
        d_gain1,
        d_shift1,
        d_query,
        d_bq,
        d_key,
        d_value,
        d_bv,
        d_out,
        d_bo,
        d_gain2,
        d_shift2,
        grad_w_in[None],
        d_b_in,
        grad_w_out[None],
        d_b_out,
    )


def solution(mesh):
    items = P(AXES, None, None)
    expert_specs = (P("expert", None, "ffn"), P("expert", "ffn"), P("expert", "ffn", None), P("expert", None))
    return jax.shard_map(
        body,
        mesh=mesh,
        in_specs=(items, items, P(AXES, None)) + (P(),) * 11 + expert_specs,
        out_specs=(items, items) + (P(),) * 11 + expert_specs,
        check_vma=False,
    )
```

```python
import functools

import jax
import jax.numpy as jnp
from jax import lax
from jax.experimental import pallas as pl
from jax.experimental.pallas import tpu as pltpu
from jax.sharding import PartitionSpec as P

D = 768
HEAD_DIM = 64
HEADS = D // HEAD_DIM
PATCHES = 197
SEQ = 256
ITEMS = 2
ROWS = ITEMS * SEQ
TEXT_AT = 192
VIS = 208
TXT = 48
CUT = ITEMS * VIS
CUT_TXT = ITEMS * TXT
SENT = VIS + CUT_TXT + TXT + 16
BACK = VIS + CUT_TXT
VEC = 24

epsilon = 1e-05
root_half = 0.7071067811865476
inv_root_tau = 0.3989422804014327
AXES = ("dp", "expert", "ffn")
bf16 = jnp.bfloat16
f32 = jnp.float32


def split_index(index):
    return index // 32, index // 8 % 4, index // 4 % 2, index % 4


def join_index(x, z, core, y):
    return ((x * 4 + z) * 2 + core) * 4 + y


def send(value, where):
    pairs = []
    for index in range(128):
        target = where(*split_index(index))
        if target is not None:
            pairs.append((index, join_index(*target)))
    return lax.ppermute(value, AXES, pairs)


def swap_core(value):
    return send(value, lambda x, z, c, y: (x, z, 1 - c, y))


def swap_pair(value):
    return send(value, lambda x, z, c, y: (x, z, c, y ^ 1))


def swap_other(value):
    return send(value, lambda x, z, c, y: (x, z, c, 3 - y))


def swap_far(value):
    return send(value, lambda x, z, c, y: (x, z, c, y ^ 2))


def shift(value, axes, step):
    def where(x, z, c, y):
        at = dict(x=x, z=z, y=y)
        at[axes[c]] = (at[axes[c]] + step) % 4
        return at["x"], at["z"], c, at["y"]

    return send(value, where)


def shifts(pieces, axes):
    return [shift(piece, axes, step) for piece, step in zip(pieces, (1, 3, 2))]


def tie(value, *others):
    return lax.optimization_barrier((value, others))[0]


def core_index():
    return lax.axis_index("expert")


def place(axes):
    dp = lax.axis_index("dp")
    at = dict(x=dp // 4, z=dp % 4, y=lax.axis_index("ffn"))
    return jnp.where(core_index() == 0, at[axes[0]], at[axes[1]])


def norm_forward(values, gain_vec, shift_vec):
    centre = values - jnp.mean(values, axis=-1, keepdims=True)
    scaled = lax.rsqrt(jnp.mean(centre * centre, axis=-1, keepdims=True) + epsilon)
    normal_hat = centre * scaled
    return (normal_hat * gain_vec + shift_vec, normal_hat, scaled)


def norm_backward(grad_result, normal_hat, scaled, gain_vec):
    grad_hat = grad_result * gain_vec
    inner_term = (
        grad_hat
        - jnp.mean(grad_hat, axis=-1, keepdims=True)
        - normal_hat * jnp.mean(grad_hat * normal_hat, axis=-1, keepdims=True)
    )
    return (
        scaled * inner_term,
        jnp.sum(grad_result * normal_hat, axis=0, keepdims=True),
        jnp.sum(grad_result, axis=0, keepdims=True),
    )


def matmul(first_op, second_op):
    return jnp.dot(first_op, second_op, preferred_element_type=f32)


def contract_rows(first_op, second_op):
    return lax.dot_general(first_op, second_op, (((0,), (0,)), ((), ())), preferred_element_type=f32)


def times_transpose(first_op, second_op):
    return lax.dot_general(first_op, second_op, (((1,), (1,)), ((), ())), preferred_element_type=f32)


def vector(ref):
    return ref[...].astype(f32).reshape(1, D)


def slots_of(row):
    has_image = jnp.max(jnp.where(row == 0, 1.0, 0.0), axis=1, keepdims=True)
    texts = jnp.sum(jnp.where(row == 1, 1.0, 0.0), axis=1, keepdims=True)
    start = has_image * PATCHES
    slot = lax.broadcasted_iota(jnp.int32, (SEQ, 1), 0).astype(f32)
    modal = jnp.where(slot < start, 0.0, jnp.where(slot < start + texts, 1.0, 2.0))
    return has_image > 0.5, modal


def text_of(rows, has_image, modal):
    at = slice(TEXT_AT, TEXT_AT + TXT)
    return jnp.where(has_image, jnp.where(modal[at] == 1, rows[at], 0.0), jnp.where(modal[:TXT] == 1, rows[:TXT], 0.0))


def unpack_item(vision, text, has_image, modal):
    whole = jnp.concatenate(
        [
            jnp.where(has_image, vision[:TXT], text),
            vision[TXT:TEXT_AT],
            jnp.where(modal[TEXT_AT:VIS] == 1, text[: VIS - TEXT_AT], vision[TEXT_AT:]),
            text[VIS - TEXT_AT :],
            jnp.zeros((SEQ - TEXT_AT - TXT, D), f32),
        ],
        axis=0,
    )
    return jnp.where(modal < 2, whole, 0.0)


VMEM = pl.BlockSpec(memory_space=pltpu.VMEM)
ANY = pl.BlockSpec(memory_space=pl.ANY)


def cost(micros):
    return pl.CostEstimate(flops=0, bytes_accessed=int(micros * 1e5), transcendentals=0)


def params(mebibytes):
    return pltpu.CompilerParams(vmem_limit_bytes=mebibytes * 1024 * 1024)


def call(kernel, outs, *args, scratch=(), any_from=None, micros=1.5, mebibytes=12):
    specs = [VMEM] * len(args) if any_from is None else [VMEM] * any_from + [ANY] * (len(args) - any_from)
    return pl.pallas_call(
        kernel,
        out_shape=[jax.ShapeDtypeStruct(shape, dtype) for shape, dtype in outs],
        in_specs=specs,
        out_specs=[VMEM] * len(outs),
        scratch_shapes=list(scratch),
        cost_estimate=cost(micros),
        compiler_params=params(mebibytes),
    )(*args)


def pack_kernel(grad_ref, modal_ref, out_ref, sum_ref):
    sums = [0.0, 0.0]
    for item in range(ITEMS):
        has_image, modal = slots_of(modal_ref[item : item + 1])
        grad = grad_ref[item * SEQ : (item + 1) * SEQ].astype(f32)
        vision = jnp.where(modal[:VIS] == 0, grad[:VIS], 0.0)
        out_ref[item * VIS : (item + 1) * VIS] = vision.astype(bf16)
        sums[0] += jnp.sum(vision, axis=0, keepdims=True)
        sums[1] += jnp.sum(text_of(grad, has_image, modal), axis=0, keepdims=True)
    sum_ref[...] = jnp.concatenate(sums, axis=0)


def part_kernel(w_in, w_out, grad, b_in, b_out, in_ref, out_ref, first_ref, second_ref, sems):
    dp, share = lax.axis_index("dp"), D // 4
    x, z = lax.div(dp, 4), lax.rem(dp, 4)
    copies = [
        pltpu.make_async_copy(w_in.at[pl.ds(pl.multiple_of(x * share, 16), share)], in_ref.at[:share], sems.at[0]),
        pltpu.make_async_copy(w_out.at[pl.ds(pl.multiple_of(z * share, 16), share)], out_ref.at[:share], sems.at[1]),
        pltpu.make_async_copy(grad.at[:SEQ], first_ref, sems.at[2]),
        pltpu.make_async_copy(grad.at[SEQ:], second_ref, sems.at[3]),
    ]
    for copy in copies:
        copy.start()
    small = [b_in[...].astype(f32), b_out[...].astype(f32), jnp.zeros((14, D), f32)]
    small = jnp.concatenate(small, axis=0).astype(bf16)
    in_ref[share:] = small
    out_ref[share:] = small
    for copy in copies:
        copy.wait()


def parts(*args):
    return pl.pallas_call(
        part_kernel,
        out_shape=[jax.ShapeDtypeStruct((D // 4 + 16, D), bf16)] * 2 + [jax.ShapeDtypeStruct((SEQ, D), bf16)] * 2,
        in_specs=[ANY] * 3 + [VMEM] * 2,
        out_specs=[VMEM] * 4,
        scratch_shapes=[pltpu.SemaphoreType.DMA((4,))],
        cost_estimate=cost(1),
        compiler_params=params(60),
    )(*args)


def forward_kernel(
    tok_ref, modal_ref, gain1, shift1, b_query, b_value, b_out, gain2, shift2, wq_ref, wk_ref, wv_ref, wo_ref,
    cot_ref, small_in, small_out, q_out, k_out, v_out, p_out, att_out, hid_out, first_out, second_out, text_out,
    held, sems, q_all, k_all, v_all, p_all, att_all, hid_all, out_sems, first_ref, second_ref, text_ref, sent_sems,
):
    item = pl.program_id(0)
    pieces = 4
    rows = D // pieces

    def weight_copy(i, piece):
        at = pl.ds(piece * rows, rows)
        return pltpu.make_async_copy((wq_ref, wk_ref, wv_ref, wo_ref)[i].at[at], held.at[i, at], sems.at[i, piece])

    def start_weight(i):
        @pl.when(item == 0)
        def _():
            for piece in range(pieces):
                weight_copy(i, piece).start()

    def wait_weight(i):
        @pl.when(item == 0)
        def _():
            for piece in range(pieces):
                weight_copy(i, piece).wait()

    start_weight(0)

    @pl.when(item == 0)
    def _():
        small = [small_in[...].astype(f32), small_out[...].astype(f32), jnp.zeros((14, D), f32)]
        text_ref[2 * CUT_TXT :] = jnp.concatenate(small, axis=0).astype(bf16)
        modal = jnp.concatenate([modal_ref[...].astype(f32), jnp.zeros((16 - ITEMS, SEQ), f32)], axis=0)
        modal = jnp.concatenate([modal, jnp.zeros((16, D - SEQ), f32)], axis=1).astype(bf16)
        first_ref[SENT - 16 :] = modal
        second_ref[SENT - 16 :] = modal

    outs = [(q_all, q_out), (k_all, k_out), (v_all, v_out), (p_all, p_out), (att_all, att_out), (hid_all, hid_out)]

    def copy_out(i, at):
        return pltpu.make_async_copy(outs[i][0].at[at], outs[i][1].at[at], out_sems.at[at, i])

    sent = [
        (first_ref.at[:VIS], first_out.at[:VIS]),
        (second_ref.at[:VIS], second_out.at[:VIS]),
        (first_ref.at[VIS:], first_out.at[VIS:]),
        (second_ref.at[VIS:], second_out.at[VIS:]),
        (text_ref, text_out),
    ]
    sent = [pltpu.make_async_copy(source, target, sent_sems.at[i]) for i, (source, target) in enumerate(sent)]

    q_ref, k_ref, v_ref, p_ref, att_ref = (ref.at[item] for ref in (q_all, k_all, v_all, p_all, att_all))
    x = tok_ref[...].astype(f32)
    unit, _, _ = norm_forward(x, vector(gain1), vector(shift1))
    unit = unit.astype(bf16)
    start_weight(1)
    wait_weight(0)
    q_ref[...] = ((matmul(unit, held[0]) + vector(b_query)).astype(bf16) * 0.125).astype(bf16)
    copy_out(0, item).start()
    start_weight(2)
    wait_weight(1)
    k_ref[...] = matmul(unit, held[1]).astype(bf16)
    copy_out(1, item).start()
    start_weight(3)
    wait_weight(2)
    v_ref[...] = (matmul(unit, held[2]) + vector(b_value)).astype(bf16)
    copy_out(2, item).start()
    row = modal_ref[pl.ds(item, 1)]
    bias = jnp.where(row < 2, 0.0, -1e30)
    low_half = lax.broadcasted_iota(jnp.int32, (1, 128), 1) < HEAD_DIM
    ones = jnp.ones((SEQ, 128), bf16)
    for pair in range(HEADS // 2):
        lanes = slice(pair * 128, (pair + 1) * 128)
        q, k, v = q_ref[:, lanes], k_ref[:, lanes], v_ref[:, lanes]
        halves = []
        for half in range(2):
            mine = low_half if half == 0 else jnp.logical_not(low_half)
            scores = times_transpose(jnp.where(mine, q, 0).astype(bf16), k) + bias
            scores = jnp.exp(scores - jnp.max(scores, axis=-1, keepdims=True))
            both = matmul(scores.astype(bf16), jnp.concatenate([v, ones], axis=1))
            inverse = 1.0 / both[:, 128:]
            p_ref[2 * pair + half] = (scores * jnp.concatenate([inverse, inverse], axis=1)).astype(bf16)
            halves.append(both[:, :128] * inverse)
        att_ref[:, lanes] = jnp.where(low_half, halves[0], halves[1]).astype(bf16)
    copy_out(3, item).start()
    copy_out(4, item).start()
    wait_weight(3)
    hidden = x + matmul(att_ref[...], held[3]) + vector(b_out)
    hid_all[item] = hidden
    copy_out(5, item).start()
    unit, _, _ = norm_forward(hidden, vector(gain2), vector(shift2))
    has_image, modal = slots_of(row)
    grad_text = text_of(cot_ref[...].astype(f32), has_image, modal).astype(bf16)
    text_ref[pl.ds(pl.multiple_of(CUT_TXT + item * TXT, 16), TXT)] = grad_text
    vision = unit[:VIS].astype(bf16)
    text = jnp.where(has_image, unit[TEXT_AT : TEXT_AT + TXT], unit[:TXT]).astype(bf16)
    text_ref[pl.ds(pl.multiple_of(item * TXT, 16), TXT)] = text
    first_ref[pl.ds(pl.multiple_of(VIS + item * TXT, 16), TXT)] = text
    second_ref[pl.ds(pl.multiple_of(VIS + item * TXT, 16), TXT)] = text

    @pl.when(item == 0)
    def _():
        first_ref[:VIS] = vision
        second_ref[BACK : BACK + TXT] = grad_text
        sent[0].start()

    @pl.when(item == 1)
    def _():
        second_ref[:VIS] = vision
        first_ref[BACK : BACK + TXT] = grad_text
        for copy in sent[1:]:
            copy.start()
        for at in range(ITEMS):
            for i in range(len(outs)):
                copy_out(i, at).wait()
        for copy in sent:
            copy.wait()


def forward_attention(tokens, modality, vectors, weights, *rest):
    block = pl.BlockSpec((SEQ, D), lambda i: (i, 0))
    shapes = [((ITEMS, SEQ, D), bf16)] * 3 + [((ITEMS, HEADS, SEQ, SEQ), bf16), ((ITEMS, SEQ, D), bf16), ((ITEMS, SEQ, D), f32)]
    sent = [((SENT, D), bf16), ((SENT, D), bf16), ((2 * CUT_TXT + 16, D), bf16)]
    outs = pl.pallas_call(
        forward_kernel,
        grid=(ITEMS,),
        out_shape=[jax.ShapeDtypeStruct(*s) for s in shapes + sent],
        in_specs=[block] + [VMEM] * 8 + [ANY] * 4 + [block] + [VMEM] * 2,
        out_specs=[ANY] * 9,
        scratch_shapes=[pltpu.VMEM((4, D, D), bf16), pltpu.SemaphoreType.DMA((4, 4))]
        + [pltpu.VMEM(*s) for s in shapes]
        + [pltpu.SemaphoreType.DMA((ITEMS, 6))]
        + [pltpu.VMEM(*s) for s in sent]
        + [pltpu.SemaphoreType.DMA((5,))],
        cost_estimate=cost(10),
        compiler_params=params(56),
    )(tokens, modality, *vectors, *weights, *rest)
    flat = [out.reshape(ROWS, D) for out in outs[:3]]
    return flat + [outs[3], outs[4].reshape(ROWS, D), outs[5].reshape(ROWS, D)] + list(outs[6:])


def fetch(first, second, buffer, sem):
    @pl.when(core_index() == 0)
    def _():
        pltpu.make_async_copy(first, buffer, sem).start()

    @pl.when(core_index() == 1)
    def _():
        pltpu.make_async_copy(second, buffer, sem).start()


def row_pass(unit, grad, first, bias, second, act_ref, pre_ref, base):
    for at in range(0, D, 256):
        cols = slice(at, at + 256)
        kept = slice(base + at, base + at + 256)
        pre_act = matmul(unit, first[:, cols]) + bias[:, cols]
        cdf = 0.5 + 0.5 * lax.erf(pre_act * root_half)
        act_ref[:, kept] = (pre_act * cdf).astype(bf16)
        slope = cdf + pre_act * (jnp.exp(-0.5 * pre_act * pre_act) * inv_root_tau)
        pre_ref[:, kept] = (times_transpose(grad, second[cols, :]) * slope).astype(bf16)


def vision_kernel(
    mates, first_unit, second_unit, grad_ref, text_ref, b_in, far_part, near_small,
    w_in, w_out, near_in, near_out, far_mine, far_other, *refs,
):
    outs, (act_ref, pre_ref, held, sems, units) = refs[:-5], refs[-5:]
    fetch(w_in, near_in, held.at[0], sems.at[0])
    fetch(w_out, near_out, held.at[1], sems.at[1])
    fetch(far_mine, far_other, held.at[2], sems.at[2])
    fetch(far_other, far_mine, held.at[3], sems.at[3])
    first = core_index() == 0
    biases = (
        jnp.where(first, b_in[...].astype(f32), near_small[0:1].astype(f32)),
        far_part[D // 4 : D // 4 + 1].astype(f32),
    )
    units[:VIS] = first_unit[:VIS]
    units[VIS:] = second_unit[:VIS]
    unit, grad = units[...], grad_ref[...]
    for part in range(2):
        for slot in (2 * part, 2 * part + 1):
            pltpu.make_async_copy(w_in, held.at[slot], sems.at[slot]).wait()
        row_pass(unit, grad, held.at[2 * part], biases[part], held.at[2 * part + 1], act_ref, pre_ref, part * D)
    back = times_transpose(pre_ref[:, :D], held[0]) + times_transpose(pre_ref[:, D:], held[2])
    out = matmul(act_ref[:, :D], held[1]) + matmul(act_ref[:, D:], held[3])
    if mates:
        for item in range(2):
            at = slice(item * VIS, (item + 1) * VIS)
            outs[item][:VIS] = back[at].astype(bf16)
            outs[item][VIS:] = text_ref[2 * item * CUT_TXT : (2 * item + 1) * CUT_TXT]
            outs[2 + item][:VIS] = out[at].astype(bf16)
            outs[2 + item][VIS:] = text_ref[(2 * item + 1) * CUT_TXT : (2 * item + 2) * CUT_TXT]
    else:
        outs[0][:CUT] = back
        outs[0][CUT:] = text_ref[:CUT_TXT]
        outs[1][:CUT] = out
        outs[1][CUT:] = text_ref[CUT_TXT:]


def vision_rows(mates, units, grad, text, smalls, weights):
    outs = [((BACK, D), bf16)] * 4 if mates else [((ROWS, D), f32)] * 2
    outs += [((CUT, 2 * D), bf16)] * 2
    scratch = [pltpu.VMEM((4, D, D), bf16), pltpu.SemaphoreType.DMA((4,)), pltpu.VMEM((CUT, D), bf16)]
    kernel = functools.partial(vision_kernel, mates)
    return call(kernel, outs, *units, grad, text, *smalls, *weights, scratch=scratch, any_from=7, micros=3, mebibytes=28)


def text_kernel(
    own_text, got_first, got_second, got_b, cot_first, cot_second, b_in, near_small, w_in, w_out, near_in, near_out,
    home_ref, mates_ref, b_ref, mate_grad, unit_ref, grad_ref, act_ref, pre_ref, held, sems,
):
    fetch(near_in, w_in, held.at[0], sems.at[0])
    fetch(near_out, w_out, held.at[1], sems.at[1])
    unit_ref[:CUT_TXT] = own_text[:CUT_TXT]
    unit_ref[CUT_TXT : 2 * CUT_TXT] = got_first[VIS:BACK]
    unit_ref[2 * CUT_TXT : 3 * CUT_TXT] = got_second[VIS:BACK]
    unit_ref[3 * CUT_TXT :] = got_b[:CUT_TXT]
    grad_ref[:CUT_TXT] = own_text[CUT_TXT : 2 * CUT_TXT]
    grad_ref[3 * CUT_TXT :] = got_b[CUT_TXT : 2 * CUT_TXT]
    for item, got, cot in ((0, got_first, cot_first), (1, got_second, cot_second)):
        modality = got[SENT - 16 : SENT, :SEQ].astype(f32)
        has_image, modal = slots_of(modality[item : item + 1])
        grad = cot[...].astype(f32)
        mate_grad[item * VIS : (item + 1) * VIS] = jnp.where(modal[:VIS] == 0, grad[:VIS], 0.0).astype(bf16)
        at = (item + 1) * CUT_TXT
        here, there = at + item * TXT, at + (1 - item) * TXT
        grad_ref[here : here + TXT] = text_of(grad, has_image, modal).astype(bf16)
        grad_ref[there : there + TXT] = got[BACK : BACK + TXT]
    bias = jnp.where(core_index() == 0, near_small[0:1].astype(f32), b_in[...].astype(f32))
    for slot in range(2):
        pltpu.make_async_copy(w_in, held.at[slot], sems.at[slot]).wait()
    row_pass(unit_ref[...], grad_ref[...], held.at[0], bias, held.at[1], act_ref, pre_ref, 0)
    back = times_transpose(pre_ref[...], held[0])
    out = matmul(act_ref[...], held[1])
    for piece, (target, base) in enumerate(((home_ref, 0), (mates_ref, 0), (mates_ref, 2 * CUT_TXT), (b_ref, 0))):
        at = slice(piece * CUT_TXT, (piece + 1) * CUT_TXT)
        target[base : base + CUT_TXT] = back[at].astype(target.dtype)
        target[base + CUT_TXT : base + 2 * CUT_TXT] = out[at].astype(target.dtype)


def text_rows(*args):
    outs = [((2 * CUT_TXT, D), f32), ((4 * CUT_TXT, D), bf16), ((2 * CUT_TXT, D), bf16), ((CUT, D), bf16)]
    outs += [((4 * CUT_TXT, D), bf16)] * 4
    scratch = [pltpu.VMEM((2, D, D), bf16), pltpu.SemaphoreType.DMA((2,))]
    return call(text_kernel, outs, *args, scratch=scratch, any_from=8, micros=5, mebibytes=20)


class Outputs:
    def __init__(self, keep, away, blocks, sems):
        self.keep, self.away, self.blocks, self.sems, self.pending = keep, away, blocks, sems, []

    def put(self, index, value, kind):
        slot = len(self.pending) % 2
        if len(self.pending) >= 2:
            self.pending[-2].wait()
        self.blocks[slot] = value.astype(bf16)
        rows = pl.ds(index * D, D)
        kept = core_index() == kind

        @pl.when(kept)
        def _():
            pltpu.make_async_copy(self.blocks.at[slot], self.keep.at[rows], self.sems.at[slot]).start()

        @pl.when(jnp.logical_not(kept))
        def _():
            pltpu.make_async_copy(self.blocks.at[slot], self.away.at[rows], self.sems.at[slot]).start()

        self.pending.append(pltpu.make_async_copy(self.blocks.at[slot], self.keep.at[rows], self.sems.at[slot]))

    def finish(self):
        for copy in self.pending[-2:]:
            copy.wait()


def column_sum(value):
    return jnp.sum(value.astype(f32), axis=0, keepdims=True)


def near_grads_kernel(
    own_first, own_second, got_first, got_second, grad_own, grad_mate, act_own, act_mate, pre_own, pre_mate,
    unit_text, grad_text, act_text, pre_text, keep_ref, away_ref, units, grads, bias_ref, blocks, sems, acts, pres, in_sems,
):
    near = slice(0, D)
    loads = []

    def load(source, target):
        loads.append(pltpu.make_async_copy(source, target, in_sems.at[len(loads)]))
        loads[-1].start()

    for piece, source in enumerate((own_first, own_second, got_first, got_second)):
        load(source.at[:VIS], units.at[piece * VIS : (piece + 1) * VIS])
    for own, mate, total in ((pre_own, pre_mate, pres), (act_own, act_mate, acts)):
        load(own.at[:, near], total.at[:CUT])
        load(mate.at[:, near], total.at[CUT:])
    load(grad_own, grads.at[:CUT])
    load(grad_mate, grads.at[CUT:])
    outputs = Outputs(keep_ref, away_ref, blocks, sems)
    outputs.put(1, contract_rows(unit_text[...], pre_text[...]), 0)
    outputs.put(1, contract_rows(act_text[...], grad_text[...]), 1)
    for copy in loads[:6]:
        copy.wait()
    outputs.put(0, contract_rows(units[...], pres[...]), 0)
    for copy in loads[6:]:
        copy.wait()
    outputs.put(0, contract_rows(acts[...], grads[...]), 1)
    at_y = lax.axis_index("ffn")
    bias_ref[...] = jnp.zeros_like(bias_ref)
    bias_ref[pl.ds(at_y, 1)] = column_sum(pres[...])
    bias_ref[pl.ds(4 + at_y, 1)] = column_sum(pre_text[...])
    outputs.finish()


def far_grads_kernel(
    units, grads, act_own, act_mate, pre_own, pre_mate, bias_in, keep_ref, away_ref, bias_ref, blocks, sems, acts, pres, in_sems
):
    far = slice(D, 2 * D)
    loads = []
    for own, mate, total in ((pre_own, pre_mate, pres), (act_own, act_mate, acts)):
        for source, target in ((own, total.at[:CUT]), (mate, total.at[CUT:])):
            loads.append(pltpu.make_async_copy(source.at[:, far], target, in_sems.at[len(loads)]))
            loads[-1].start()
    outputs = Outputs(keep_ref, away_ref, blocks, sems)
    for copy in loads[:2]:
        copy.wait()
    outputs.put(0, contract_rows(units[...], pres[...]), 0)
    for copy in loads[2:]:
        copy.wait()
    outputs.put(0, contract_rows(acts[...], grads[...]), 1)
    bias_ref[...] = bias_in[...]
    bias_ref[pl.ds(lax.rem(lax.axis_index("ffn") + 2, 4), 1)] = column_sum(pres[...])
    outputs.finish()


def near_grads(*args):
    rows = jax.ShapeDtypeStruct((2 * CUT, D), bf16)
    return pl.pallas_call(
        near_grads_kernel,
        out_shape=[jax.ShapeDtypeStruct((2 * D, D), bf16)] * 2 + [rows, rows, jax.ShapeDtypeStruct((8, D), f32)],
        in_specs=[ANY] * 10 + [VMEM] * 4,
        out_specs=[ANY, ANY] + [VMEM] * 3,
        scratch_shapes=[pltpu.VMEM((2, D, D), bf16), pltpu.SemaphoreType.DMA((2,))]
        + [pltpu.VMEM((2 * CUT, D), bf16)] * 2
        + [pltpu.SemaphoreType.DMA((10,))],
        cost_estimate=cost(1),
        compiler_params=params(24),
    )(*args)


def far_grads(*args):
    return pl.pallas_call(
        far_grads_kernel,
        out_shape=[jax.ShapeDtypeStruct((D, D), bf16)] * 2 + [jax.ShapeDtypeStruct((8, D), f32)],
        in_specs=[VMEM] * 2 + [ANY] * 4 + [VMEM],
        out_specs=[ANY, ANY, VMEM],
        scratch_shapes=[pltpu.VMEM((2, D, D), bf16), pltpu.SemaphoreType.DMA((2,))]
        + [pltpu.VMEM((2 * CUT, D), bf16)] * 2
        + [pltpu.SemaphoreType.DMA((4,))],
        cost_estimate=cost(1),
        compiler_params=params(24),
    )(*args)


def text_sum(own_ref, got_first, got_second, b_ref, item, base):
    txt = slice(VIS + item * TXT, VIS + (item + 1) * TXT)
    total = own_ref[CUT + item * TXT : CUT + (item + 1) * TXT] + b_ref[base + item * TXT : base + (item + 1) * TXT].astype(f32)
    return total + got_first[txt].astype(f32) + got_second[txt].astype(f32)


def branch_kernel(
    own_ref, got_first, got_second, b_ref, modal_ref, cot_ref, hid_ref, att_ref, gain_ref, wo_ref,
    hidden_ref, gatt_ref, dwo_ref, sum_ref,
):
    gain = vector(gain_ref)
    sums = [0.0, 0.0, 0.0]
    for item in range(ITEMS):
        at = slice(item * SEQ, (item + 1) * SEQ)
        vis = slice(item * VIS, (item + 1) * VIS)
        vision = own_ref[vis] + (got_first, got_second)[item][:VIS].astype(f32)
        text = text_sum(own_ref, got_first, got_second, b_ref, item, 0)
        grad_unit = unpack_item(vision, text, *slots_of(modal_ref[item : item + 1])).astype(bf16).astype(f32)
        _, hat, scaled = norm_forward(hid_ref[at], 1.0, 0.0)
        grad_norm, grad_gain, grad_shift = norm_backward(grad_unit, hat, scaled, gain)
        grad_hidden = cot_ref[at].astype(f32) + grad_norm
        hidden_ref[at] = grad_hidden
        branch = grad_hidden.astype(bf16)
        gatt_ref[at] = branch
        sums[0] += grad_gain
        sums[1] += grad_shift
        sums[2] += jnp.sum(branch.astype(f32), axis=0, keepdims=True)
    dwo_ref[...] = contract_rows(att_ref[...], gatt_ref[...]).astype(bf16)
    gatt_ref[...] = times_transpose(gatt_ref[...], wo_ref[...]).astype(bf16)
    sum_ref[...] = jnp.concatenate(sums, axis=0)


def scores_kernel(q_ref, k_ref, v_ref, p_ref, gatt_ref, gq_ref, gk_ref, gv_ref):
    low_half = lax.broadcasted_iota(jnp.int32, (1, 128), 1) < HEAD_DIM
    for pair in range(HEADS // 2):
        lanes = slice(pair * 128, (pair + 1) * 128)
        q, k, v, g = q_ref[:, lanes], k_ref[:, lanes], v_ref[:, lanes], gatt_ref[:, lanes]
        gq = gk = gv = 0.0
        for half in range(2):
            mine = low_half if half == 0 else jnp.logical_not(low_half)
            mask = lambda a: jnp.where(mine, a, 0).astype(bf16)
            low = p_ref[0, 2 * pair + half]
            probs = low.astype(f32)
            inner = times_transpose(mask(g), v) * probs
            scores = (inner - probs * jnp.sum(inner, axis=-1, keepdims=True)).astype(bf16)
            gv += contract_rows(low, mask(g))
            gq += matmul(scores, mask(k))
            gk += contract_rows(scores, mask(q))
        gq_ref[:, lanes] = (gq * 0.125).astype(bf16)
        gk_ref[:, lanes] = gk.astype(bf16)
        gv_ref[:, lanes] = gv.astype(bf16)


def backward_scores(q, k, v, p, gatt):
    block = pl.BlockSpec((SEQ, D), lambda i: (i, 0))
    heads = pl.BlockSpec((1, HEADS, SEQ, SEQ), lambda i: (i, 0, 0, 0))
    return pl.pallas_call(
        scores_kernel,
        grid=(ITEMS,),
        out_shape=[jax.ShapeDtypeStruct((ROWS, D), bf16)] * 3,
        in_specs=[block] * 3 + [heads, block],
        out_specs=[block] * 3,
        cost_estimate=cost(25),
        compiler_params=params(20),
    )(q, k, v, p, gatt)


def shared_kernel(
    tok_ref, gain1, shift1, gq_ref, gk_ref, gv_ref, wq_ref, wk_ref, wv_ref, hidden_ref, dwo_ref, sums_two, grad_live, bias_rows,
    tok_out, keep_ref, away_ref,
):
    gain = vector(gain1)
    unit, hat, scaled = norm_forward(tok_ref[...].astype(f32), gain, vector(shift1))
    low = unit.astype(bf16)
    dwq = contract_rows(low, gq_ref[...]).astype(bf16)
    dwk = contract_rows(low, gk_ref[...]).astype(bf16)
    dwv = contract_rows(low, gv_ref[...]).astype(bf16)
    back = times_transpose(gq_ref[...], wq_ref[...]) + times_transpose(gk_ref[...], wk_ref[...]) + times_transpose(gv_ref[...], wv_ref[...])
    grad_norm, grad_gain, grad_shift = norm_backward(back, hat, scaled, gain)
    tok_out[...] = (hidden_ref[...] + grad_norm).astype(bf16)
    total = lambda ref: jnp.sum(ref[...].astype(f32), axis=0, keepdims=True)
    rows = [grad_gain, grad_shift, total(gq_ref), total(gv_ref), sums_two[...], grad_live[...], bias_rows[...]]
    vec = jnp.concatenate(rows + [jnp.zeros((VEC - 17, D), f32)], axis=0).astype(bf16)

    def put(mine, other):
        mine[:D] = dwq
        mine[D : 2 * D] = dwk
        other[:D] = dwv
        other[D : 2 * D] = dwo_ref[...]
        mine[2 * D :] = vec
        other[2 * D :] = vec

    @pl.when(core_index() == 0)
    def _():
        put(keep_ref, away_ref)

    @pl.when(core_index() == 1)
    def _():
        put(away_ref, keep_ref)


def mixed_kernel(own_ref, got_first, got_second, b_ref, modal_ref, hid_ref, b_out, near_small, out_ref):
    first = core_index() == 0
    mine, other = b_out[...].astype(f32), near_small[1:2].astype(f32)
    bias_vision, bias_text = jnp.where(first, mine, other), jnp.where(first, other, mine)
    for item in range(ITEMS):
        at = slice(item * SEQ, (item + 1) * SEQ)
        vis = slice(item * VIS, (item + 1) * VIS)
        vision = own_ref[vis] + (got_first, got_second)[item][:VIS].astype(f32) + bias_vision
        text = text_sum(own_ref, got_first, got_second, b_ref, item, CUT_TXT) + bias_text
        rows = unpack_item(vision, text, *slots_of(modal_ref[item : item + 1])).astype(bf16).astype(f32)
        out_ref[at] = (hid_ref[at] + rows).astype(bf16)


def split_kernel(count, size, axes, *refs):
    ins, outs, total = refs[:count], refs[count:-1], refs[-1]
    extra = total.shape[0] - 4 * size
    total[...] = sum(ref[: 4 * size + extra].astype(f32) for ref in ins).astype(bf16)
    me = place(axes)
    for step, out in zip((0, 1, 3, 2), outs):
        at = pl.multiple_of(lax.rem(me + step, 4) * size, 16)
        out[:size] = total[pl.ds(at, size)]
        if extra:
            out[size:] = total[4 * size :]


def split(pieces, size, extra, axes):
    outs = [((size + extra, D), bf16)] * 4
    scratch = [pltpu.VMEM((4 * size + extra, D), bf16)]
    return call(functools.partial(split_kernel, len(pieces), size, axes), outs, *pieces, scratch=scratch)


def block_steps(size):
    first = core_index() == 0
    return jnp.where(first, 4 * size, size), jnp.where(first, size, 4 * size)


def expert_split_kernel(size, near_keep, near_got, far_keep, far_got, *refs):
    outs, total = refs[:-1], refs[-1]
    near = (near_keep[...].astype(f32) + near_got[...].astype(f32)).astype(bf16)
    total[:D] = near[:D]
    total[D : 2 * D] = (far_keep[...].astype(f32) + far_got[...].astype(f32)).astype(bf16)
    total[2 * D :] = near[D:]
    me = place("xz")
    outer, inner = block_steps(size)
    for step, out in zip((0, 1, 3, 2), outs):
        base = lax.rem(me + step, 4) * outer
        for matrix in range(3):
            for block in range(4):
                at = pl.multiple_of(base + matrix * D + block * inner, 16)
                to = (matrix * 4 + block) * size
                out[to : to + size] = total[pl.ds(at, size)]


EXP = D // 16


def expert_second_kernel(*refs):
    ins, outs, total = refs[:4], refs[4:-1], refs[-1]
    total[...] = sum(ref[...].astype(f32) for ref in ins).astype(bf16)
    me = place("zx")
    for step, out in zip((0, 1, 3, 2), outs):
        index = lax.rem(me + step, 4)
        for matrix in range(3):
            at = pl.multiple_of((matrix * 4 + index) * EXP, 16)
            out[matrix * EXP : (matrix + 1) * EXP] = total[pl.ds(at, EXP)]


def expert_third_kernel(*refs):
    ins, outs = refs[:4], refs[4:]
    total = sum(ref[...].astype(f32) for ref in ins).astype(bf16)
    for matrix, out in enumerate(outs):
        out[...] = total[matrix * EXP : (matrix + 1) * EXP]


def expert_keep_kernel(near, far, text, keep, away):
    first = core_index() == 0
    vision, language = near[...].astype(f32) + far[...].astype(f32), text[...].astype(f32)
    keep[...] = jnp.where(first, vision, language).astype(bf16)
    away[...] = jnp.where(first, language, vision).astype(bf16)


def sum_kernel(*refs):
    ins, out = refs[:4], refs[4]
    out[...] = sum(ref[...].astype(f32) for ref in ins).astype(bf16)


def fourth_kernel(*refs):
    ins, (keep, got, out, vec) = refs[:4], refs[4:]
    total = sum(ref[...].astype(f32) for ref in ins)
    out[: 2 * EXP] = total[: 2 * EXP].astype(bf16)
    vec[...] = total[2 * EXP :]
    first = core_index() == 0
    k, g = keep[...].astype(f32), got[...].astype(f32)
    out[2 * EXP : 3 * EXP] = jnp.where(first, k, g).astype(bf16)
    out[3 * EXP :] = jnp.where(first, g, k).astype(bf16)


def fifth_kernel(mine, first, third, second, shared, expert):
    me = place("zx")
    for step, piece in zip((0, 1, 3, 2), (mine, first, third, second)):
        index = lax.rem(me + 4 - step, 4)
        shared[pl.ds(pl.multiple_of(index * 2 * EXP, 16), 2 * EXP)] = piece[: 2 * EXP]
        at = pl.multiple_of(index * EXP, 16)
        expert[pl.ds(at, EXP)] = piece[2 * EXP : 3 * EXP]
        expert[pl.ds(4 * EXP + at, EXP)] = piece[3 * EXP :]


def expert_finish_kernel(low, w_in, w_out):
    outer, inner = block_steps(EXP)
    for p in range(4):
        for q in range(4):
            at = pl.multiple_of(p * outer + q * inner, 16)
            base = (p * 8 + q) * EXP
            w_in[pl.ds(at, EXP)] = low[base : base + EXP].astype(f32)
            w_out[pl.ds(at, EXP)] = low[base + 4 * EXP : base + 5 * EXP].astype(f32)


def join_kernel(axes, *refs):
    ins, out = refs[:4], refs[4]
    size = out.shape[0] // 4
    me = place(axes)
    for step, piece in zip((0, 1, 3, 2), ins):
        at = pl.multiple_of(lax.rem(me + 4 - step, 4) * size, 16)
        out[pl.ds(at, size)] = piece[:size]


def join(piece, got, axes, size=None):
    return call(functools.partial(join_kernel, axes), [((4 * (size or piece.shape[0]), D), bf16)], piece, *got)[0]


def finish_kernel(mine, other, vec, wq, wk, wv, wo, g1, s1, bq, bv, g2, s2, bo, b_in, b_out):
    first = core_index() == 0
    for low, high, at in ((wq, wv, 0), (wk, wo, 1)):
        m, o = mine[at].astype(f32), other[at].astype(f32)
        low[...] = jnp.where(first, m, o)
        high[...] = jnp.where(first, o, m)

    @pl.when(pl.program_id(0) == 0)
    def _():
        for ref, row in ((g1, 0), (s1, 1), (bq, 2), (bv, 3), (g2, 4), (s2, 5), (bo, 6)):
            ref[...] = vec[row]
        b_in[...] = vec[pl.ds(9 + 4 * core_index() + lax.axis_index("ffn"), 1)]
        b_out[...] = vec[pl.ds(7 + core_index(), 1)]


def finish(mine, other, vec):
    steps = 4
    size = D // steps
    pair = pl.BlockSpec((2, size, D), lambda i: (0, i, 0))
    block = pl.BlockSpec((size, D), lambda i: (i, 0))
    return pl.pallas_call(
        finish_kernel,
        grid=(steps,),
        out_shape=[jax.ShapeDtypeStruct((D, D), f32)] * 4
        + [jax.ShapeDtypeStruct((D,), f32)] * 7
        + [jax.ShapeDtypeStruct((1, D), f32)] * 2,
        in_specs=[pair, pair, VMEM],
        out_specs=[block] * 4 + [VMEM] * 9,
        cost_estimate=cost(5),
        compiler_params=params(12),
    )(mine.reshape(2, D, D), other.reshape(2, D, D), vec)


def body(
    tokens,
    cotangent,
    modality,
    ln1_gain,
    ln1_shift,
    w_query,
    b_query,
    w_key,
    w_value,
    b_value,
    w_attn_out,
    b_attn_out,
    ln2_gain,
    ln2_shift,
    w_in,
    b_in,
    w_out,
    b_out,
):
    flat_tokens = tokens.reshape(ROWS, D)
    flat_cot = cotangent.reshape(ROWS, D)
    w_in, w_out = w_in[0], w_out[0]

    part_in, part_out, cot_first, cot_second = parts(w_in, w_out, flat_cot, b_in, b_out)
    part_in = send(part_in, lambda x, z, c, y: (x, z, 0, (y + 2) % 4) if c == 0 else None)
    part_out = send(part_out, lambda x, z, c, y: (x, z, 1, (y + 2) % 4) if c == 0 else None)

    cot_first, cot_second = swap_pair(cot_first), swap_other(cot_second)

    vectors = (ln1_gain, ln1_shift, b_query, b_value, b_attn_out, ln2_gain, ln2_shift)
    query, key, value, probs, attended, hidden_one, own_first, own_second, text_own = forward_attention(
        flat_tokens, modality, vectors, (w_query, w_key, w_value, w_attn_out), flat_cot, b_in, b_out
    )
    sent_first, sent_second, text_own = tie((own_first, own_second, text_own), cot_first, cot_second)
    got_first, got_second, got_b = swap_pair(sent_first), swap_other(sent_second), swap_far(text_own)
    near_in, near_out = swap_core(tie(w_in, own_first)), swap_core(tie(w_out, own_first))
    far_part = jnp.where(core_index() == 0, *tie((part_in, part_out), own_first))
    far_got = shifts([far_part] * 3, "xz")
    near_small = swap_core(tie(text_own[2 * CUT_TXT :], far_got[2]))
    far_mine = join(far_part, tie(far_got, got_first, got_second, got_b, near_small), "xz", D // 4)
    far_other = swap_core(far_mine)

    grad_own, grad_live = call(pack_kernel, [((CUT, D), bf16), ((2, D), f32)], tie(flat_cot, own_first), modality, micros=2)
    text_weights = (w_in, w_out, near_in, near_out)
    vision_weights = text_weights + (far_mine, far_other)
    text_home, text_mates, text_b, grad_mate, units_text, grads_text, text_act, text_pre = text_rows(
        text_own, got_first, got_second, got_b, cot_first, cot_second, b_in, near_small, *text_weights
    )
    got_text = swap_far(text_b)
    smalls = (b_in, far_part, near_small)
    back_first, back_second, out_first, out_second, mate_act, mate_pre = vision_rows(
        True, (got_first, got_second), grad_mate, text_mates, smalls, vision_weights
    )
    back_first, back_second = swap_pair(back_first), swap_other(back_second)
    own_back, own_out, own_act, own_pre = vision_rows(
        False, (own_first, own_second), tie(grad_own, grad_mate, mate_act), text_home, smalls, vision_weights
    )

    near_keep, near_away, units, grads, bias_rows = near_grads(
        own_first, own_second, got_first, got_second, grad_own, grad_mate, own_act, mate_act, own_pre, mate_pre,
        units_text, grads_text, text_act, text_pre,
    )
    far_keep, far_away, bias_rows = far_grads(units, grads, own_act, mate_act, own_pre, mate_pre, bias_rows)
    near_away_got = swap_core(tie(near_away, back_first, back_second, got_text))

    grad_hidden, grad_attended, grad_w_attn_out, sums_two = call(
        branch_kernel,
        [((ROWS, D), f32), ((ROWS, D), bf16), ((D, D), bf16), ((3, D), f32)],
        own_back, tie(back_first, far_keep), back_second, got_text, modality, flat_cot, hidden_one, attended, ln2_gain, w_attn_out,
        micros=100, mebibytes=20,
    )
    far_away_got = swap_core(tie(far_away, back_first, back_second, got_text))
    out_first, out_second = tie((out_first, out_second), back_first, back_second)
    out_first, out_second = swap_pair(out_first), swap_other(out_second)
    expert_pieces = call(
        functools.partial(expert_split_kernel, EXP),
        [((12 * EXP, D), bf16)] * 4,
        near_keep, near_away_got, far_keep, tie(far_away_got, grad_attended),
        scratch=[pltpu.VMEM((3 * D, D), bf16)], micros=2, mebibytes=20,
    )
    expert_got = shifts(expert_pieces[1:], "xz")
    grad_query, grad_key, grad_value = backward_scores(query, key, value, probs, tie(grad_attended, *expert_pieces))
    grad_tokens, shared_keep, shared_away = call(
        shared_kernel,
        [((ROWS, D), bf16)] + [((2 * D + VEC, D), bf16)] * 2,
        flat_tokens, ln1_gain, ln1_shift, grad_query, grad_key, grad_value, w_query, w_key, w_value,
        grad_hidden, grad_w_attn_out, sums_two, grad_live, bias_rows,
        micros=11, mebibytes=28,
    )

    shared_got = swap_core(tie(shared_away, *expert_got, out_first, out_second))
    shared_pieces = split([shared_keep, shared_got], 2 * D // 4, VEC, "xz")
    shared_got = shifts(shared_pieces[1:], "xz")
    expert_pieces = call(
        expert_second_kernel,
        [((3 * EXP, D), bf16)] * 4,
        expert_pieces[0], *tie(expert_got, *shared_pieces),
        scratch=[pltpu.VMEM((12 * EXP, D), bf16)],
    )
    expert_got = shifts(expert_pieces[1:], "zx")
    shared_pieces = split([shared_pieces[0]] + tie(shared_got, *expert_got[:2]), 2 * EXP, VEC, "zx")
    shared_got = shifts(shared_pieces[1:], "zx")
    near, far, text = call(expert_third_kernel, [((EXP, D), bf16)] * 3, expert_pieces[0], *expert_got)
    far = swap_far(far)
    size = 2 * EXP + VEC
    (shared_total,) = call(sum_kernel, [((size, D), bf16)], shared_pieces[0], *tie(shared_got, far))
    shared_got = shifts([shared_total] * 3, "yy")
    expert_keep, expert_away = call(expert_keep_kernel, [((EXP, D), bf16)] * 2, near, far, text)
    low, vec = call(
        fourth_kernel,
        [((4 * EXP, D), bf16), ((VEC, D), f32)],
        shared_total, *shared_got, expert_keep, swap_core(expert_away),
    )
    shared_sum, expert_sum = call(
        fifth_kernel, [((8 * EXP, D), bf16)] * 2, low, *shifts([low] * 3, "zx")
    )
    shared_got = shifts([shared_sum] * 3, "xz")
    expert_got = shifts([expert_sum] * 3, "xz")
    shared_sum = join(shared_sum, shared_got, "xz")
    shared_sum = tie(shared_sum, expert_got[0], expert_got[1])
    outs = finish(shared_sum, swap_core(shared_sum), vec)
    d_query, d_key, d_value, d_out, d_gain1, d_shift1, d_bq, d_bv, d_gain2, d_shift2, d_bo, d_b_in, d_b_out = outs
    expert_sum = join(tie(expert_sum, d_query), expert_got, "xz")
    grad_w_in, grad_w_out = call(expert_finish_kernel, [((D, D), f32)] * 2, expert_sum, micros=3)
    (mixed,) = call(
        mixed_kernel,
        [((ROWS, D), bf16)],
        own_out, out_first, out_second, got_text, modality, hidden_one, b_out, near_small,
        micros=4, mebibytes=16,
    )
    return (
        mixed.reshape(tokens.shape),
        grad_tokens.reshape(tokens.shape),
        d_gain1,
        d_shift1,
        d_query,
        d_bq,
        d_key,
        d_value,
        d_bv,
        d_out,
        d_bo,
        d_gain2,
        d_shift2,
        grad_w_in[None],
        d_b_in,
        grad_w_out[None],
        d_b_out,
    )


def solution(mesh):
    items = P(AXES, None, None)
    expert_specs = (P("expert", None, "ffn"), P("expert", "ffn"), P("expert", "ffn", None), P("expert", None))
    return jax.shard_map(
        body,
        mesh=mesh,
        in_specs=(items, items, P(AXES, None)) + (P(),) * 11 + expert_specs,
        out_specs=(items, items) + (P(),) * 11 + expert_specs,
        check_vma=False,
    )
```

```python
import functools

import jax
import jax.numpy as jnp
from jax import lax
from jax.experimental import pallas as pl
from jax.experimental.pallas import tpu as pltpu
from jax.sharding import PartitionSpec as P

D = 768
HEAD_DIM = 64
HEADS = D // HEAD_DIM
PATCHES = 197
SEQ = 256
ITEMS = 2
ROWS = ITEMS * SEQ
TEXT_AT = 192
VIS = 208
TXT = 48
CUT = ITEMS * VIS
CUT_TXT = ITEMS * TXT
SENT = VIS + CUT_TXT + 16
BACK = VIS + CUT_TXT
VEC = 24

epsilon = 1e-05
root_half = 0.7071067811865476
inv_root_tau = 0.3989422804014327
AXES = ("dp", "expert", "ffn")
bf16 = jnp.bfloat16
f32 = jnp.float32


def split_index(index):
    return index // 32, index // 8 % 4, index // 4 % 2, index % 4


def join_index(x, z, core, y):
    return ((x * 4 + z) * 2 + core) * 4 + y


def send(value, where):
    pairs = []
    for index in range(128):
        target = where(*split_index(index))
        if target is not None:
            pairs.append((index, join_index(*target)))
    return lax.ppermute(value, AXES, pairs)


def swap_core(value):
    return send(value, lambda x, z, c, y: (x, z, 1 - c, y))


def swap_pair(value):
    return send(value, lambda x, z, c, y: (x, z, c, y ^ 1))


def swap_other(value):
    return send(value, lambda x, z, c, y: (x, z, c, 3 - y))


def swap_far(value):
    return send(value, lambda x, z, c, y: (x, z, c, y ^ 2))


def shift(value, axes, step):
    def where(x, z, c, y):
        at = dict(x=x, z=z, y=y)
        at[axes[c]] = (at[axes[c]] + step) % 4
        return at["x"], at["z"], c, at["y"]

    return send(value, where)


def shifts(pieces, axes):
    return [shift(piece, axes, step) for piece, step in zip(pieces, (1, 3, 2))]


def tie(value, *others):
    return lax.optimization_barrier((value, others))[0]


def core_index():
    return lax.axis_index("expert")


def place(axes):
    dp = lax.axis_index("dp")
    at = dict(x=dp // 4, z=dp % 4, y=lax.axis_index("ffn"))
    return jnp.where(core_index() == 0, at[axes[0]], at[axes[1]])


def norm_forward(values, gain_vec, shift_vec):
    centre = values - jnp.mean(values, axis=-1, keepdims=True)
    scaled = lax.rsqrt(jnp.mean(centre * centre, axis=-1, keepdims=True) + epsilon)
    normal_hat = centre * scaled
    return (normal_hat * gain_vec + shift_vec, normal_hat, scaled)


def norm_backward(grad_result, normal_hat, scaled, gain_vec):
    grad_hat = grad_result * gain_vec
    inner_term = (
        grad_hat
        - jnp.mean(grad_hat, axis=-1, keepdims=True)
        - normal_hat * jnp.mean(grad_hat * normal_hat, axis=-1, keepdims=True)
    )
    return (
        scaled * inner_term,
        jnp.sum(grad_result * normal_hat, axis=0, keepdims=True),
        jnp.sum(grad_result, axis=0, keepdims=True),
    )


def matmul(first_op, second_op):
    return jnp.dot(first_op, second_op, preferred_element_type=f32)


def contract_rows(first_op, second_op):
    return lax.dot_general(first_op, second_op, (((0,), (0,)), ((), ())), preferred_element_type=f32)


def times_transpose(first_op, second_op):
    return lax.dot_general(first_op, second_op, (((1,), (1,)), ((), ())), preferred_element_type=f32)


def vector(ref):
    return ref[...].astype(f32).reshape(1, D)


def slots_of(row):
    has_image = jnp.max(jnp.where(row == 0, 1.0, 0.0), axis=1, keepdims=True)
    texts = jnp.sum(jnp.where(row == 1, 1.0, 0.0), axis=1, keepdims=True)
    start = has_image * PATCHES
    slot = lax.broadcasted_iota(jnp.int32, (SEQ, 1), 0).astype(f32)
    modal = jnp.where(slot < start, 0.0, jnp.where(slot < start + texts, 1.0, 2.0))
    return has_image > 0.5, modal


def text_of(rows, has_image, modal):
    at = slice(TEXT_AT, TEXT_AT + TXT)
    return jnp.where(has_image, jnp.where(modal[at] == 1, rows[at], 0.0), jnp.where(modal[:TXT] == 1, rows[:TXT], 0.0))


def unpack_item(vision, text, has_image, modal):
    whole = jnp.concatenate(
        [
            jnp.where(has_image, vision[:TXT], text),
            vision[TXT:TEXT_AT],
            jnp.where(modal[TEXT_AT:VIS] == 1, text[: VIS - TEXT_AT], vision[TEXT_AT:]),
            text[VIS - TEXT_AT :],
            jnp.zeros((SEQ - TEXT_AT - TXT, D), f32),
        ],
        axis=0,
    )
    return jnp.where(modal < 2, whole, 0.0)


VMEM = pl.BlockSpec(memory_space=pltpu.VMEM)
ANY = pl.BlockSpec(memory_space=pl.ANY)


def cost(micros):
    return pl.CostEstimate(flops=0, bytes_accessed=int(micros * 1e5), transcendentals=0)


def params(mebibytes):
    return pltpu.CompilerParams(vmem_limit_bytes=mebibytes * 1024 * 1024)


def call(kernel, outs, *args, scratch=(), any_from=None, micros=1.5, mebibytes=12):
    specs = [VMEM] * len(args) if any_from is None else [VMEM] * any_from + [ANY] * (len(args) - any_from)
    return pl.pallas_call(
        kernel,
        out_shape=[jax.ShapeDtypeStruct(shape, dtype) for shape, dtype in outs],
        in_specs=specs,
        out_specs=[VMEM] * len(outs),
        scratch_shapes=list(scratch),
        cost_estimate=cost(micros),
        compiler_params=params(mebibytes),
    )(*args)


def pack_kernel(grad_ref, modal_ref, out_ref, sum_ref):
    sums = [0.0, 0.0]
    for item in range(ITEMS):
        has_image, modal = slots_of(modal_ref[item : item + 1])
        grad = grad_ref[item * SEQ : (item + 1) * SEQ].astype(f32)
        vision = jnp.where(modal[:VIS] == 0, grad[:VIS], 0.0)
        out_ref[item * VIS : (item + 1) * VIS] = vision.astype(bf16)
        sums[0] += jnp.sum(vision, axis=0, keepdims=True)
        sums[1] += jnp.sum(text_of(grad, has_image, modal), axis=0, keepdims=True)
    sum_ref[...] = jnp.concatenate(sums, axis=0)


def part_kernel(w_in, w_out, grad, b_in, b_out, modal_ref, in_ref, out_ref, first_ref, second_ref, small_ref, sems):
    dp, share = lax.axis_index("dp"), D // 4
    x, z = lax.div(dp, 4), lax.rem(dp, 4)
    copies = [
        pltpu.make_async_copy(w_in.at[pl.ds(pl.multiple_of(x * share, 16), share)], in_ref.at[:share], sems.at[0]),
        pltpu.make_async_copy(w_out.at[pl.ds(pl.multiple_of(z * share, 16), share)], out_ref.at[:share], sems.at[1]),
        pltpu.make_async_copy(grad.at[:SEQ], first_ref.at[:SEQ], sems.at[2]),
        pltpu.make_async_copy(grad.at[SEQ:], second_ref.at[:SEQ], sems.at[3]),
    ]
    for copy in copies:
        copy.start()
    small = [b_in[...].astype(f32), b_out[...].astype(f32), jnp.zeros((14, D), f32)]
    small = jnp.concatenate(small, axis=0).astype(bf16)
    small_ref[...] = small
    in_ref[share:] = small
    out_ref[share:] = small
    for copy in copies:
        copy.wait()
    for item, source, target in ((0, first_ref, second_ref), (1, second_ref, first_ref)):
        text = text_of(source[:SEQ].astype(f32), *slots_of(modal_ref[item : item + 1]))
        target[SEQ:] = text.astype(bf16)


def parts(*args):
    return pl.pallas_call(
        part_kernel,
        out_shape=[jax.ShapeDtypeStruct((D // 4 + 16, D), bf16)] * 2 + [jax.ShapeDtypeStruct((SEQ + TXT, D), bf16)] * 2
        + [jax.ShapeDtypeStruct((16, D), bf16)],
        in_specs=[ANY] * 3 + [VMEM] * 3,
        out_specs=[VMEM] * 5,
        scratch_shapes=[pltpu.SemaphoreType.DMA((4,))],
        cost_estimate=cost(1),
        compiler_params=params(60),
    )(*args)


def forward_kernel(
    tok_ref, modal_ref, gain1, shift1, b_query, b_value, b_out, gain2, shift2, wq_ref, wk_ref, wv_ref, wo_ref,
    cot_ref, q_out, k_out, v_out, p_out, att_out, hid_out, first_out, second_out, text_out,
    held, sems, q_all, k_all, v_all, p_all, att_all, hid_all, out_sems, first_ref, second_ref, text_ref, sent_sems,
):
    item = pl.program_id(0)
    pieces = 4
    rows = D // pieces

    def weight_copy(i, piece):
        at = pl.ds(piece * rows, rows)
        return pltpu.make_async_copy((wq_ref, wk_ref, wv_ref, wo_ref)[i].at[at], held.at[i, at], sems.at[i, piece])

    def start_weight(i):
        @pl.when(item == 0)
        def _():
            for piece in range(pieces):
                weight_copy(i, piece).start()

    def wait_weight(i):
        @pl.when(item == 0)
        def _():
            for piece in range(pieces):
                weight_copy(i, piece).wait()

    start_weight(0)

    @pl.when(item == 0)
    def _():
        modal = jnp.concatenate([modal_ref[...].astype(f32), jnp.zeros((16 - ITEMS, SEQ), f32)], axis=0)
        modal = jnp.concatenate([modal, jnp.zeros((16, D - SEQ), f32)], axis=1).astype(bf16)
        first_ref[SENT - 16 :] = modal
        second_ref[SENT - 16 :] = modal

    outs = [(q_all, q_out), (k_all, k_out), (v_all, v_out), (p_all, p_out), (att_all, att_out), (hid_all, hid_out)]

    def copy_out(i, at):
        return pltpu.make_async_copy(outs[i][0].at[at], outs[i][1].at[at], out_sems.at[at, i])

    sent = [
        (first_ref.at[:VIS], first_out.at[:VIS]),
        (second_ref.at[:VIS], second_out.at[:VIS]),
        (first_ref.at[VIS:], first_out.at[VIS:]),
        (second_ref.at[VIS:], second_out.at[VIS:]),
        (text_ref, text_out),
    ]
    sent = [pltpu.make_async_copy(source, target, sent_sems.at[i]) for i, (source, target) in enumerate(sent)]

    q_ref, k_ref, v_ref, p_ref, att_ref = (ref.at[item] for ref in (q_all, k_all, v_all, p_all, att_all))
    x = tok_ref[...].astype(f32)
    unit, _, _ = norm_forward(x, vector(gain1), vector(shift1))
    unit = unit.astype(bf16)
    start_weight(1)
    wait_weight(0)
    q_ref[...] = ((matmul(unit, held[0]) + vector(b_query)).astype(bf16) * 0.125).astype(bf16)
    copy_out(0, item).start()
    start_weight(2)
    wait_weight(1)
    k_ref[...] = matmul(unit, held[1]).astype(bf16)
    copy_out(1, item).start()
    start_weight(3)
    wait_weight(2)
    v_ref[...] = (matmul(unit, held[2]) + vector(b_value)).astype(bf16)
    copy_out(2, item).start()
    row = modal_ref[pl.ds(item, 1)]
    bias = jnp.where(row < 2, 0.0, -1e30)
    low_half = lax.broadcasted_iota(jnp.int32, (1, 128), 1) < HEAD_DIM
    ones = jnp.ones((SEQ, 128), bf16)
    for pair in range(HEADS // 2):
        lanes = slice(pair * 128, (pair + 1) * 128)
        q, k, v = q_ref[:, lanes], k_ref[:, lanes], v_ref[:, lanes]
        halves = []
        for half in range(2):
            mine = low_half if half == 0 else jnp.logical_not(low_half)
            scores = times_transpose(jnp.where(mine, q, 0).astype(bf16), k) + bias
            scores = jnp.exp(scores - jnp.max(scores, axis=-1, keepdims=True))
            both = matmul(scores.astype(bf16), jnp.concatenate([v, ones], axis=1))
            inverse = 1.0 / both[:, 128:]
            p_ref[2 * pair + half] = (scores * jnp.concatenate([inverse, inverse], axis=1)).astype(bf16)
            halves.append(both[:, :128] * inverse)
        att_ref[:, lanes] = jnp.where(low_half, halves[0], halves[1]).astype(bf16)
    copy_out(3, item).start()
    copy_out(4, item).start()
    wait_weight(3)
    hidden = x + matmul(att_ref[...], held[3]) + vector(b_out)
    hid_all[item] = hidden
    copy_out(5, item).start()
    unit, _, _ = norm_forward(hidden, vector(gain2), vector(shift2))
    has_image, modal = slots_of(row)
    grad_text = text_of(cot_ref[...].astype(f32), has_image, modal).astype(bf16)
    text_ref[pl.ds(pl.multiple_of(CUT_TXT + item * TXT, 16), TXT)] = grad_text
    vision = unit[:VIS].astype(bf16)
    text = jnp.where(has_image, unit[TEXT_AT : TEXT_AT + TXT], unit[:TXT]).astype(bf16)
    text_ref[pl.ds(pl.multiple_of(item * TXT, 16), TXT)] = text
    first_ref[pl.ds(pl.multiple_of(VIS + item * TXT, 16), TXT)] = text
    second_ref[pl.ds(pl.multiple_of(VIS + item * TXT, 16), TXT)] = text

    @pl.when(item == 0)
    def _():
        first_ref[:VIS] = vision
        sent[0].start()

    @pl.when(item == 1)
    def _():
        second_ref[:VIS] = vision
        for copy in sent[1:]:
            copy.start()
        for at in range(ITEMS):
            for i in range(len(outs)):
                copy_out(i, at).wait()
        for copy in sent:
            copy.wait()


def forward_attention(tokens, modality, vectors, weights, *rest):
    block = pl.BlockSpec((SEQ, D), lambda i: (i, 0))
    shapes = [((ITEMS, SEQ, D), bf16)] * 3 + [((ITEMS, HEADS, SEQ, SEQ), bf16), ((ITEMS, SEQ, D), bf16), ((ITEMS, SEQ, D), f32)]
    sent = [((SENT, D), bf16), ((SENT, D), bf16), ((2 * CUT_TXT, D), bf16)]
    outs = pl.pallas_call(
        forward_kernel,
        grid=(ITEMS,),
        out_shape=[jax.ShapeDtypeStruct(*s) for s in shapes + sent],
        in_specs=[block] + [VMEM] * 8 + [ANY] * 4 + [block],
        out_specs=[ANY] * 9,
        scratch_shapes=[pltpu.VMEM((4, D, D), bf16), pltpu.SemaphoreType.DMA((4, 4))]
        + [pltpu.VMEM(*s) for s in shapes]
        + [pltpu.SemaphoreType.DMA((ITEMS, 6))]
        + [pltpu.VMEM(*s) for s in sent]
        + [pltpu.SemaphoreType.DMA((5,))],
        cost_estimate=cost(10),
        compiler_params=params(56),
    )(tokens, modality, *vectors, *weights, *rest)
    flat = [out.reshape(ROWS, D) for out in outs[:3]]
    return flat + [outs[3], outs[4].reshape(ROWS, D), outs[5].reshape(ROWS, D)] + list(outs[6:])


def fetch(first, second, buffer, sem):
    @pl.when(core_index() == 0)
    def _():
        pltpu.make_async_copy(first, buffer, sem).start()

    @pl.when(core_index() == 1)
    def _():
        pltpu.make_async_copy(second, buffer, sem).start()


def row_pass(unit, grad, first, bias, second, act_ref, pre_ref, base):
    for at in range(0, D, 256):
        cols = slice(at, at + 256)
        kept = slice(base + at, base + at + 256)
        pre_act = matmul(unit, first[:, cols]) + bias[:, cols]
        cdf = 0.5 + 0.5 * lax.erf(pre_act * root_half)
        act_ref[:, kept] = (pre_act * cdf).astype(bf16)
        slope = cdf + pre_act * (jnp.exp(-0.5 * pre_act * pre_act) * inv_root_tau)
        pre_ref[:, kept] = (times_transpose(grad, second[cols, :]) * slope).astype(bf16)


def vision_kernel(
    mates, first_unit, second_unit, grad_ref, text_ref, b_in, far_part, near_small,
    w_in, w_out, near_in, near_out, far_mine, far_other, *refs,
):
    outs, (act_ref, pre_ref, held, sems, units) = refs[:-5], refs[-5:]
    fetch(w_in, near_in, held.at[0], sems.at[0])
    fetch(w_out, near_out, held.at[1], sems.at[1])
    fetch(far_mine, far_other, held.at[2], sems.at[2])
    fetch(far_other, far_mine, held.at[3], sems.at[3])
    first = core_index() == 0
    biases = (
        jnp.where(first, b_in[...].astype(f32), near_small[0:1].astype(f32)),
        far_part[D // 4 : D // 4 + 1].astype(f32),
    )
    units[:VIS] = first_unit[:VIS]
    units[VIS:] = second_unit[:VIS]
    unit, grad = units[...], grad_ref[...]
    for part in range(2):
        for slot in (2 * part, 2 * part + 1):
            pltpu.make_async_copy(w_in, held.at[slot], sems.at[slot]).wait()
        row_pass(unit, grad, held.at[2 * part], biases[part], held.at[2 * part + 1], act_ref, pre_ref, part * D)
    back = times_transpose(pre_ref[:, :D], held[0]) + times_transpose(pre_ref[:, D:], held[2])
    out = matmul(act_ref[:, :D], held[1]) + matmul(act_ref[:, D:], held[3])
    if mates:
        for item in range(2):
            at = slice(item * VIS, (item + 1) * VIS)
            outs[item][:VIS] = back[at].astype(bf16)
            outs[item][VIS:] = text_ref[2 * item * CUT_TXT : (2 * item + 1) * CUT_TXT]
            outs[2 + item][:VIS] = out[at].astype(bf16)
            outs[2 + item][VIS:] = text_ref[(2 * item + 1) * CUT_TXT : (2 * item + 2) * CUT_TXT]
    else:
        outs[0][:CUT] = back
        outs[0][CUT:] = text_ref[:CUT_TXT]
        outs[1][:CUT] = out
        outs[1][CUT:] = text_ref[CUT_TXT:]


def vision_rows(mates, units, grad, text, smalls, weights):
    outs = [((BACK, D), bf16)] * 4 if mates else [((ROWS, D), f32)] * 2
    outs += [((CUT, 2 * D), bf16)] * 2
    scratch = [pltpu.VMEM((4, D, D), bf16), pltpu.SemaphoreType.DMA((4,)), pltpu.VMEM((CUT, D), bf16)]
    kernel = functools.partial(vision_kernel, mates)
    return call(kernel, outs, *units, grad, text, *smalls, *weights, scratch=scratch, any_from=7, micros=3, mebibytes=28)


def text_kernel(
    own_text, got_first, got_second, got_b, cot_first, cot_second, b_in, near_small, w_in, w_out, near_in, near_out,
    home_ref, mates_ref, b_ref, mate_grad, unit_ref, grad_ref, act_ref, pre_ref, held, sems,
):
    fetch(near_in, w_in, held.at[0], sems.at[0])
    fetch(near_out, w_out, held.at[1], sems.at[1])
    unit_ref[:CUT_TXT] = own_text[:CUT_TXT]
    unit_ref[CUT_TXT : 2 * CUT_TXT] = got_first[VIS:BACK]
    unit_ref[2 * CUT_TXT : 3 * CUT_TXT] = got_second[VIS:BACK]
    unit_ref[3 * CUT_TXT :] = got_b[:CUT_TXT]
    grad_ref[:CUT_TXT] = own_text[CUT_TXT : 2 * CUT_TXT]
    grad_ref[3 * CUT_TXT :] = got_b[CUT_TXT : 2 * CUT_TXT]
    for item, got, cot in ((0, got_first, cot_first), (1, got_second, cot_second)):
        modality = got[SENT - 16 : SENT, :SEQ].astype(f32)
        has_image, modal = slots_of(modality[item : item + 1])
        grad = cot[:SEQ].astype(f32)
        mate_grad[item * VIS : (item + 1) * VIS] = jnp.where(modal[:VIS] == 0, grad[:VIS], 0.0).astype(bf16)
        at = (item + 1) * CUT_TXT
        here, there = at + item * TXT, at + (1 - item) * TXT
        grad_ref[here : here + TXT] = text_of(grad, has_image, modal).astype(bf16)
        grad_ref[there : there + TXT] = cot[SEQ:]
    bias = jnp.where(core_index() == 0, near_small[0:1].astype(f32), b_in[...].astype(f32))
    for slot in range(2):
        pltpu.make_async_copy(w_in, held.at[slot], sems.at[slot]).wait()
    row_pass(unit_ref[...], grad_ref[...], held.at[0], bias, held.at[1], act_ref, pre_ref, 0)
    back = times_transpose(pre_ref[...], held[0])
    out = matmul(act_ref[...], held[1])
    for piece, (target, base) in enumerate(((home_ref, 0), (mates_ref, 0), (mates_ref, 2 * CUT_TXT), (b_ref, 0))):
        at = slice(piece * CUT_TXT, (piece + 1) * CUT_TXT)
        target[base : base + CUT_TXT] = back[at].astype(target.dtype)
        target[base + CUT_TXT : base + 2 * CUT_TXT] = out[at].astype(target.dtype)


def text_rows(*args):
    outs = [((2 * CUT_TXT, D), f32), ((4 * CUT_TXT, D), bf16), ((2 * CUT_TXT, D), bf16), ((CUT, D), bf16)]
    outs += [((4 * CUT_TXT, D), bf16)] * 4
    scratch = [pltpu.VMEM((2, D, D), bf16), pltpu.SemaphoreType.DMA((2,))]
    return call(text_kernel, outs, *args, scratch=scratch, any_from=8, micros=5, mebibytes=20)


class Outputs:
    def __init__(self, keep, away, blocks, sems):
        self.keep, self.away, self.blocks, self.sems, self.pending = keep, away, blocks, sems, []

    def put(self, index, value, kind):
        slot = len(self.pending) % 2
        if len(self.pending) >= 2:
            self.pending[-2].wait()
        self.blocks[slot] = value.astype(bf16)
        rows = pl.ds(index * D, D)
        kept = core_index() == kind

        @pl.when(kept)
        def _():
            pltpu.make_async_copy(self.blocks.at[slot], self.keep.at[rows], self.sems.at[slot]).start()

        @pl.when(jnp.logical_not(kept))
        def _():
            pltpu.make_async_copy(self.blocks.at[slot], self.away.at[rows], self.sems.at[slot]).start()

        self.pending.append(pltpu.make_async_copy(self.blocks.at[slot], self.keep.at[rows], self.sems.at[slot]))

    def finish(self):
        for copy in self.pending[-2:]:
            copy.wait()


def column_sum(value):
    return jnp.sum(value.astype(f32), axis=0, keepdims=True)


def near_grads_kernel(
    own_first, own_second, got_first, got_second, grad_own, grad_mate, act_own, act_mate, pre_own, pre_mate,
    unit_text, grad_text, act_text, pre_text, keep_ref, away_ref, units, grads, bias_ref, blocks, sems, acts, pres, in_sems,
):
    near = slice(0, D)
    loads = []

    def load(source, target):
        loads.append(pltpu.make_async_copy(source, target, in_sems.at[len(loads)]))
        loads[-1].start()

    for piece, source in enumerate((own_first, own_second, got_first, got_second)):
        load(source.at[:VIS], units.at[piece * VIS : (piece + 1) * VIS])
    for own, mate, total in ((pre_own, pre_mate, pres), (act_own, act_mate, acts)):
        load(own.at[:, near], total.at[:CUT])
        load(mate.at[:, near], total.at[CUT:])
    load(grad_own, grads.at[:CUT])
    load(grad_mate, grads.at[CUT:])
    outputs = Outputs(keep_ref, away_ref, blocks, sems)
    outputs.put(1, contract_rows(unit_text[...], pre_text[...]), 0)
    outputs.put(1, contract_rows(act_text[...], grad_text[...]), 1)
    for copy in loads[:6]:
        copy.wait()
    outputs.put(0, contract_rows(units[...], pres[...]), 0)
    for copy in loads[6:]:
        copy.wait()
    outputs.put(0, contract_rows(acts[...], grads[...]), 1)
    at_y = lax.axis_index("ffn")
    bias_ref[...] = jnp.zeros_like(bias_ref)
    bias_ref[pl.ds(at_y, 1)] = column_sum(pres[...])
    bias_ref[pl.ds(4 + at_y, 1)] = column_sum(pre_text[...])
    outputs.finish()


def far_grads_kernel(
    units, grads, act_own, act_mate, pre_own, pre_mate, bias_in, keep_ref, away_ref, bias_ref, blocks, sems, acts, pres, in_sems
):
    far = slice(D, 2 * D)
    loads = []
    for own, mate, total in ((pre_own, pre_mate, pres), (act_own, act_mate, acts)):
        for source, target in ((own, total.at[:CUT]), (mate, total.at[CUT:])):
            loads.append(pltpu.make_async_copy(source.at[:, far], target, in_sems.at[len(loads)]))
            loads[-1].start()
    outputs = Outputs(keep_ref, away_ref, blocks, sems)
    for copy in loads[:2]:
        copy.wait()
    outputs.put(0, contract_rows(units[...], pres[...]), 0)
    for copy in loads[2:]:
        copy.wait()
    outputs.put(0, contract_rows(acts[...], grads[...]), 1)
    bias_ref[...] = bias_in[...]
    bias_ref[pl.ds(lax.rem(lax.axis_index("ffn") + 2, 4), 1)] = column_sum(pres[...])
    outputs.finish()


def near_grads(*args):
    rows = jax.ShapeDtypeStruct((2 * CUT, D), bf16)
    return pl.pallas_call(
        near_grads_kernel,
        out_shape=[jax.ShapeDtypeStruct((2 * D, D), bf16)] * 2 + [rows, rows, jax.ShapeDtypeStruct((8, D), f32)],
        in_specs=[ANY] * 10 + [VMEM] * 4,
        out_specs=[ANY, ANY] + [VMEM] * 3,
        scratch_shapes=[pltpu.VMEM((2, D, D), bf16), pltpu.SemaphoreType.DMA((2,))]
        + [pltpu.VMEM((2 * CUT, D), bf16)] * 2
        + [pltpu.SemaphoreType.DMA((10,))],
        cost_estimate=cost(1),
        compiler_params=params(24),
    )(*args)


def far_grads(*args):
    return pl.pallas_call(
        far_grads_kernel,
        out_shape=[jax.ShapeDtypeStruct((D, D), bf16)] * 2 + [jax.ShapeDtypeStruct((8, D), f32)],
        in_specs=[VMEM] * 2 + [ANY] * 4 + [VMEM],
        out_specs=[ANY, ANY, VMEM],
        scratch_shapes=[pltpu.VMEM((2, D, D), bf16), pltpu.SemaphoreType.DMA((2,))]
        + [pltpu.VMEM((2 * CUT, D), bf16)] * 2
        + [pltpu.SemaphoreType.DMA((4,))],
        cost_estimate=cost(1),
        compiler_params=params(24),
    )(*args)


def text_sum(own_ref, got_first, got_second, b_ref, item, base):
    txt = slice(VIS + item * TXT, VIS + (item + 1) * TXT)
    total = own_ref[CUT + item * TXT : CUT + (item + 1) * TXT] + b_ref[base + item * TXT : base + (item + 1) * TXT].astype(f32)
    return total + got_first[txt].astype(f32) + got_second[txt].astype(f32)


def branch_kernel(
    own_ref, got_first, got_second, b_ref, modal_ref, cot_ref, hid_ref, att_ref, gain_ref, wo_ref,
    hidden_ref, gatt_ref, dwo_ref, sum_ref,
):
    gain = vector(gain_ref)
    sums = [0.0, 0.0, 0.0]
    for item in range(ITEMS):
        at = slice(item * SEQ, (item + 1) * SEQ)
        vis = slice(item * VIS, (item + 1) * VIS)
        vision = own_ref[vis] + (got_first, got_second)[item][:VIS].astype(f32)
        text = text_sum(own_ref, got_first, got_second, b_ref, item, 0)
        grad_unit = unpack_item(vision, text, *slots_of(modal_ref[item : item + 1])).astype(bf16).astype(f32)
        _, hat, scaled = norm_forward(hid_ref[at], 1.0, 0.0)
        grad_norm, grad_gain, grad_shift = norm_backward(grad_unit, hat, scaled, gain)
        grad_hidden = cot_ref[at].astype(f32) + grad_norm
        hidden_ref[at] = grad_hidden
        branch = grad_hidden.astype(bf16)
        gatt_ref[at] = branch
        sums[0] += grad_gain
        sums[1] += grad_shift
        sums[2] += jnp.sum(branch.astype(f32), axis=0, keepdims=True)
    dwo_ref[...] = contract_rows(att_ref[...], gatt_ref[...]).astype(bf16)
    gatt_ref[...] = times_transpose(gatt_ref[...], wo_ref[...]).astype(bf16)
    sum_ref[...] = jnp.concatenate(sums, axis=0)


def scores_kernel(q_ref, k_ref, v_ref, p_ref, gatt_ref, gq_ref, gk_ref, gv_ref):
    low_half = lax.broadcasted_iota(jnp.int32, (1, 128), 1) < HEAD_DIM
    for pair in range(HEADS // 2):
        lanes = slice(pair * 128, (pair + 1) * 128)
        q, k, v, g = q_ref[:, lanes], k_ref[:, lanes], v_ref[:, lanes], gatt_ref[:, lanes]
        gq = gk = gv = 0.0
        for half in range(2):
            mine = low_half if half == 0 else jnp.logical_not(low_half)
            mask = lambda a: jnp.where(mine, a, 0).astype(bf16)
            low = p_ref[0, 2 * pair + half]
            probs = low.astype(f32)
            inner = times_transpose(mask(g), v) * probs
            scores = (inner - probs * jnp.sum(inner, axis=-1, keepdims=True)).astype(bf16)
            gv += contract_rows(low, mask(g))
            gq += matmul(scores, mask(k))
            gk += contract_rows(scores, mask(q))
        gq_ref[:, lanes] = (gq * 0.125).astype(bf16)
        gk_ref[:, lanes] = gk.astype(bf16)
        gv_ref[:, lanes] = gv.astype(bf16)


def backward_scores(q, k, v, p, gatt):
    block = pl.BlockSpec((SEQ, D), lambda i: (i, 0))
    heads = pl.BlockSpec((1, HEADS, SEQ, SEQ), lambda i: (i, 0, 0, 0))
    return pl.pallas_call(
        scores_kernel,
        grid=(ITEMS,),
        out_shape=[jax.ShapeDtypeStruct((ROWS, D), bf16)] * 3,
        in_specs=[block] * 3 + [heads, block],
        out_specs=[block] * 3,
        cost_estimate=cost(25),
        compiler_params=params(20),
    )(q, k, v, p, gatt)


def shared_kernel(
    tok_ref, gain1, shift1, gq_ref, gk_ref, gv_ref, wq_ref, wk_ref, wv_ref, hidden_ref, dwo_ref, sums_two, grad_live, bias_rows,
    tok_out, keep_ref, away_ref,
):
    gain = vector(gain1)
    unit, hat, scaled = norm_forward(tok_ref[...].astype(f32), gain, vector(shift1))
    low = unit.astype(bf16)
    dwq = contract_rows(low, gq_ref[...]).astype(bf16)
    dwk = contract_rows(low, gk_ref[...]).astype(bf16)
    dwv = contract_rows(low, gv_ref[...]).astype(bf16)
    back = times_transpose(gq_ref[...], wq_ref[...]) + times_transpose(gk_ref[...], wk_ref[...]) + times_transpose(gv_ref[...], wv_ref[...])
    grad_norm, grad_gain, grad_shift = norm_backward(back, hat, scaled, gain)
    tok_out[...] = (hidden_ref[...] + grad_norm).astype(bf16)
    total = lambda ref: jnp.sum(ref[...].astype(f32), axis=0, keepdims=True)
    rows = [grad_gain, grad_shift, total(gq_ref), total(gv_ref), sums_two[...], grad_live[...], bias_rows[...]]
    vec = jnp.concatenate(rows + [jnp.zeros((VEC - 17, D), f32)], axis=0).astype(bf16)

    def put(mine, other):
        mine[:D] = dwq
        mine[D : 2 * D] = dwk
        other[:D] = dwv
        other[D : 2 * D] = dwo_ref[...]
        mine[2 * D :] = vec
        other[2 * D :] = vec

    @pl.when(core_index() == 0)
    def _():
        put(keep_ref, away_ref)

    @pl.when(core_index() == 1)
    def _():
        put(away_ref, keep_ref)


def mixed_kernel(own_ref, got_first, got_second, b_ref, modal_ref, hid_ref, b_out, near_small, out_ref):
    first = core_index() == 0
    mine, other = b_out[...].astype(f32), near_small[1:2].astype(f32)
    bias_vision, bias_text = jnp.where(first, mine, other), jnp.where(first, other, mine)
    for item in range(ITEMS):
        at = slice(item * SEQ, (item + 1) * SEQ)
        vis = slice(item * VIS, (item + 1) * VIS)
        vision = own_ref[vis] + (got_first, got_second)[item][:VIS].astype(f32) + bias_vision
        text = text_sum(own_ref, got_first, got_second, b_ref, item, CUT_TXT) + bias_text
        rows = unpack_item(vision, text, *slots_of(modal_ref[item : item + 1])).astype(bf16).astype(f32)
        out_ref[at] = (hid_ref[at] + rows).astype(bf16)


def split_kernel(count, size, axes, *refs):
    ins, outs, total = refs[:count], refs[count:-1], refs[-1]
    extra = total.shape[0] - 4 * size
    total[...] = sum(ref[: 4 * size + extra].astype(f32) for ref in ins).astype(bf16)
    me = place(axes)
    for step, out in zip((0, 1, 3, 2), outs):
        at = pl.multiple_of(lax.rem(me + step, 4) * size, 16)
        out[:size] = total[pl.ds(at, size)]
        if extra:
            out[size:] = total[4 * size :]


def split(pieces, size, extra, axes):
    outs = [((size + extra, D), bf16)] * 4
    scratch = [pltpu.VMEM((4 * size + extra, D), bf16)]
    return call(functools.partial(split_kernel, len(pieces), size, axes), outs, *pieces, scratch=scratch)


def block_steps(size):
    first = core_index() == 0
    return jnp.where(first, 4 * size, size), jnp.where(first, size, 4 * size)


def expert_split_kernel(size, near_keep, near_got, far_keep, far_got, *refs):
    outs, total = refs[:-1], refs[-1]
    near = (near_keep[...].astype(f32) + near_got[...].astype(f32)).astype(bf16)
    total[:D] = near[:D]
    total[D : 2 * D] = (far_keep[...].astype(f32) + far_got[...].astype(f32)).astype(bf16)
    total[2 * D :] = near[D:]
    me = place("xz")
    outer, inner = block_steps(size)
    for step, out in zip((0, 1, 3, 2), outs):
        base = lax.rem(me + step, 4) * outer
        for matrix in range(3):
            for block in range(4):
                at = pl.multiple_of(base + matrix * D + block * inner, 16)
                to = (matrix * 4 + block) * size
                out[to : to + size] = total[pl.ds(at, size)]


EXP = D // 16


def expert_second_kernel(*refs):
    ins, outs, total = refs[:4], refs[4:-1], refs[-1]
    total[...] = sum(ref[...].astype(f32) for ref in ins).astype(bf16)
    me = place("zx")
    for step, out in zip((0, 1, 3, 2), outs):
        index = lax.rem(me + step, 4)
        for matrix in range(3):
            at = pl.multiple_of((matrix * 4 + index) * EXP, 16)
            out[matrix * EXP : (matrix + 1) * EXP] = total[pl.ds(at, EXP)]


def expert_third_kernel(*refs):
    ins, outs = refs[:4], refs[4:]
    total = sum(ref[...].astype(f32) for ref in ins).astype(bf16)
    for matrix, out in enumerate(outs):
        out[...] = total[matrix * EXP : (matrix + 1) * EXP]


def expert_keep_kernel(near, far, text, keep, away):
    first = core_index() == 0
    vision, language = near[...].astype(f32) + far[...].astype(f32), text[...].astype(f32)
    keep[...] = jnp.where(first, vision, language).astype(bf16)
    away[...] = jnp.where(first, language, vision).astype(bf16)


def sum_kernel(*refs):
    ins, out = refs[:4], refs[4]
    out[...] = sum(ref[...].astype(f32) for ref in ins).astype(bf16)


def fourth_kernel(*refs):
    ins, (keep, got, out, vec) = refs[:4], refs[4:]
    total = sum(ref[...].astype(f32) for ref in ins)
    out[: 2 * EXP] = total[: 2 * EXP].astype(bf16)
    vec[...] = total[2 * EXP :]
    first = core_index() == 0
    k, g = keep[...].astype(f32), got[...].astype(f32)
    out[2 * EXP : 3 * EXP] = jnp.where(first, k, g).astype(bf16)
    out[3 * EXP :] = jnp.where(first, g, k).astype(bf16)


def fifth_kernel(mine, first, third, second, shared, expert):
    me = place("xz")
    for step, piece in zip((0, 1, 3, 2), (mine, first, third, second)):
        index = lax.rem(me + 4 - step, 4)
        shared[pl.ds(pl.multiple_of(index * 2 * EXP, 16), 2 * EXP)] = piece[: 2 * EXP]
        at = pl.multiple_of(index * EXP, 16)
        expert[pl.ds(at, EXP)] = piece[2 * EXP : 3 * EXP]
        expert[pl.ds(4 * EXP + at, EXP)] = piece[3 * EXP :]


def expert_finish_kernel(mine, first, third, second, w_in, w_out):
    outer, inner = block_steps(EXP)
    me = place("zx")
    for step, piece in zip((0, 1, 3, 2), (mine, first, third, second)):
        base = lax.rem(me + 4 - step, 4) * inner
        for block in range(4):
            at = pl.ds(pl.multiple_of(base + block * outer, 16), EXP)
            w_in[at] = piece[block * EXP : (block + 1) * EXP].astype(f32)
            w_out[at] = piece[(4 + block) * EXP : (5 + block) * EXP].astype(f32)


def join_kernel(axes, *refs):
    ins, out = refs[:4], refs[4]
    size = out.shape[0] // 4
    me = place(axes)
    for step, piece in zip((0, 1, 3, 2), ins):
        at = pl.multiple_of(lax.rem(me + 4 - step, 4) * size, 16)
        out[pl.ds(at, size)] = piece[:size]


def join(piece, got, axes, size=None):
    return call(functools.partial(join_kernel, axes), [((4 * (size or piece.shape[0]), D), bf16)], piece, *got)[0]


def finish_kernel(mine, other, vec, wq, wk, wv, wo, g1, s1, bq, bv, g2, s2, bo, b_in, b_out):
    first = core_index() == 0
    for low, high, at in ((wq, wv, 0), (wk, wo, 1)):
        m, o = mine[at].astype(f32), other[at].astype(f32)
        low[...] = jnp.where(first, m, o)
        high[...] = jnp.where(first, o, m)

    @pl.when(pl.program_id(0) == 0)
    def _():
        for ref, row in ((g1, 0), (s1, 1), (bq, 2), (bv, 3), (g2, 4), (s2, 5), (bo, 6)):
            ref[...] = vec[row]
        b_in[...] = vec[pl.ds(9 + 4 * core_index() + lax.axis_index("ffn"), 1)]
        b_out[...] = vec[pl.ds(7 + core_index(), 1)]


def finish(mine, other, vec):
    steps = 4
    size = D // steps
    pair = pl.BlockSpec((2, size, D), lambda i: (0, i, 0))
    block = pl.BlockSpec((size, D), lambda i: (i, 0))
    return pl.pallas_call(
        finish_kernel,
        grid=(steps,),
        out_shape=[jax.ShapeDtypeStruct((D, D), f32)] * 4
        + [jax.ShapeDtypeStruct((D,), f32)] * 7
        + [jax.ShapeDtypeStruct((1, D), f32)] * 2,
        in_specs=[pair, pair, VMEM],
        out_specs=[block] * 4 + [VMEM] * 9,
        cost_estimate=cost(5),
        compiler_params=params(12),
    )(mine.reshape(2, D, D), other.reshape(2, D, D), vec)


def body(
    tokens,
    cotangent,
    modality,
    ln1_gain,
    ln1_shift,
    w_query,
    b_query,
    w_key,
    w_value,
    b_value,
    w_attn_out,
    b_attn_out,
    ln2_gain,
    ln2_shift,
    w_in,
    b_in,
    w_out,
    b_out,
):
    flat_tokens = tokens.reshape(ROWS, D)
    flat_cot = cotangent.reshape(ROWS, D)
    w_in, w_out = w_in[0], w_out[0]

    part_in, part_out, cot_first, cot_second, small = parts(w_in, w_out, flat_cot, b_in, b_out, modality)
    part_in = send(part_in, lambda x, z, c, y: (x, z, 0, (y + 2) % 4) if c == 0 else None)
    part_out = send(part_out, lambda x, z, c, y: (x, z, 1, (y + 2) % 4) if c == 0 else None)

    cot_first, cot_second = swap_pair(cot_first), swap_other(cot_second)

    vectors = (ln1_gain, ln1_shift, b_query, b_value, b_attn_out, ln2_gain, ln2_shift)
    query, key, value, probs, attended, hidden_one, own_first, own_second, text_own = forward_attention(
        flat_tokens, modality, vectors, (w_query, w_key, w_value, w_attn_out), flat_cot
    )
    sent_first, sent_second, text_own = tie((own_first, own_second, text_own), cot_first, cot_second)
    got_first, got_second, got_b = swap_pair(sent_first), swap_other(sent_second), swap_far(text_own)
    near_in, near_out = swap_core(tie(w_in, own_first)), swap_core(tie(w_out, own_first))
    far_part = jnp.where(core_index() == 0, *tie((part_in, part_out), own_first))
    far_got = shifts([far_part] * 3, "xz")
    near_small = swap_core(tie(small, far_got[2]))
    far_mine = join(far_part, tie(far_got, got_first, got_second, got_b, near_small), "xz", D // 4)
    far_other = swap_core(far_mine)

    grad_own, grad_live = call(pack_kernel, [((CUT, D), bf16), ((2, D), f32)], tie(flat_cot, own_first), modality, micros=2)
    text_weights = (w_in, w_out, near_in, near_out)
    vision_weights = text_weights + (far_mine, far_other)
    text_home, text_mates, text_b, grad_mate, units_text, grads_text, text_act, text_pre = text_rows(
        text_own, got_first, got_second, got_b, cot_first, cot_second, b_in, near_small, *text_weights
    )
    got_text = swap_far(text_b)
    smalls = (b_in, far_part, near_small)
    back_first, back_second, out_first, out_second, mate_act, mate_pre = vision_rows(
        True, (got_first, got_second), grad_mate, text_mates, smalls, vision_weights
    )
    back_first, back_second = swap_pair(back_first), swap_other(back_second)
    own_back, own_out, own_act, own_pre = vision_rows(
        False, (own_first, own_second), tie(grad_own, grad_mate, mate_act), text_home, smalls, vision_weights
    )

    near_keep, near_away, units, grads, bias_rows = near_grads(
        own_first, own_second, got_first, got_second, grad_own, grad_mate, own_act, mate_act, own_pre, mate_pre,
        units_text, grads_text, text_act, text_pre,
    )
    far_keep, far_away, bias_rows = far_grads(units, grads, own_act, mate_act, own_pre, mate_pre, bias_rows)
    near_away_got = swap_core(tie(near_away, back_first, back_second, got_text))

    grad_hidden, grad_attended, grad_w_attn_out, sums_two = call(
        branch_kernel,
        [((ROWS, D), f32), ((ROWS, D), bf16), ((D, D), bf16), ((3, D), f32)],
        own_back, tie(back_first, far_keep), back_second, got_text, modality, flat_cot, hidden_one, attended, ln2_gain, w_attn_out,
        micros=100, mebibytes=20,
    )
    far_away_got = swap_core(tie(far_away, back_first, back_second, got_text))
    out_first, out_second = tie((out_first, out_second), back_first, back_second)
    out_first, out_second = swap_pair(out_first), swap_other(out_second)
    expert_pieces = call(
        functools.partial(expert_split_kernel, EXP),
        [((12 * EXP, D), bf16)] * 4,
        near_keep, near_away_got, far_keep, tie(far_away_got, grad_attended),
        scratch=[pltpu.VMEM((3 * D, D), bf16)], micros=2, mebibytes=20,
    )
    expert_got = shifts(expert_pieces[1:], "xz")
    grad_query, grad_key, grad_value = backward_scores(query, key, value, probs, tie(grad_attended, *expert_pieces))
    grad_tokens, shared_keep, shared_away = call(
        shared_kernel,
        [((ROWS, D), bf16)] + [((2 * D + VEC, D), bf16)] * 2,
        flat_tokens, ln1_gain, ln1_shift, grad_query, grad_key, grad_value, w_query, w_key, w_value,
        grad_hidden, grad_w_attn_out, sums_two, grad_live, bias_rows,
        micros=11, mebibytes=28,
    )

    shared_got = swap_core(tie(shared_away, *expert_got[:2], out_first, out_second))
    shared_pieces = split([shared_keep, shared_got], 2 * D // 4, VEC, "yx")
    shared_got = shifts(shared_pieces[1:], "yx")
    expert_pieces = call(
        expert_second_kernel,
        [((3 * EXP, D), bf16)] * 4,
        expert_pieces[0], *tie(expert_got, *shared_pieces),
        scratch=[pltpu.VMEM((12 * EXP, D), bf16)],
    )
    expert_got = shifts(expert_pieces[1:], "zx")
    shared_pieces = split([shared_pieces[0]] + tie(shared_got, *expert_got[:2]), 2 * EXP, VEC, "xz")
    shared_got = shifts(shared_pieces[1:], "xz")
    near, far, text = call(expert_third_kernel, [((EXP, D), bf16)] * 3, expert_pieces[0], *expert_got)
    far = swap_far(far)
    size = 2 * EXP + VEC
    (shared_total,) = call(sum_kernel, [((size, D), bf16)], shared_pieces[0], *tie(shared_got, far))
    shared_got = shifts([shared_total] * 3, "zy")
    expert_keep, expert_away = call(expert_keep_kernel, [((EXP, D), bf16)] * 2, near, far, text)
    low, vec = call(
        fourth_kernel,
        [((4 * EXP, D), bf16), ((VEC, D), f32)],
        shared_total, *shared_got, expert_keep, swap_core(expert_away),
    )
    shared_sum, expert_sum = call(
        fifth_kernel, [((8 * EXP, D), bf16)] * 2, low, *shifts([low] * 3, "xz")
    )
    shared_got = shifts([shared_sum] * 3, "yx")
    expert_got = shifts([expert_sum] * 3, "zx")
    shared_sum = join(shared_sum, shared_got, "yx")
    shared_sum = tie(shared_sum, expert_got[0], expert_got[1])
    outs = finish(shared_sum, swap_core(shared_sum), vec)
    d_query, d_key, d_value, d_out, d_gain1, d_shift1, d_bq, d_bv, d_gain2, d_shift2, d_bo, d_b_in, d_b_out = outs
    grad_w_in, grad_w_out = call(expert_finish_kernel, [((D, D), f32)] * 2, tie(expert_sum, d_query), *expert_got)
    (mixed,) = call(
        mixed_kernel,
        [((ROWS, D), bf16)],
        own_out, out_first, out_second, got_text, modality, hidden_one, b_out, near_small,
        micros=4, mebibytes=16,
    )
    return (
        mixed.reshape(tokens.shape),
        grad_tokens.reshape(tokens.shape),
        d_gain1,
        d_shift1,
        d_query,
        d_bq,
        d_key,
        d_value,
        d_bv,
        d_out,
        d_bo,
        d_gain2,
        d_shift2,
        grad_w_in[None],
        d_b_in,
        grad_w_out[None],
        d_b_out,
    )


def solution(mesh):
    items = P(AXES, None, None)
    expert_specs = (P("expert", None, "ffn"), P("expert", "ffn"), P("expert", "ffn", None), P("expert", None))
    return jax.shard_map(
        body,
        mesh=mesh,
        in_specs=(items, items, P(AXES, None)) + (P(),) * 11 + expert_specs,
        out_specs=(items, items) + (P(),) * 11 + expert_specs,
        check_vma=False,
    )
```

```python
import functools

import jax
import jax.numpy as jnp
from jax import lax
from jax.experimental import pallas as pl
from jax.experimental.pallas import tpu as pltpu
from jax.sharding import PartitionSpec as P

D = 768
HEAD_DIM = 64
HEADS = D // HEAD_DIM
PATCHES = 197
SEQ = 256
ITEMS = 2
ROWS = ITEMS * SEQ
TEXT_AT = 192
VIS = 208
TXT = 48
CUT = ITEMS * VIS
CUT_TXT = ITEMS * TXT
BACK = VIS + CUT_TXT
COT = SEQ + TXT + 16
VEC = 24

epsilon = 1e-05
root_half = 0.7071067811865476
inv_root_tau = 0.3989422804014327
AXES = ("dp", "expert", "ffn")
bf16 = jnp.bfloat16
f32 = jnp.float32


def split_index(index):
    return index // 32, index // 8 % 4, index // 4 % 2, index % 4


def join_index(x, z, core, y):
    return ((x * 4 + z) * 2 + core) * 4 + y


def send(value, where):
    pairs = []
    for index in range(128):
        target = where(*split_index(index))
        if target is not None:
            pairs.append((index, join_index(*target)))
    return lax.ppermute(value, AXES, pairs)


def swap_core(value):
    return send(value, lambda x, z, c, y: (x, z, 1 - c, y))


def swap_pair(value):
    return send(value, lambda x, z, c, y: (x, z, c, y ^ 1))


def swap_other(value):
    return send(value, lambda x, z, c, y: (x, z, c, 3 - y))


def swap_far(value):
    return send(value, lambda x, z, c, y: (x, z, c, y ^ 2))


def shift(value, axes, step):
    def where(x, z, c, y):
        at = dict(x=x, z=z, y=y)
        at[axes[c]] = (at[axes[c]] + step) % 4
        return at["x"], at["z"], c, at["y"]

    return send(value, where)


def shifts(pieces, axes):
    return [shift(piece, axes, step) for piece, step in zip(pieces, (1, 3, 2))]


def tie(value, *others):
    return lax.optimization_barrier((value, others))[0]


def core_index():
    return lax.axis_index("expert")


def place(axes):
    dp = lax.axis_index("dp")
    at = dict(x=dp // 4, z=dp % 4, y=lax.axis_index("ffn"))
    return jnp.where(core_index() == 0, at[axes[0]], at[axes[1]])


def norm_forward(values, gain_vec, shift_vec):
    centre = values - jnp.mean(values, axis=-1, keepdims=True)
    scaled = lax.rsqrt(jnp.mean(centre * centre, axis=-1, keepdims=True) + epsilon)
    normal_hat = centre * scaled
    return (normal_hat * gain_vec + shift_vec, normal_hat, scaled)


def norm_backward(grad_result, normal_hat, scaled, gain_vec):
    grad_hat = grad_result * gain_vec
    inner_term = (
        grad_hat
        - jnp.mean(grad_hat, axis=-1, keepdims=True)
        - normal_hat * jnp.mean(grad_hat * normal_hat, axis=-1, keepdims=True)
    )
    return (
        scaled * inner_term,
        jnp.sum(grad_result * normal_hat, axis=0, keepdims=True),
        jnp.sum(grad_result, axis=0, keepdims=True),
    )


def matmul(first_op, second_op):
    return jnp.dot(first_op, second_op, preferred_element_type=f32)


def contract_rows(first_op, second_op):
    return lax.dot_general(first_op, second_op, (((0,), (0,)), ((), ())), preferred_element_type=f32)


def times_transpose(first_op, second_op):
    return lax.dot_general(first_op, second_op, (((1,), (1,)), ((), ())), preferred_element_type=f32)


def vector(ref):
    return ref[...].astype(f32).reshape(1, D)


def slots_of(row):
    has_image = jnp.max(jnp.where(row == 0, 1.0, 0.0), axis=1, keepdims=True)
    texts = jnp.sum(jnp.where(row == 1, 1.0, 0.0), axis=1, keepdims=True)
    start = has_image * PATCHES
    slot = lax.broadcasted_iota(jnp.int32, (SEQ, 1), 0).astype(f32)
    modal = jnp.where(slot < start, 0.0, jnp.where(slot < start + texts, 1.0, 2.0))
    return has_image > 0.5, modal


def text_of(rows, has_image, modal):
    at = slice(TEXT_AT, TEXT_AT + TXT)
    return jnp.where(has_image, jnp.where(modal[at] == 1, rows[at], 0.0), jnp.where(modal[:TXT] == 1, rows[:TXT], 0.0))


def unpack_item(vision, text, has_image, modal):
    whole = jnp.concatenate(
        [
            jnp.where(has_image, vision[:TXT], text),
            vision[TXT:TEXT_AT],
            jnp.where(modal[TEXT_AT:VIS] == 1, text[: VIS - TEXT_AT], vision[TEXT_AT:]),
            text[VIS - TEXT_AT :],
            jnp.zeros((SEQ - TEXT_AT - TXT, D), f32),
        ],
        axis=0,
    )
    return jnp.where(modal < 2, whole, 0.0)


VMEM = pl.BlockSpec(memory_space=pltpu.VMEM)
ANY = pl.BlockSpec(memory_space=pl.ANY)


def cost(micros):
    return pl.CostEstimate(flops=0, bytes_accessed=int(micros * 1e5), transcendentals=0)


def params(mebibytes):
    return pltpu.CompilerParams(vmem_limit_bytes=mebibytes * 1024 * 1024)


def call(kernel, outs, *args, scratch=(), any_from=None, micros=1.5, mebibytes=12):
    specs = [VMEM] * len(args) if any_from is None else [VMEM] * any_from + [ANY] * (len(args) - any_from)
    return pl.pallas_call(
        kernel,
        out_shape=[jax.ShapeDtypeStruct(shape, dtype) for shape, dtype in outs],
        in_specs=specs,
        out_specs=[VMEM] * len(outs),
        scratch_shapes=list(scratch),
        cost_estimate=cost(micros),
        compiler_params=params(mebibytes),
    )(*args)


def pack_kernel(grad_ref, modal_ref, out_ref, sum_ref):
    sums = [0.0, 0.0]
    for item in range(ITEMS):
        has_image, modal = slots_of(modal_ref[item : item + 1])
        grad = grad_ref[item * SEQ : (item + 1) * SEQ].astype(f32)
        vision = jnp.where(modal[:VIS] == 0, grad[:VIS], 0.0)
        out_ref[item * VIS : (item + 1) * VIS] = vision.astype(bf16)
        sums[0] += jnp.sum(vision, axis=0, keepdims=True)
        sums[1] += jnp.sum(text_of(grad, has_image, modal), axis=0, keepdims=True)
    sum_ref[...] = jnp.concatenate(sums, axis=0)


def part_kernel(w_in, w_out, grad, b_in, b_out, modal_ref, in_ref, out_ref, first_ref, second_ref, small_ref, text_ref, sems):
    dp, share = lax.axis_index("dp"), D // 4
    x, z = lax.div(dp, 4), lax.rem(dp, 4)
    copies = [
        pltpu.make_async_copy(w_in.at[pl.ds(pl.multiple_of(x * share, 16), share)], in_ref.at[:share], sems.at[0]),
        pltpu.make_async_copy(w_out.at[pl.ds(pl.multiple_of(z * share, 16), share)], out_ref.at[:share], sems.at[1]),
        pltpu.make_async_copy(grad.at[:SEQ], first_ref.at[:SEQ], sems.at[2]),
        pltpu.make_async_copy(grad.at[SEQ:], second_ref.at[:SEQ], sems.at[3]),
    ]
    for copy in copies:
        copy.start()
    small = [b_in[...].astype(f32), b_out[...].astype(f32), jnp.zeros((14, D), f32)]
    small = jnp.concatenate(small, axis=0).astype(bf16)
    small_ref[...] = small
    modal = jnp.concatenate([modal_ref[...].astype(f32), jnp.zeros((16 - ITEMS, SEQ), f32)], axis=0)
    modal = jnp.concatenate([modal, jnp.zeros((16, D - SEQ), f32)], axis=1).astype(bf16)
    first_ref[SEQ + TXT :] = modal
    second_ref[SEQ + TXT :] = modal
    in_ref[share:] = small
    out_ref[share:] = small
    for copy in copies:
        copy.wait()
    for item, source, target in ((0, first_ref, second_ref), (1, second_ref, first_ref)):
        text = text_of(source[:SEQ].astype(f32), *slots_of(modal_ref[item : item + 1]))
        target[SEQ : SEQ + TXT] = text.astype(bf16)
        text_ref[item * TXT : (item + 1) * TXT] = text.astype(bf16)


def parts(*args):
    return pl.pallas_call(
        part_kernel,
        out_shape=[jax.ShapeDtypeStruct((D // 4 + 16, D), bf16)] * 2 + [jax.ShapeDtypeStruct((COT, D), bf16)] * 2
        + [jax.ShapeDtypeStruct((16, D), bf16), jax.ShapeDtypeStruct((CUT_TXT, D), bf16)],
        in_specs=[ANY] * 3 + [VMEM] * 3,
        out_specs=[VMEM] * 6,
        scratch_shapes=[pltpu.SemaphoreType.DMA((4,))],
        cost_estimate=cost(1),
        compiler_params=params(60),
    )(*args)


def forward_kernel(
    tok_ref, modal_ref, gain1, shift1, b_query, b_value, b_out, gain2, shift2, wq_ref, wk_ref, wv_ref, wo_ref,
    grad_text, q_out, k_out, v_out, p_out, att_out, hid_out, first_out, second_out, text_out,
    held, sems, q_all, k_all, v_all, p_all, att_all, hid_all, out_sems, first_ref, second_ref, text_ref, sent_sems,
):
    item = pl.program_id(0)
    pieces = 4
    rows = D // pieces

    def weight_copy(i, piece):
        at = pl.ds(piece * rows, rows)
        return pltpu.make_async_copy((wq_ref, wk_ref, wv_ref, wo_ref)[i].at[at], held.at[i, at], sems.at[i, piece])

    def start_weight(i):
        @pl.when(item == 0)
        def _():
            for piece in range(pieces):
                weight_copy(i, piece).start()

    def wait_weight(i):
        @pl.when(item == 0)
        def _():
            for piece in range(pieces):
                weight_copy(i, piece).wait()

    start_weight(0)

    @pl.when(item == 0)
    def _():
        text_ref[CUT_TXT:] = grad_text[...]

    outs = [(q_all, q_out), (k_all, k_out), (v_all, v_out), (p_all, p_out), (att_all, att_out), (hid_all, hid_out)]

    def copy_out(i, at):
        return pltpu.make_async_copy(outs[i][0].at[at], outs[i][1].at[at], out_sems.at[at, i])

    sent = [
        (first_ref.at[:VIS], first_out.at[:VIS]),
        (second_ref.at[:VIS], second_out.at[:VIS]),
        (first_ref.at[VIS:], first_out.at[VIS:]),
        (second_ref.at[VIS:], second_out.at[VIS:]),
        (text_ref, text_out),
    ]
    sent = [pltpu.make_async_copy(source, target, sent_sems.at[i]) for i, (source, target) in enumerate(sent)]

    q_ref, k_ref, v_ref, p_ref, att_ref = (ref.at[item] for ref in (q_all, k_all, v_all, p_all, att_all))
    x = tok_ref[...].astype(f32)
    unit, _, _ = norm_forward(x, vector(gain1), vector(shift1))
    unit = unit.astype(bf16)
    start_weight(1)
    wait_weight(0)
    q_ref[...] = ((matmul(unit, held[0]) + vector(b_query)).astype(bf16) * 0.125).astype(bf16)
    copy_out(0, item).start()
    start_weight(2)
    wait_weight(1)
    k_ref[...] = matmul(unit, held[1]).astype(bf16)
    copy_out(1, item).start()
    start_weight(3)
    wait_weight(2)
    v_ref[...] = (matmul(unit, held[2]) + vector(b_value)).astype(bf16)
    copy_out(2, item).start()
    row = modal_ref[pl.ds(item, 1)]
    bias = jnp.where(row < 2, 0.0, -1e30)
    low_half = lax.broadcasted_iota(jnp.int32, (1, 128), 1) < HEAD_DIM
    ones = jnp.ones((SEQ, 128), bf16)
    for pair in range(HEADS // 2):
        lanes = slice(pair * 128, (pair + 1) * 128)
        q, k, v = q_ref[:, lanes], k_ref[:, lanes], v_ref[:, lanes]
        halves = []
        for half in range(2):
            mine = low_half if half == 0 else jnp.logical_not(low_half)
            scores = times_transpose(jnp.where(mine, q, 0).astype(bf16), k) + bias
            scores = jnp.exp(scores - jnp.max(scores, axis=-1, keepdims=True))
            both = matmul(scores.astype(bf16), jnp.concatenate([v, ones], axis=1))
            inverse = 1.0 / both[:, 128:]
            p_ref[2 * pair + half] = (scores * jnp.concatenate([inverse, inverse], axis=1)).astype(bf16)
            halves.append(both[:, :128] * inverse)
        att_ref[:, lanes] = jnp.where(low_half, halves[0], halves[1]).astype(bf16)
    copy_out(3, item).start()
    copy_out(4, item).start()
    wait_weight(3)
    hidden = x + matmul(att_ref[...], held[3]) + vector(b_out)
    hid_all[item] = hidden
    copy_out(5, item).start()
    unit, _, _ = norm_forward(hidden, vector(gain2), vector(shift2))
    has_image, _ = slots_of(row)
    vision = unit[:VIS].astype(bf16)
    text = jnp.where(has_image, unit[TEXT_AT : TEXT_AT + TXT], unit[:TXT]).astype(bf16)
    text_ref[pl.ds(pl.multiple_of(item * TXT, 16), TXT)] = text
    first_ref[pl.ds(pl.multiple_of(VIS + item * TXT, 16), TXT)] = text
    second_ref[pl.ds(pl.multiple_of(VIS + item * TXT, 16), TXT)] = text

    @pl.when(item == 0)
    def _():
        first_ref[:VIS] = vision
        sent[0].start()

    @pl.when(item == 1)
    def _():
        second_ref[:VIS] = vision
        for copy in sent[1:]:
            copy.start()
        for at in range(ITEMS):
            for i in range(len(outs)):
                copy_out(i, at).wait()
        for copy in sent:
            copy.wait()


def forward_attention(tokens, modality, vectors, weights, *rest):
    block = pl.BlockSpec((SEQ, D), lambda i: (i, 0))
    shapes = [((ITEMS, SEQ, D), bf16)] * 3 + [((ITEMS, HEADS, SEQ, SEQ), bf16), ((ITEMS, SEQ, D), bf16), ((ITEMS, SEQ, D), f32)]
    sent = [((BACK, D), bf16), ((BACK, D), bf16), ((2 * CUT_TXT, D), bf16)]
    outs = pl.pallas_call(
        forward_kernel,
        grid=(ITEMS,),
        out_shape=[jax.ShapeDtypeStruct(*s) for s in shapes + sent],
        in_specs=[block] + [VMEM] * 8 + [ANY] * 4 + [VMEM],
        out_specs=[ANY] * 9,
        scratch_shapes=[pltpu.VMEM((4, D, D), bf16), pltpu.SemaphoreType.DMA((4, 4))]
        + [pltpu.VMEM(*s) for s in shapes]
        + [pltpu.SemaphoreType.DMA((ITEMS, 6))]
        + [pltpu.VMEM(*s) for s in sent]
        + [pltpu.SemaphoreType.DMA((5,))],
        cost_estimate=cost(10),
        compiler_params=params(56),
    )(tokens, modality, *vectors, *weights, *rest)
    flat = [out.reshape(ROWS, D) for out in outs[:3]]
    return flat + [outs[3], outs[4].reshape(ROWS, D), outs[5].reshape(ROWS, D)] + list(outs[6:])


def fetch(first, second, buffer, sem):
    @pl.when(core_index() == 0)
    def _():
        pltpu.make_async_copy(first, buffer, sem).start()

    @pl.when(core_index() == 1)
    def _():
        pltpu.make_async_copy(second, buffer, sem).start()


def row_pass(unit, grad, first, bias, second, act_ref, pre_ref, base):
    for at in range(0, D, 256):
        cols = slice(at, at + 256)
        kept = slice(base + at, base + at + 256)
        pre_act = matmul(unit, first[:, cols]) + bias[:, cols]
        cdf = 0.5 + 0.5 * lax.erf(pre_act * root_half)
        act_ref[:, kept] = (pre_act * cdf).astype(bf16)
        slope = cdf + pre_act * (jnp.exp(-0.5 * pre_act * pre_act) * inv_root_tau)
        pre_ref[:, kept] = (times_transpose(grad, second[cols, :]) * slope).astype(bf16)


def vision_kernel(
    mates, first_unit, second_unit, grad_ref, text_ref, b_in, far_part, near_small,
    w_in, w_out, near_in, near_out, far_mine, far_other, *refs,
):
    outs, (act_ref, pre_ref, held, sems, units) = refs[:-5], refs[-5:]
    fetch(w_in, near_in, held.at[0], sems.at[0])
    fetch(w_out, near_out, held.at[1], sems.at[1])
    fetch(far_mine, far_other, held.at[2], sems.at[2])
    fetch(far_other, far_mine, held.at[3], sems.at[3])
    first = core_index() == 0
    biases = (
        jnp.where(first, b_in[...].astype(f32), near_small[0:1].astype(f32)),
        far_part[D // 4 : D // 4 + 1].astype(f32),
    )
    units[:VIS] = first_unit[:VIS]
    units[VIS:] = second_unit[:VIS]
    unit, grad = units[...], grad_ref[...]
    for part in range(2):
        for slot in (2 * part, 2 * part + 1):
            pltpu.make_async_copy(w_in, held.at[slot], sems.at[slot]).wait()
        row_pass(unit, grad, held.at[2 * part], biases[part], held.at[2 * part + 1], act_ref, pre_ref, part * D)
    back = times_transpose(pre_ref[:, :D], held[0]) + times_transpose(pre_ref[:, D:], held[2])
    out = matmul(act_ref[:, :D], held[1]) + matmul(act_ref[:, D:], held[3])
    if mates:
        for item in range(2):
            at = slice(item * VIS, (item + 1) * VIS)
            outs[item][:VIS] = back[at].astype(bf16)
            outs[item][VIS:] = text_ref[2 * item * CUT_TXT : (2 * item + 1) * CUT_TXT]
            outs[2 + item][:VIS] = out[at].astype(bf16)
            outs[2 + item][VIS:] = text_ref[(2 * item + 1) * CUT_TXT : (2 * item + 2) * CUT_TXT]
    else:
        outs[0][:CUT] = back
        outs[0][CUT:] = text_ref[:CUT_TXT]
        outs[1][:CUT] = out
        outs[1][CUT:] = text_ref[CUT_TXT:]


def vision_rows(mates, units, grad, text, smalls, weights):
    outs = [((BACK, D), bf16)] * 4 if mates else [((ROWS, D), f32)] * 2
    outs += [((CUT, 2 * D), bf16)] * 2
    scratch = [pltpu.VMEM((4, D, D), bf16), pltpu.SemaphoreType.DMA((4,)), pltpu.VMEM((CUT, D), bf16)]
    kernel = functools.partial(vision_kernel, mates)
    return call(kernel, outs, *units, grad, text, *smalls, *weights, scratch=scratch, any_from=7, micros=3, mebibytes=28)


def pack_mates_kernel(cot_first, cot_second, grad_ref, text_ref):
    for item, cot in ((0, cot_first), (1, cot_second)):
        modality = cot[SEQ + TXT :, :SEQ].astype(f32)
        has_image, modal = slots_of(modality[item : item + 1])
        grad = cot[:SEQ].astype(f32)
        grad_ref[item * VIS : (item + 1) * VIS] = jnp.where(modal[:VIS] == 0, grad[:VIS], 0.0).astype(bf16)
        at = item * CUT_TXT
        here, there = at + item * TXT, at + (1 - item) * TXT
        text_ref[here : here + TXT] = text_of(grad, has_image, modal).astype(bf16)
        text_ref[there : there + TXT] = cot[SEQ : SEQ + TXT]


def text_kernel(
    own_text, got_first, got_second, got_b, mates_grad, b_in, near_small, w_in, w_out, near_in, near_out,
    home_ref, mates_ref, b_back, b_out, unit_ref, grad_ref, act_ref, pre_ref, held, sems,
):
    fetch(near_in, w_in, held.at[0], sems.at[0])
    fetch(near_out, w_out, held.at[1], sems.at[1])
    unit_ref[:CUT_TXT] = own_text[:CUT_TXT]
    unit_ref[CUT_TXT : 2 * CUT_TXT] = got_first[VIS:]
    unit_ref[2 * CUT_TXT : 3 * CUT_TXT] = got_second[VIS:]
    unit_ref[3 * CUT_TXT :] = got_b[:CUT_TXT]
    grad_ref[:CUT_TXT] = own_text[CUT_TXT:]
    grad_ref[CUT_TXT : 3 * CUT_TXT] = mates_grad[...]
    grad_ref[3 * CUT_TXT :] = got_b[CUT_TXT:]
    bias = jnp.where(core_index() == 0, near_small[0:1].astype(f32), b_in[...].astype(f32))
    for slot in range(2):
        pltpu.make_async_copy(w_in, held.at[slot], sems.at[slot]).wait()
    row_pass(unit_ref[...], grad_ref[...], held.at[0], bias, held.at[1], act_ref, pre_ref, 0)
    back = times_transpose(pre_ref[...], held[0])
    out = matmul(act_ref[...], held[1])
    for piece, (target, base) in enumerate(((home_ref, 0), (mates_ref, 0), (mates_ref, 2 * CUT_TXT))):
        at = slice(piece * CUT_TXT, (piece + 1) * CUT_TXT)
        target[base : base + CUT_TXT] = back[at].astype(target.dtype)
        target[base + CUT_TXT : base + 2 * CUT_TXT] = out[at].astype(target.dtype)
    b_back[...] = back[3 * CUT_TXT :].astype(bf16)
    b_out[...] = out[3 * CUT_TXT :].astype(bf16)


def text_rows(*args):
    outs = [((2 * CUT_TXT, D), f32), ((4 * CUT_TXT, D), bf16)] + [((CUT_TXT, D), bf16)] * 2
    outs += [((4 * CUT_TXT, D), bf16)] * 4
    scratch = [pltpu.VMEM((2, D, D), bf16), pltpu.SemaphoreType.DMA((2,))]
    return call(text_kernel, outs, *args, scratch=scratch, any_from=7, micros=5, mebibytes=20)


class Outputs:
    def __init__(self, keep, away, blocks, sems):
        self.keep, self.away, self.blocks, self.sems, self.pending = keep, away, blocks, sems, []

    def put(self, index, value, kind):
        slot = len(self.pending) % 2
        if len(self.pending) >= 2:
            self.pending[-2].wait()
        self.blocks[slot] = value.astype(bf16)
        rows = pl.ds(index * D, D)
        kept = core_index() == kind

        @pl.when(kept)
        def _():
            pltpu.make_async_copy(self.blocks.at[slot], self.keep.at[rows], self.sems.at[slot]).start()

        @pl.when(jnp.logical_not(kept))
        def _():
            pltpu.make_async_copy(self.blocks.at[slot], self.away.at[rows], self.sems.at[slot]).start()

        self.pending.append(pltpu.make_async_copy(self.blocks.at[slot], self.keep.at[rows], self.sems.at[slot]))

    def finish(self):
        for copy in self.pending[-2:]:
            copy.wait()


def column_sum(value):
    return jnp.sum(value.astype(f32), axis=0, keepdims=True)


def near_grads_kernel(
    own_first, own_second, got_first, got_second, grad_own, grad_mate, act_own, act_mate, pre_own, pre_mate,
    unit_text, grad_text, act_text, pre_text, keep_ref, away_ref, units, grads, bias_ref, blocks, sems, acts, pres, in_sems,
):
    near = slice(0, D)
    loads = []

    def load(source, target):
        loads.append(pltpu.make_async_copy(source, target, in_sems.at[len(loads)]))
        loads[-1].start()

    for piece, source in enumerate((own_first, own_second, got_first, got_second)):
        load(source.at[:VIS], units.at[piece * VIS : (piece + 1) * VIS])
    for own, mate, total in ((pre_own, pre_mate, pres), (act_own, act_mate, acts)):
        load(own.at[:, near], total.at[:CUT])
        load(mate.at[:, near], total.at[CUT:])
    load(grad_own, grads.at[:CUT])
    load(grad_mate, grads.at[CUT:])
    outputs = Outputs(keep_ref, away_ref, blocks, sems)
    outputs.put(1, contract_rows(unit_text[...], pre_text[...]), 0)
    outputs.put(1, contract_rows(act_text[...], grad_text[...]), 1)
    for copy in loads[:6]:
        copy.wait()
    outputs.put(0, contract_rows(units[...], pres[...]), 0)
    for copy in loads[6:]:
        copy.wait()
    outputs.put(0, contract_rows(acts[...], grads[...]), 1)
    at_y = lax.axis_index("ffn")
    bias_ref[...] = jnp.zeros_like(bias_ref)
    bias_ref[pl.ds(at_y, 1)] = column_sum(pres[...])
    bias_ref[pl.ds(4 + at_y, 1)] = column_sum(pre_text[...])
    outputs.finish()


def far_grads_kernel(
    units, grads, act_own, act_mate, pre_own, pre_mate, bias_in, keep_ref, away_ref, bias_ref, blocks, sems, acts, pres, in_sems
):
    far = slice(D, 2 * D)
    loads = []
    for own, mate, total in ((pre_own, pre_mate, pres), (act_own, act_mate, acts)):
        for source, target in ((own, total.at[:CUT]), (mate, total.at[CUT:])):
            loads.append(pltpu.make_async_copy(source.at[:, far], target, in_sems.at[len(loads)]))
            loads[-1].start()
    outputs = Outputs(keep_ref, away_ref, blocks, sems)
    for copy in loads[:2]:
        copy.wait()
    outputs.put(0, contract_rows(units[...], pres[...]), 0)
    for copy in loads[2:]:
        copy.wait()
    outputs.put(0, contract_rows(acts[...], grads[...]), 1)
    bias_ref[...] = bias_in[...]
    bias_ref[pl.ds(lax.rem(lax.axis_index("ffn") + 2, 4), 1)] = column_sum(pres[...])
    outputs.finish()


def near_grads(*args):
    rows = jax.ShapeDtypeStruct((2 * CUT, D), bf16)
    return pl.pallas_call(
        near_grads_kernel,
        out_shape=[jax.ShapeDtypeStruct((2 * D, D), bf16)] * 2 + [rows, rows, jax.ShapeDtypeStruct((8, D), f32)],
        in_specs=[ANY] * 10 + [VMEM] * 4,
        out_specs=[ANY, ANY] + [VMEM] * 3,
        scratch_shapes=[pltpu.VMEM((2, D, D), bf16), pltpu.SemaphoreType.DMA((2,))]
        + [pltpu.VMEM((2 * CUT, D), bf16)] * 2
        + [pltpu.SemaphoreType.DMA((10,))],
        cost_estimate=cost(1),
        compiler_params=params(24),
    )(*args)


def far_grads(*args):
    return pl.pallas_call(
        far_grads_kernel,
        out_shape=[jax.ShapeDtypeStruct((D, D), bf16)] * 2 + [jax.ShapeDtypeStruct((8, D), f32)],
        in_specs=[VMEM] * 2 + [ANY] * 4 + [VMEM],
        out_specs=[ANY, ANY, VMEM],
        scratch_shapes=[pltpu.VMEM((2, D, D), bf16), pltpu.SemaphoreType.DMA((2,))]
        + [pltpu.VMEM((2 * CUT, D), bf16)] * 2
        + [pltpu.SemaphoreType.DMA((4,))],
        cost_estimate=cost(1),
        compiler_params=params(24),
    )(*args)


def text_sum(own_ref, got_first, got_second, b_ref, item):
    txt = slice(VIS + item * TXT, VIS + (item + 1) * TXT)
    total = own_ref[CUT + item * TXT : CUT + (item + 1) * TXT] + b_ref[item * TXT : (item + 1) * TXT].astype(f32)
    return total + got_first[txt].astype(f32) + got_second[txt].astype(f32)


def branch_kernel(
    own_ref, got_first, got_second, b_ref, modal_ref, cot_ref, hid_ref, att_ref, gain_ref, wo_ref,
    hidden_ref, gatt_ref, dwo_ref, sum_ref,
):
    gain = vector(gain_ref)
    sums = [0.0, 0.0, 0.0]
    for item in range(ITEMS):
        at = slice(item * SEQ, (item + 1) * SEQ)
        vis = slice(item * VIS, (item + 1) * VIS)
        vision = own_ref[vis] + (got_first, got_second)[item][:VIS].astype(f32)
        text = text_sum(own_ref, got_first, got_second, b_ref, item)
        grad_unit = unpack_item(vision, text, *slots_of(modal_ref[item : item + 1])).astype(bf16).astype(f32)
        _, hat, scaled = norm_forward(hid_ref[at], 1.0, 0.0)
        grad_norm, grad_gain, grad_shift = norm_backward(grad_unit, hat, scaled, gain)
        grad_hidden = cot_ref[at].astype(f32) + grad_norm
        hidden_ref[at] = grad_hidden
        branch = grad_hidden.astype(bf16)
        gatt_ref[at] = branch
        sums[0] += grad_gain
        sums[1] += grad_shift
        sums[2] += jnp.sum(branch.astype(f32), axis=0, keepdims=True)
    dwo_ref[...] = contract_rows(att_ref[...], gatt_ref[...]).astype(bf16)
    gatt_ref[...] = times_transpose(gatt_ref[...], wo_ref[...]).astype(bf16)
    sum_ref[...] = jnp.concatenate(sums, axis=0)


def scores_kernel(q_ref, k_ref, v_ref, p_ref, gatt_ref, gq_ref, gk_ref, gv_ref):
    low_half = lax.broadcasted_iota(jnp.int32, (1, 128), 1) < HEAD_DIM
    for pair in range(HEADS // 2):
        lanes = slice(pair * 128, (pair + 1) * 128)
        q, k, v, g = q_ref[:, lanes], k_ref[:, lanes], v_ref[:, lanes], gatt_ref[:, lanes]
        gq = gk = gv = 0.0
        for half in range(2):
            mine = low_half if half == 0 else jnp.logical_not(low_half)
            mask = lambda a: jnp.where(mine, a, 0).astype(bf16)
            low = p_ref[0, 2 * pair + half]
            probs = low.astype(f32)
            inner = times_transpose(mask(g), v) * probs
            scores = (inner - probs * jnp.sum(inner, axis=-1, keepdims=True)).astype(bf16)
            gv += contract_rows(low, mask(g))
            gq += matmul(scores, mask(k))
            gk += contract_rows(scores, mask(q))
        gq_ref[:, lanes] = (gq * 0.125).astype(bf16)
        gk_ref[:, lanes] = gk.astype(bf16)
        gv_ref[:, lanes] = gv.astype(bf16)


def backward_scores(q, k, v, p, gatt):
    block = pl.BlockSpec((SEQ, D), lambda i: (i, 0))
    heads = pl.BlockSpec((1, HEADS, SEQ, SEQ), lambda i: (i, 0, 0, 0))
    return pl.pallas_call(
        scores_kernel,
        grid=(ITEMS,),
        out_shape=[jax.ShapeDtypeStruct((ROWS, D), bf16)] * 3,
        in_specs=[block] * 3 + [heads, block],
        out_specs=[block] * 3,
        cost_estimate=cost(25),
        compiler_params=params(20),
    )(q, k, v, p, gatt)


def shared_kernel(
    tok_ref, gain1, shift1, gq_ref, gk_ref, gv_ref, wq_ref, wk_ref, wv_ref, hidden_ref, dwo_ref, sums_two, grad_live, bias_rows,
    tok_out, keep_ref, away_ref,
):
    gain = vector(gain1)
    unit, hat, scaled = norm_forward(tok_ref[...].astype(f32), gain, vector(shift1))
    low = unit.astype(bf16)
    dwq = contract_rows(low, gq_ref[...]).astype(bf16)
    dwk = contract_rows(low, gk_ref[...]).astype(bf16)
    dwv = contract_rows(low, gv_ref[...]).astype(bf16)
    back = times_transpose(gq_ref[...], wq_ref[...]) + times_transpose(gk_ref[...], wk_ref[...]) + times_transpose(gv_ref[...], wv_ref[...])
    grad_norm, grad_gain, grad_shift = norm_backward(back, hat, scaled, gain)
    tok_out[...] = (hidden_ref[...] + grad_norm).astype(bf16)
    total = lambda ref: jnp.sum(ref[...].astype(f32), axis=0, keepdims=True)
    rows = [grad_gain, grad_shift, total(gq_ref), total(gv_ref), sums_two[...], grad_live[...], bias_rows[...]]
    vec = jnp.concatenate(rows + [jnp.zeros((VEC - 17, D), f32)], axis=0).astype(bf16)

    def put(mine, other):
        mine[:D] = dwq
        mine[D : 2 * D] = dwk
        other[:D] = dwv
        other[D : 2 * D] = dwo_ref[...]
        mine[2 * D :] = vec
        other[2 * D :] = vec

    @pl.when(core_index() == 0)
    def _():
        put(keep_ref, away_ref)

    @pl.when(core_index() == 1)
    def _():
        put(away_ref, keep_ref)


def mixed_kernel(own_ref, got_first, got_second, b_ref, modal_ref, hid_ref, b_out, near_small, out_ref):
    first = core_index() == 0
    mine, other = b_out[...].astype(f32), near_small[1:2].astype(f32)
    bias_vision, bias_text = jnp.where(first, mine, other), jnp.where(first, other, mine)
    for item in range(ITEMS):
        at = slice(item * SEQ, (item + 1) * SEQ)
        vis = slice(item * VIS, (item + 1) * VIS)
        vision = own_ref[vis] + (got_first, got_second)[item][:VIS].astype(f32) + bias_vision
        text = text_sum(own_ref, got_first, got_second, b_ref, item) + bias_text
        rows = unpack_item(vision, text, *slots_of(modal_ref[item : item + 1])).astype(bf16).astype(f32)
        out_ref[at] = (hid_ref[at] + rows).astype(bf16)


def split_kernel(count, size, axes, *refs):
    ins, outs, total = refs[:count], refs[count:-1], refs[-1]
    extra = total.shape[0] - 4 * size
    total[...] = sum(ref[: 4 * size + extra].astype(f32) for ref in ins).astype(bf16)
    me = place(axes)
    for step, out in zip((0, 1, 3, 2), outs):
        at = pl.multiple_of(lax.rem(me + step, 4) * size, 16)
        out[:size] = total[pl.ds(at, size)]
        if extra:
            out[size:] = total[4 * size :]


def split(pieces, size, extra, axes):
    outs = [((size + extra, D), bf16)] * 4
    scratch = [pltpu.VMEM((4 * size + extra, D), bf16)]
    return call(functools.partial(split_kernel, len(pieces), size, axes), outs, *pieces, scratch=scratch)


def block_steps(size):
    first = core_index() == 0
    return jnp.where(first, 4 * size, size), jnp.where(first, size, 4 * size)


def expert_split_kernel(size, near_keep, near_got, far_keep, far_got, *refs):
    outs, total = refs[:-1], refs[-1]
    near = (near_keep[...].astype(f32) + near_got[...].astype(f32)).astype(bf16)
    total[:D] = near[:D]
    total[D : 2 * D] = (far_keep[...].astype(f32) + far_got[...].astype(f32)).astype(bf16)
    total[2 * D :] = near[D:]
    me = place("xz")
    outer, inner = block_steps(size)
    for step, out in zip((0, 1, 3, 2), outs):
        base = lax.rem(me + step, 4) * outer
        for matrix in range(3):
            for block in range(4):
                at = pl.multiple_of(base + matrix * D + block * inner, 16)
                to = (matrix * 4 + block) * size
                out[to : to + size] = total[pl.ds(at, size)]


EXP = D // 16


def expert_second_kernel(*refs):
    ins, outs, total = refs[:4], refs[4:-1], refs[-1]
    total[...] = sum(ref[...].astype(f32) for ref in ins).astype(bf16)
    me = place("zx")
    for step, out in zip((0, 1, 3, 2), outs):
        index = lax.rem(me + step, 4)
        for matrix in range(3):
            at = pl.multiple_of((matrix * 4 + index) * EXP, 16)
            out[matrix * EXP : (matrix + 1) * EXP] = total[pl.ds(at, EXP)]


def expert_third_kernel(*refs):
    ins, outs = refs[:4], refs[4:]
    total = sum(ref[...].astype(f32) for ref in ins).astype(bf16)
    for matrix, out in enumerate(outs):
        out[...] = total[matrix * EXP : (matrix + 1) * EXP]


def expert_keep_kernel(near, far, text, keep, away):
    first = core_index() == 0
    vision, language = near[...].astype(f32) + far[...].astype(f32), text[...].astype(f32)
    keep[...] = jnp.where(first, vision, language).astype(bf16)
    away[...] = jnp.where(first, language, vision).astype(bf16)


def sum_kernel(*refs):
    ins, out = refs[:4], refs[4]
    out[...] = sum(ref[...].astype(f32) for ref in ins).astype(bf16)


def fourth_kernel(*refs):
    ins, (keep, got, out, vec) = refs[:4], refs[4:]
    total = sum(ref[...].astype(f32) for ref in ins)
    out[: 2 * EXP] = total[: 2 * EXP].astype(bf16)
    vec[...] = total[2 * EXP :]
    first = core_index() == 0
    k, g = keep[...].astype(f32), got[...].astype(f32)
    out[2 * EXP : 3 * EXP] = jnp.where(first, k, g).astype(bf16)
    out[3 * EXP :] = jnp.where(first, g, k).astype(bf16)


def fifth_kernel(mine, first, third, second, shared, expert):
    me = place("xz")
    for step, piece in zip((0, 1, 3, 2), (mine, first, third, second)):
        index = lax.rem(me + 4 - step, 4)
        shared[pl.ds(pl.multiple_of(index * 2 * EXP, 16), 2 * EXP)] = piece[: 2 * EXP]
        at = pl.multiple_of(index * EXP, 16)
        expert[pl.ds(at, EXP)] = piece[2 * EXP : 3 * EXP]
        expert[pl.ds(4 * EXP + at, EXP)] = piece[3 * EXP :]


def expert_finish_kernel(mine, first, third, second, w_in, w_out):
    outer, inner = block_steps(EXP)
    me = place("zx")
    for step, piece in zip((0, 1, 3, 2), (mine, first, third, second)):
        base = lax.rem(me + 4 - step, 4) * inner
        for block in range(4):
            at = pl.ds(pl.multiple_of(base + block * outer, 16), EXP)
            w_in[at] = piece[block * EXP : (block + 1) * EXP].astype(f32)
            w_out[at] = piece[(4 + block) * EXP : (5 + block) * EXP].astype(f32)


def join_kernel(axes, *refs):
    ins, out = refs[:4], refs[4]
    size = out.shape[0] // 4
    me = place(axes)
    for step, piece in zip((0, 1, 3, 2), ins):
        at = pl.multiple_of(lax.rem(me + 4 - step, 4) * size, 16)
        out[pl.ds(at, size)] = piece[:size]


def join(piece, got, axes, size=None):
    return call(functools.partial(join_kernel, axes), [((4 * (size or piece.shape[0]), D), bf16)], piece, *got)[0]


def finish_kernel(mine, other, vec, wq, wk, wv, wo, g1, s1, bq, bv, g2, s2, bo, b_in, b_out):
    first = core_index() == 0
    for low, high, at in ((wq, wv, 0), (wk, wo, 1)):
        m, o = mine[at].astype(f32), other[at].astype(f32)
        low[...] = jnp.where(first, m, o)
        high[...] = jnp.where(first, o, m)

    @pl.when(pl.program_id(0) == 0)
    def _():
        for ref, row in ((g1, 0), (s1, 1), (bq, 2), (bv, 3), (g2, 4), (s2, 5), (bo, 6)):
            ref[...] = vec[row]
        b_in[...] = vec[pl.ds(9 + 4 * core_index() + lax.axis_index("ffn"), 1)]
        b_out[...] = vec[pl.ds(7 + core_index(), 1)]


def finish(mine, other, vec):
    steps = 4
    size = D // steps
    pair = pl.BlockSpec((2, size, D), lambda i: (0, i, 0))
    block = pl.BlockSpec((size, D), lambda i: (i, 0))
    return pl.pallas_call(
        finish_kernel,
        grid=(steps,),
        out_shape=[jax.ShapeDtypeStruct((D, D), f32)] * 4
        + [jax.ShapeDtypeStruct((D,), f32)] * 7
        + [jax.ShapeDtypeStruct((1, D), f32)] * 2,
        in_specs=[pair, pair, VMEM],
        out_specs=[block] * 4 + [VMEM] * 9,
        cost_estimate=cost(5),
        compiler_params=params(12),
    )(mine.reshape(2, D, D), other.reshape(2, D, D), vec)


def body(
    tokens,
    cotangent,
    modality,
    ln1_gain,
    ln1_shift,
    w_query,
    b_query,
    w_key,
    w_value,
    b_value,
    w_attn_out,
    b_attn_out,
    ln2_gain,
    ln2_shift,
    w_in,
    b_in,
    w_out,
    b_out,
):
    flat_tokens = tokens.reshape(ROWS, D)
    flat_cot = cotangent.reshape(ROWS, D)
    w_in, w_out = w_in[0], w_out[0]

    part_in, part_out, cot_first, cot_second, small, grad_text = parts(w_in, w_out, flat_cot, b_in, b_out, modality)
    part_in = send(part_in, lambda x, z, c, y: (x, z, 0, (y + 2) % 4) if c == 0 else None)
    part_out = send(part_out, lambda x, z, c, y: (x, z, 1, (y + 2) % 4) if c == 0 else None)

    cot_first, cot_second = swap_pair(cot_first), swap_other(cot_second)

    vectors = (ln1_gain, ln1_shift, b_query, b_value, b_attn_out, ln2_gain, ln2_shift)
    query, key, value, probs, attended, hidden_one, own_first, own_second, text_own = forward_attention(
        flat_tokens, modality, vectors, (w_query, w_key, w_value, w_attn_out), grad_text
    )
    sent_first, sent_second, text_own = tie((own_first, own_second, text_own), cot_first, cot_second)
    got_first, got_second, got_b = swap_pair(sent_first), swap_other(sent_second), swap_far(text_own)
    near_in, near_out = swap_core(tie(w_in, own_first)), swap_core(tie(w_out, own_first))
    far_part = jnp.where(core_index() == 0, *tie((part_in, part_out), own_first))
    far_got = shifts([far_part] * 3, "xz")
    near_small = swap_core(tie(small, far_got[2]))
    grad_own, grad_live = call(pack_kernel, [((CUT, D), bf16), ((2, D), f32)], tie(flat_cot, own_first), modality, micros=2)
    grad_mate, text_mate = call(pack_mates_kernel, [((CUT, D), bf16), ((2 * CUT_TXT, D), bf16)], cot_first, tie(cot_second, own_first))
    far_got = tie(far_got, got_first, got_second, got_b, near_small, grad_own, grad_mate)
    far_mine = join(far_part, far_got, "xz", D // 4)
    far_other = swap_core(far_mine)

    text_weights = (w_in, w_out, near_in, near_out)
    vision_weights = text_weights + (far_mine, far_other)
    text_home, text_mates, text_back, text_out, units_text, grads_text, text_act, text_pre = text_rows(
        text_own, got_first, got_second, got_b, text_mate, b_in, near_small, *text_weights
    )
    got_text = swap_far(text_back)
    smalls = (b_in, far_part, near_small)
    back_first, back_second, out_first, out_second, mate_act, mate_pre = vision_rows(
        True, (got_first, got_second), grad_mate, text_mates, smalls, vision_weights
    )
    back_first, back_second = swap_pair(back_first), swap_other(back_second)
    own_back, own_out, own_act, own_pre = vision_rows(
        False, (own_first, own_second), tie(grad_own, grad_mate, mate_act), text_home, smalls, vision_weights
    )

    near_keep, near_away, units, grads, bias_rows = near_grads(
        own_first, own_second, got_first, got_second, grad_own, grad_mate, own_act, mate_act, own_pre, mate_pre,
        units_text, grads_text, text_act, text_pre,
    )
    far_keep, far_away, bias_rows = far_grads(units, grads, own_act, mate_act, own_pre, mate_pre, bias_rows)
    near_away_got = swap_core(tie(near_away, back_first, back_second, got_text))

    grad_hidden, grad_attended, grad_w_attn_out, sums_two = call(
        branch_kernel,
        [((ROWS, D), f32), ((ROWS, D), bf16), ((D, D), bf16), ((3, D), f32)],
        own_back, tie(back_first, far_keep), back_second, got_text, modality, flat_cot, hidden_one, attended, ln2_gain, w_attn_out,
        micros=100, mebibytes=20,
    )
    far_away_got = swap_core(tie(far_away, back_first, back_second, got_text))
    out_first, out_second = tie((out_first, out_second), back_first, back_second)
    out_first, out_second = swap_pair(out_first), swap_other(out_second)
    expert_pieces = call(
        functools.partial(expert_split_kernel, EXP),
        [((12 * EXP, D), bf16)] * 4,
        near_keep, near_away_got, far_keep, tie(far_away_got, grad_attended),
        scratch=[pltpu.VMEM((3 * D, D), bf16)], micros=2, mebibytes=20,
    )
    expert_got = shifts(expert_pieces[1:], "xz")
    grad_query, grad_key, grad_value = backward_scores(query, key, value, probs, tie(grad_attended, *expert_pieces))
    grad_tokens, shared_keep, shared_away = call(
        shared_kernel,
        [((ROWS, D), bf16)] + [((2 * D + VEC, D), bf16)] * 2,
        flat_tokens, ln1_gain, ln1_shift, grad_query, grad_key, grad_value, w_query, w_key, w_value,
        grad_hidden, grad_w_attn_out, sums_two, grad_live, bias_rows,
        micros=11, mebibytes=28,
    )

    shared_got = swap_core(tie(shared_away, *expert_got[:2], out_first, out_second))
    shared_pieces = split([shared_keep, shared_got], 2 * D // 4, VEC, "yx")
    shared_got = shifts(shared_pieces[1:], "yx")
    expert_pieces = call(
        expert_second_kernel,
        [((3 * EXP, D), bf16)] * 4,
        expert_pieces[0], *tie(expert_got, *shared_pieces),
        scratch=[pltpu.VMEM((12 * EXP, D), bf16)],
    )
    expert_got = shifts(expert_pieces[1:], "zx")
    shared_pieces = split([shared_pieces[0]] + tie(shared_got, *expert_got[:2]), 2 * EXP, VEC, "xz")
    shared_got = shifts(shared_pieces[1:], "xz")
    near, far, text = call(expert_third_kernel, [((EXP, D), bf16)] * 3, expert_pieces[0], *expert_got)
    far = swap_far(far)
    size = 2 * EXP + VEC
    (shared_total,) = call(sum_kernel, [((size, D), bf16)], shared_pieces[0], *tie(shared_got, far))
    shared_got = shifts([shared_total] * 3, "zy")
    expert_keep, expert_away = call(expert_keep_kernel, [((EXP, D), bf16)] * 2, near, far, text)
    low, vec = call(
        fourth_kernel,
        [((4 * EXP, D), bf16), ((VEC, D), f32)],
        shared_total, *shared_got, expert_keep, swap_core(expert_away),
    )
    got_text_out = swap_far(tie(text_out, low))
    shared_sum, expert_sum = call(
        fifth_kernel, [((8 * EXP, D), bf16)] * 2, low, *shifts([low] * 3, "xz")
    )
    shared_got = shifts([shared_sum] * 3, "yx")
    expert_got = shifts([expert_sum] * 3, "zx")
    shared_sum = join(shared_sum, shared_got, "yx")
    shared_sum = tie(shared_sum, expert_got[0], expert_got[1])
    outs = finish(shared_sum, swap_core(shared_sum), vec)
    d_query, d_key, d_value, d_out, d_gain1, d_shift1, d_bq, d_bv, d_gain2, d_shift2, d_bo, d_b_in, d_b_out = outs
    grad_w_in, grad_w_out = call(expert_finish_kernel, [((D, D), f32)] * 2, tie(expert_sum, d_query), *expert_got)
    (mixed,) = call(
        mixed_kernel,
        [((ROWS, D), bf16)],
        tie(own_out, d_query), out_first, out_second, got_text_out, modality, hidden_one, b_out, near_small,
        micros=4, mebibytes=16,
    )
    return (
        mixed.reshape(tokens.shape),
        grad_tokens.reshape(tokens.shape),
        d_gain1,
        d_shift1,
        d_query,
        d_bq,
        d_key,
        d_value,
        d_bv,
        d_out,
        d_bo,
        d_gain2,
        d_shift2,
        grad_w_in[None],
        d_b_in,
        grad_w_out[None],
        d_b_out,
    )


def solution(mesh):
    items = P(AXES, None, None)
    expert_specs = (P("expert", None, "ffn"), P("expert", "ffn"), P("expert", "ffn", None), P("expert", None))
    return jax.shard_map(
        body,
        mesh=mesh,
        in_specs=(items, items, P(AXES, None)) + (P(),) * 11 + expert_specs,
        out_specs=(items, items) + (P(),) * 11 + expert_specs,
        check_vma=False,
    )
```

```python
import functools

import jax
import jax.numpy as jnp
from jax import lax
from jax.experimental import pallas as pl
from jax.experimental.pallas import tpu as pltpu
from jax.sharding import PartitionSpec as P

D = 768
HEAD_DIM = 64
HEADS = D // HEAD_DIM
PATCHES = 197
SEQ = 256
ITEMS = 2
ROWS = ITEMS * SEQ
TEXT_AT = 192
VIS = 208
TXT = 48
CUT = ITEMS * VIS
CUT_TXT = ITEMS * TXT
BACK = VIS + CUT_TXT
COT = SEQ + TXT + 16
VEC = 24

epsilon = 1e-05
root_half = 0.7071067811865476
inv_root_tau = 0.3989422804014327
AXES = ("dp", "expert", "ffn")
bf16 = jnp.bfloat16
f32 = jnp.float32


def split_index(index):
    return index // 32, index // 8 % 4, index // 4 % 2, index % 4


def join_index(x, z, core, y):
    return ((x * 4 + z) * 2 + core) * 4 + y


def send(value, where):
    pairs = []
    for index in range(128):
        target = where(*split_index(index))
        if target is not None:
            pairs.append((index, join_index(*target)))
    return lax.ppermute(value, AXES, pairs)


def swap_core(value):
    return send(value, lambda x, z, c, y: (x, z, 1 - c, y))


def swap_pair(value):
    return send(value, lambda x, z, c, y: (x, z, c, y ^ 1))


def swap_other(value):
    return send(value, lambda x, z, c, y: (x, z, c, 3 - y))


def swap_far(value):
    return send(value, lambda x, z, c, y: (x, z, c, y ^ 2))


def shift(value, axes, step):
    def where(x, z, c, y):
        at = dict(x=x, z=z, y=y)
        at[axes[c]] = (at[axes[c]] + step) % 4
        return at["x"], at["z"], c, at["y"]

    return send(value, where)


def shifts(pieces, axes):
    return [shift(piece, axes, step) for piece, step in zip(pieces, (1, 3, 2))]


def tie(value, *others):
    return lax.optimization_barrier((value, others))[0]


def core_index():
    return lax.axis_index("expert")


def place(axes):
    dp = lax.axis_index("dp")
    at = dict(x=dp // 4, z=dp % 4, y=lax.axis_index("ffn"))
    return jnp.where(core_index() == 0, at[axes[0]], at[axes[1]])


def norm_forward(values, gain_vec, shift_vec):
    centre = values - jnp.mean(values, axis=-1, keepdims=True)
    scaled = lax.rsqrt(jnp.mean(centre * centre, axis=-1, keepdims=True) + epsilon)
    normal_hat = centre * scaled
    return (normal_hat * gain_vec + shift_vec, normal_hat, scaled)


def norm_backward(grad_result, normal_hat, scaled, gain_vec):
    grad_hat = grad_result * gain_vec
    inner_term = (
        grad_hat
        - jnp.mean(grad_hat, axis=-1, keepdims=True)
        - normal_hat * jnp.mean(grad_hat * normal_hat, axis=-1, keepdims=True)
    )
    return (
        scaled * inner_term,
        jnp.sum(grad_result * normal_hat, axis=0, keepdims=True),
        jnp.sum(grad_result, axis=0, keepdims=True),
    )


def matmul(first_op, second_op):
    return jnp.dot(first_op, second_op, preferred_element_type=f32)


def contract_rows(first_op, second_op):
    return lax.dot_general(first_op, second_op, (((0,), (0,)), ((), ())), preferred_element_type=f32)


def times_transpose(first_op, second_op):
    return lax.dot_general(first_op, second_op, (((1,), (1,)), ((), ())), preferred_element_type=f32)


def vector(ref):
    return ref[...].astype(f32).reshape(1, D)


def slots_of(row):
    has_image = jnp.max(jnp.where(row == 0, 1.0, 0.0), axis=1, keepdims=True)
    texts = jnp.sum(jnp.where(row == 1, 1.0, 0.0), axis=1, keepdims=True)
    start = has_image * PATCHES
    slot = lax.broadcasted_iota(jnp.int32, (SEQ, 1), 0).astype(f32)
    modal = jnp.where(slot < start, 0.0, jnp.where(slot < start + texts, 1.0, 2.0))
    return has_image > 0.5, modal


def text_of(rows, has_image, modal):
    at = slice(TEXT_AT, TEXT_AT + TXT)
    return jnp.where(has_image, jnp.where(modal[at] == 1, rows[at], 0.0), jnp.where(modal[:TXT] == 1, rows[:TXT], 0.0))


def unpack_item(vision, text, has_image, modal):
    whole = jnp.concatenate(
        [
            jnp.where(has_image, vision[:TXT], text),
            vision[TXT:TEXT_AT],
            jnp.where(modal[TEXT_AT:VIS] == 1, text[: VIS - TEXT_AT], vision[TEXT_AT:]),
            text[VIS - TEXT_AT :],
            jnp.zeros((SEQ - TEXT_AT - TXT, D), f32),
        ],
        axis=0,
    )
    return jnp.where(modal < 2, whole, 0.0)


VMEM = pl.BlockSpec(memory_space=pltpu.VMEM)
ANY = pl.BlockSpec(memory_space=pl.ANY)


def cost(micros):
    return pl.CostEstimate(flops=0, bytes_accessed=int(micros * 1e5), transcendentals=0)


def params(mebibytes):
    return pltpu.CompilerParams(vmem_limit_bytes=mebibytes * 1024 * 1024)


def call(kernel, outs, *args, scratch=(), any_from=None, micros=1.5, mebibytes=12):
    specs = [VMEM] * len(args) if any_from is None else [VMEM] * any_from + [ANY] * (len(args) - any_from)
    return pl.pallas_call(
        kernel,
        out_shape=[jax.ShapeDtypeStruct(shape, dtype) for shape, dtype in outs],
        in_specs=specs,
        out_specs=[VMEM] * len(outs),
        scratch_shapes=list(scratch),
        cost_estimate=cost(micros),
        compiler_params=params(mebibytes),
    )(*args)


def pack_kernel(grad_ref, modal_ref, out_ref, sum_ref):
    sums = [0.0, 0.0]
    for item in range(ITEMS):
        has_image, modal = slots_of(modal_ref[item : item + 1])
        grad = grad_ref[item * SEQ : (item + 1) * SEQ].astype(f32)
        vision = jnp.where(modal[:VIS] == 0, grad[:VIS], 0.0)
        out_ref[item * VIS : (item + 1) * VIS] = vision.astype(bf16)
        sums[0] += jnp.sum(vision, axis=0, keepdims=True)
        sums[1] += jnp.sum(text_of(grad, has_image, modal), axis=0, keepdims=True)
    sum_ref[...] = jnp.concatenate(sums, axis=0)


def part_kernel(w_in, w_out, grad, b_in, b_out, modal_ref, in_ref, out_ref, first_ref, second_ref, small_ref, text_ref, sems):
    dp, share = lax.axis_index("dp"), D // 4
    x, z = lax.div(dp, 4), lax.rem(dp, 4)
    copies = [
        pltpu.make_async_copy(w_in.at[pl.ds(pl.multiple_of(x * share, 16), share)], in_ref.at[:share], sems.at[0]),
        pltpu.make_async_copy(w_out.at[pl.ds(pl.multiple_of(z * share, 16), share)], out_ref.at[:share], sems.at[1]),
        pltpu.make_async_copy(grad.at[:SEQ], first_ref.at[:SEQ], sems.at[2]),
        pltpu.make_async_copy(grad.at[SEQ:], second_ref.at[:SEQ], sems.at[3]),
    ]
    for copy in copies:
        copy.start()
    small = [b_in[...].astype(f32), b_out[...].astype(f32), jnp.zeros((14, D), f32)]
    small = jnp.concatenate(small, axis=0).astype(bf16)
    small_ref[...] = small
    modal = jnp.concatenate([modal_ref[...].astype(f32), jnp.zeros((16 - ITEMS, SEQ), f32)], axis=0)
    modal = jnp.concatenate([modal, jnp.zeros((16, D - SEQ), f32)], axis=1).astype(bf16)
    first_ref[SEQ + TXT :] = modal
    second_ref[SEQ + TXT :] = modal
    in_ref[share:] = small
    out_ref[share:] = small
    for copy in copies:
        copy.wait()
    for item, source, target in ((0, first_ref, second_ref), (1, second_ref, first_ref)):
        text = text_of(source[:SEQ].astype(f32), *slots_of(modal_ref[item : item + 1]))
        target[SEQ : SEQ + TXT] = text.astype(bf16)
        text_ref[item * TXT : (item + 1) * TXT] = text.astype(bf16)


def parts(*args):
    return pl.pallas_call(
        part_kernel,
        out_shape=[jax.ShapeDtypeStruct((D // 4 + 16, D), bf16)] * 2 + [jax.ShapeDtypeStruct((COT, D), bf16)] * 2
        + [jax.ShapeDtypeStruct((16, D), bf16), jax.ShapeDtypeStruct((CUT_TXT, D), bf16)],
        in_specs=[ANY] * 3 + [VMEM] * 3,
        out_specs=[VMEM] * 6,
        scratch_shapes=[pltpu.SemaphoreType.DMA((4,))],
        cost_estimate=cost(1),
        compiler_params=params(60),
    )(*args)


def forward_kernel(
    tok_ref, modal_ref, gain1, shift1, b_query, b_value, b_out, gain2, shift2, wq_ref, wk_ref, wv_ref, wo_ref,
    grad_text, q_out, k_out, v_out, p_out, att_out, hid_out, first_out, second_out, text_out,
    held, sems, q_all, k_all, v_all, p_all, att_all, hid_all, out_sems, first_ref, second_ref, text_ref, sent_sems,
):
    item = pl.program_id(0)
    pieces = 4
    rows = D // pieces

    def weight_copy(i, piece):
        at = pl.ds(piece * rows, rows)
        return pltpu.make_async_copy((wq_ref, wk_ref, wv_ref, wo_ref)[i].at[at], held.at[i, at], sems.at[i, piece])

    def start_weight(i):
        @pl.when(item == 0)
        def _():
            for piece in range(pieces):
                weight_copy(i, piece).start()

    def wait_weight(i):
        @pl.when(item == 0)
        def _():
            for piece in range(pieces):
                weight_copy(i, piece).wait()

    start_weight(0)

    @pl.when(item == 0)
    def _():
        text_ref[CUT_TXT:] = grad_text[...]

    outs = [(q_all, q_out), (k_all, k_out), (v_all, v_out), (p_all, p_out), (att_all, att_out), (hid_all, hid_out)]

    def copy_out(i, at):
        return pltpu.make_async_copy(outs[i][0].at[at], outs[i][1].at[at], out_sems.at[at, i])

    sent = [
        (first_ref.at[:VIS], first_out.at[:VIS]),
        (second_ref.at[:VIS], second_out.at[:VIS]),
        (first_ref.at[VIS:], first_out.at[VIS:]),
        (second_ref.at[VIS:], second_out.at[VIS:]),
        (text_ref, text_out),
    ]
    sent = [pltpu.make_async_copy(source, target, sent_sems.at[i]) for i, (source, target) in enumerate(sent)]

    q_ref, k_ref, v_ref, p_ref, att_ref = (ref.at[item] for ref in (q_all, k_all, v_all, p_all, att_all))
    x = tok_ref[...].astype(f32)
    unit, _, _ = norm_forward(x, vector(gain1), vector(shift1))
    unit = unit.astype(bf16)
    start_weight(1)
    wait_weight(0)
    q_ref[...] = ((matmul(unit, held[0]) + vector(b_query)).astype(bf16) * 0.125).astype(bf16)
    copy_out(0, item).start()
    start_weight(2)
    wait_weight(1)
    k_ref[...] = matmul(unit, held[1]).astype(bf16)
    copy_out(1, item).start()
    start_weight(3)
    wait_weight(2)
    v_ref[...] = (matmul(unit, held[2]) + vector(b_value)).astype(bf16)
    copy_out(2, item).start()
    row = modal_ref[pl.ds(item, 1)]
    bias = jnp.where(row < 2, 0.0, -1e30)
    low_half = lax.broadcasted_iota(jnp.int32, (1, 128), 1) < HEAD_DIM
    ones = jnp.ones((SEQ, 128), bf16)
    for pair in range(HEADS // 2):
        lanes = slice(pair * 128, (pair + 1) * 128)
        q, k, v = q_ref[:, lanes], k_ref[:, lanes], v_ref[:, lanes]
        halves = []
        for half in range(2):
            mine = low_half if half == 0 else jnp.logical_not(low_half)
            scores = times_transpose(jnp.where(mine, q, 0).astype(bf16), k) + bias
            scores = jnp.exp(scores - jnp.max(scores, axis=-1, keepdims=True))
            both = matmul(scores.astype(bf16), jnp.concatenate([v, ones], axis=1))
            inverse = 1.0 / both[:, 128:]
            p_ref[2 * pair + half] = (scores * jnp.concatenate([inverse, inverse], axis=1)).astype(bf16)
            halves.append(both[:, :128] * inverse)
        att_ref[:, lanes] = jnp.where(low_half, halves[0], halves[1]).astype(bf16)
    copy_out(3, item).start()
    copy_out(4, item).start()
    wait_weight(3)
    hidden = x + matmul(att_ref[...], held[3]) + vector(b_out)
    hid_all[item] = hidden
    copy_out(5, item).start()
    unit, _, _ = norm_forward(hidden, vector(gain2), vector(shift2))
    has_image, _ = slots_of(row)
    vision = unit[:VIS].astype(bf16)
    text = jnp.where(has_image, unit[TEXT_AT : TEXT_AT + TXT], unit[:TXT]).astype(bf16)
    text_ref[pl.ds(pl.multiple_of(item * TXT, 16), TXT)] = text
    first_ref[pl.ds(pl.multiple_of(VIS + item * TXT, 16), TXT)] = text
    second_ref[pl.ds(pl.multiple_of(VIS + item * TXT, 16), TXT)] = text

    @pl.when(item == 0)
    def _():
        first_ref[:VIS] = vision
        sent[0].start()

    @pl.when(item == 1)
    def _():
        second_ref[:VIS] = vision
        for copy in sent[1:]:
            copy.start()
        for at in range(ITEMS):
            for i in range(len(outs)):
                copy_out(i, at).wait()
        for copy in sent:
            copy.wait()


def forward_attention(tokens, modality, vectors, weights, *rest):
    block = pl.BlockSpec((SEQ, D), lambda i: (i, 0))
    shapes = [((ITEMS, SEQ, D), bf16)] * 3 + [((ITEMS, HEADS, SEQ, SEQ), bf16), ((ITEMS, SEQ, D), bf16), ((ITEMS, SEQ, D), f32)]
    sent = [((BACK, D), bf16), ((BACK, D), bf16), ((2 * CUT_TXT, D), bf16)]
    outs = pl.pallas_call(
        forward_kernel,
        grid=(ITEMS,),
        out_shape=[jax.ShapeDtypeStruct(*s) for s in shapes + sent],
        in_specs=[block] + [VMEM] * 8 + [ANY] * 4 + [VMEM],
        out_specs=[ANY] * 9,
        scratch_shapes=[pltpu.VMEM((4, D, D), bf16), pltpu.SemaphoreType.DMA((4, 4))]
        + [pltpu.VMEM(*s) for s in shapes]
        + [pltpu.SemaphoreType.DMA((ITEMS, 6))]
        + [pltpu.VMEM(*s) for s in sent]
        + [pltpu.SemaphoreType.DMA((5,))],
        cost_estimate=cost(10),
        compiler_params=params(56),
    )(tokens, modality, *vectors, *weights, *rest)
    flat = [out.reshape(ROWS, D) for out in outs[:3]]
    return flat + [outs[3], outs[4].reshape(ROWS, D), outs[5].reshape(ROWS, D)] + list(outs[6:])


def fetch(first, second, buffer, sem):
    @pl.when(core_index() == 0)
    def _():
        pltpu.make_async_copy(first, buffer, sem).start()

    @pl.when(core_index() == 1)
    def _():
        pltpu.make_async_copy(second, buffer, sem).start()


def row_pass(unit, grad, first, bias, second, act_ref, pre_ref, base):
    for at in range(0, D, 256):
        cols = slice(at, at + 256)
        kept = slice(base + at, base + at + 256)
        pre_act = matmul(unit, first[:, cols]) + bias[:, cols]
        cdf = 0.5 + 0.5 * lax.erf(pre_act * root_half)
        act_ref[:, kept] = (pre_act * cdf).astype(bf16)
        slope = cdf + pre_act * (jnp.exp(-0.5 * pre_act * pre_act) * inv_root_tau)
        pre_ref[:, kept] = (times_transpose(grad, second[cols, :]) * slope).astype(bf16)


def vision_kernel(
    mates, first_unit, second_unit, grad_ref, text_ref, b_in, far_part, near_small,
    w_in, w_out, near_in, near_out, far_mine, far_other, *refs,
):
    outs, (act_ref, pre_ref, held, sems, units) = refs[:-5], refs[-5:]
    fetch(w_in, near_in, held.at[0], sems.at[0])
    fetch(w_out, near_out, held.at[1], sems.at[1])
    fetch(far_mine, far_other, held.at[2], sems.at[2])
    fetch(far_other, far_mine, held.at[3], sems.at[3])
    first = core_index() == 0
    biases = (
        jnp.where(first, b_in[...].astype(f32), near_small[0:1].astype(f32)),
        far_part[D // 4 : D // 4 + 1].astype(f32),
    )
    units[:VIS] = first_unit[:VIS]
    units[VIS:] = second_unit[:VIS]
    unit, grad = units[...], grad_ref[...]
    for part in range(2):
        for slot in (2 * part, 2 * part + 1):
            pltpu.make_async_copy(w_in, held.at[slot], sems.at[slot]).wait()
        row_pass(unit, grad, held.at[2 * part], biases[part], held.at[2 * part + 1], act_ref, pre_ref, part * D)
    back = times_transpose(pre_ref[:, :D], held[0]) + times_transpose(pre_ref[:, D:], held[2])
    out = matmul(act_ref[:, :D], held[1]) + matmul(act_ref[:, D:], held[3])
    if mates:
        for item in range(2):
            at = slice(item * VIS, (item + 1) * VIS)
            outs[item][:VIS] = back[at].astype(bf16)
            outs[item][VIS:] = text_ref[2 * item * CUT_TXT : (2 * item + 1) * CUT_TXT]
            outs[2 + item][:VIS] = out[at].astype(bf16)
            outs[2 + item][VIS:] = text_ref[(2 * item + 1) * CUT_TXT : (2 * item + 2) * CUT_TXT]
    else:
        outs[0][:CUT] = back
        outs[0][CUT:] = text_ref[:CUT_TXT]
        outs[1][:CUT] = out
        outs[1][CUT:] = text_ref[CUT_TXT:]


def vision_rows(mates, units, grad, text, smalls, weights):
    outs = [((BACK, D), bf16)] * 4 if mates else [((ROWS, D), f32)] * 2
    outs += [((CUT, 2 * D), bf16)] * 2
    scratch = [pltpu.VMEM((4, D, D), bf16), pltpu.SemaphoreType.DMA((4,)), pltpu.VMEM((CUT, D), bf16)]
    kernel = functools.partial(vision_kernel, mates)
    return call(kernel, outs, *units, grad, text, *smalls, *weights, scratch=scratch, any_from=7, micros=3, mebibytes=28)


def pack_mates_kernel(cot_first, cot_second, grad_ref, text_ref):
    for item, cot in ((0, cot_first), (1, cot_second)):
        modality = cot[SEQ + TXT :, :SEQ].astype(f32)
        has_image, modal = slots_of(modality[item : item + 1])
        grad = cot[:SEQ].astype(f32)
        grad_ref[item * VIS : (item + 1) * VIS] = jnp.where(modal[:VIS] == 0, grad[:VIS], 0.0).astype(bf16)
        at = item * CUT_TXT
        here, there = at + item * TXT, at + (1 - item) * TXT
        text_ref[here : here + TXT] = text_of(grad, has_image, modal).astype(bf16)
        text_ref[there : there + TXT] = cot[SEQ : SEQ + TXT]


def text_kernel(
    own_text, got_first, got_second, got_b, mates_grad, b_in, near_small, w_in, w_out, near_in, near_out,
    home_ref, mates_ref, b_back, b_out, unit_ref, grad_ref, act_ref, pre_ref, held, sems,
):
    fetch(near_in, w_in, held.at[0], sems.at[0])
    fetch(near_out, w_out, held.at[1], sems.at[1])
    unit_ref[:CUT_TXT] = own_text[:CUT_TXT]
    unit_ref[CUT_TXT : 2 * CUT_TXT] = got_first[VIS:]
    unit_ref[2 * CUT_TXT : 3 * CUT_TXT] = got_second[VIS:]
    unit_ref[3 * CUT_TXT :] = got_b[:CUT_TXT]
    grad_ref[:CUT_TXT] = own_text[CUT_TXT:]
    grad_ref[CUT_TXT : 3 * CUT_TXT] = mates_grad[...]
    grad_ref[3 * CUT_TXT :] = got_b[CUT_TXT:]
    bias = jnp.where(core_index() == 0, near_small[0:1].astype(f32), b_in[...].astype(f32))
    for slot in range(2):
        pltpu.make_async_copy(w_in, held.at[slot], sems.at[slot]).wait()
    row_pass(unit_ref[...], grad_ref[...], held.at[0], bias, held.at[1], act_ref, pre_ref, 0)
    back = times_transpose(pre_ref[...], held[0])
    out = matmul(act_ref[...], held[1])
    for piece, (target, base) in enumerate(((home_ref, 0), (mates_ref, 0), (mates_ref, 2 * CUT_TXT))):
        at = slice(piece * CUT_TXT, (piece + 1) * CUT_TXT)
        target[base : base + CUT_TXT] = back[at].astype(target.dtype)
        target[base + CUT_TXT : base + 2 * CUT_TXT] = out[at].astype(target.dtype)
    b_back[...] = back[3 * CUT_TXT :].astype(bf16)
    b_out[...] = out[3 * CUT_TXT :].astype(bf16)


def text_rows(*args):
    outs = [((2 * CUT_TXT, D), f32), ((4 * CUT_TXT, D), bf16)] + [((CUT_TXT, D), bf16)] * 2
    outs += [((4 * CUT_TXT, D), bf16)] * 4
    scratch = [pltpu.VMEM((2, D, D), bf16), pltpu.SemaphoreType.DMA((2,))]
    return call(text_kernel, outs, *args, scratch=scratch, any_from=7, micros=5, mebibytes=20)


class Outputs:
    def __init__(self, keep, away, blocks, sems):
        self.keep, self.away, self.blocks, self.sems, self.pending = keep, away, blocks, sems, []

    def put(self, index, value, kind):
        slot = len(self.pending) % 2
        if len(self.pending) >= 2:
            self.pending[-2].wait()
        self.blocks[slot] = value.astype(bf16)
        rows = pl.ds(index * D, D)
        kept = core_index() == kind

        @pl.when(kept)
        def _():
            pltpu.make_async_copy(self.blocks.at[slot], self.keep.at[rows], self.sems.at[slot]).start()

        @pl.when(jnp.logical_not(kept))
        def _():
            pltpu.make_async_copy(self.blocks.at[slot], self.away.at[rows], self.sems.at[slot]).start()

        self.pending.append(pltpu.make_async_copy(self.blocks.at[slot], self.keep.at[rows], self.sems.at[slot]))

    def finish(self):
        for copy in self.pending[-2:]:
            copy.wait()


def column_sum(value):
    return jnp.sum(value.astype(f32), axis=0, keepdims=True)


def near_grads_kernel(
    own_first, own_second, got_first, got_second, grad_own, grad_mate, act_own, act_mate, pre_own, pre_mate,
    unit_text, grad_text, act_text, pre_text, keep_ref, away_ref, units, grads, bias_ref, blocks, sems, acts, pres, in_sems,
):
    near = slice(0, D)
    loads = []

    def load(source, target):
        loads.append(pltpu.make_async_copy(source, target, in_sems.at[len(loads)]))
        loads[-1].start()

    for piece, source in enumerate((own_first, own_second, got_first, got_second)):
        load(source.at[:VIS], units.at[piece * VIS : (piece + 1) * VIS])
    for own, mate, total in ((pre_own, pre_mate, pres), (act_own, act_mate, acts)):
        load(own.at[:, near], total.at[:CUT])
        load(mate.at[:, near], total.at[CUT:])
    load(grad_own, grads.at[:CUT])
    load(grad_mate, grads.at[CUT:])
    outputs = Outputs(keep_ref, away_ref, blocks, sems)
    outputs.put(1, contract_rows(unit_text[...], pre_text[...]), 0)
    outputs.put(1, contract_rows(act_text[...], grad_text[...]), 1)
    for copy in loads[:6]:
        copy.wait()
    outputs.put(0, contract_rows(units[...], pres[...]), 0)
    for copy in loads[6:]:
        copy.wait()
    outputs.put(0, contract_rows(acts[...], grads[...]), 1)
    at_y = lax.axis_index("ffn")
    bias_ref[...] = jnp.zeros_like(bias_ref)
    bias_ref[pl.ds(at_y, 1)] = column_sum(pres[...])
    bias_ref[pl.ds(4 + at_y, 1)] = column_sum(pre_text[...])
    outputs.finish()


def far_grads_kernel(
    units, grads, act_own, act_mate, pre_own, pre_mate, bias_in, keep_ref, away_ref, bias_ref, blocks, sems, acts, pres, in_sems
):
    far = slice(D, 2 * D)
    loads = []
    for own, mate, total in ((pre_own, pre_mate, pres), (act_own, act_mate, acts)):
        for source, target in ((own, total.at[:CUT]), (mate, total.at[CUT:])):
            loads.append(pltpu.make_async_copy(source.at[:, far], target, in_sems.at[len(loads)]))
            loads[-1].start()
    outputs = Outputs(keep_ref, away_ref, blocks, sems)
    for copy in loads[:2]:
        copy.wait()
    outputs.put(0, contract_rows(units[...], pres[...]), 0)
    for copy in loads[2:]:
        copy.wait()
    outputs.put(0, contract_rows(acts[...], grads[...]), 1)
    bias_ref[...] = bias_in[...]
    bias_ref[pl.ds(lax.rem(lax.axis_index("ffn") + 2, 4), 1)] = column_sum(pres[...])
    outputs.finish()


def near_grads(*args):
    rows = jax.ShapeDtypeStruct((2 * CUT, D), bf16)
    return pl.pallas_call(
        near_grads_kernel,
        out_shape=[jax.ShapeDtypeStruct((2 * D, D), bf16)] * 2 + [rows, rows, jax.ShapeDtypeStruct((8, D), f32)],
        in_specs=[ANY] * 10 + [VMEM] * 4,
        out_specs=[ANY, ANY] + [VMEM] * 3,
        scratch_shapes=[pltpu.VMEM((2, D, D), bf16), pltpu.SemaphoreType.DMA((2,))]
        + [pltpu.VMEM((2 * CUT, D), bf16)] * 2
        + [pltpu.SemaphoreType.DMA((10,))],
        cost_estimate=cost(1),
        compiler_params=params(24),
    )(*args)


def far_grads(*args):
    return pl.pallas_call(
        far_grads_kernel,
        out_shape=[jax.ShapeDtypeStruct((D, D), bf16)] * 2 + [jax.ShapeDtypeStruct((8, D), f32)],
        in_specs=[VMEM] * 2 + [ANY] * 4 + [VMEM],
        out_specs=[ANY, ANY, VMEM],
        scratch_shapes=[pltpu.VMEM((2, D, D), bf16), pltpu.SemaphoreType.DMA((2,))]
        + [pltpu.VMEM((2 * CUT, D), bf16)] * 2
        + [pltpu.SemaphoreType.DMA((4,))],
        cost_estimate=cost(1),
        compiler_params=params(24),
    )(*args)


def text_sum(own_ref, got_first, got_second, b_ref, item):
    txt = slice(VIS + item * TXT, VIS + (item + 1) * TXT)
    total = own_ref[CUT + item * TXT : CUT + (item + 1) * TXT] + b_ref[item * TXT : (item + 1) * TXT].astype(f32)
    return total + got_first[txt].astype(f32) + got_second[txt].astype(f32)


def branch_kernel(
    own_ref, got_first, got_second, b_ref, modal_ref, cot_ref, hid_ref, att_ref, gain_ref, wo_ref,
    hidden_ref, gatt_ref, dwo_ref, sum_ref,
):
    gain = vector(gain_ref)
    sums = [0.0, 0.0, 0.0]
    for item in range(ITEMS):
        at = slice(item * SEQ, (item + 1) * SEQ)
        vis = slice(item * VIS, (item + 1) * VIS)
        vision = own_ref[vis] + (got_first, got_second)[item][:VIS].astype(f32)
        text = text_sum(own_ref, got_first, got_second, b_ref, item)
        grad_unit = unpack_item(vision, text, *slots_of(modal_ref[item : item + 1])).astype(bf16).astype(f32)
        _, hat, scaled = norm_forward(hid_ref[at], 1.0, 0.0)
        grad_norm, grad_gain, grad_shift = norm_backward(grad_unit, hat, scaled, gain)
        grad_hidden = cot_ref[at].astype(f32) + grad_norm
        hidden_ref[at] = grad_hidden
        branch = grad_hidden.astype(bf16)
        gatt_ref[at] = branch
        sums[0] += grad_gain
        sums[1] += grad_shift
        sums[2] += jnp.sum(branch.astype(f32), axis=0, keepdims=True)
    dwo_ref[...] = contract_rows(att_ref[...], gatt_ref[...]).astype(bf16)
    gatt_ref[...] = times_transpose(gatt_ref[...], wo_ref[...]).astype(bf16)
    sum_ref[...] = jnp.concatenate(sums, axis=0)


def scores_kernel(q_ref, k_ref, v_ref, p_ref, gatt_ref, gq_ref, gk_ref, gv_ref):
    low_half = lax.broadcasted_iota(jnp.int32, (1, 128), 1) < HEAD_DIM
    for pair in range(HEADS // 2):
        lanes = slice(pair * 128, (pair + 1) * 128)
        q, k, v, g = q_ref[:, lanes], k_ref[:, lanes], v_ref[:, lanes], gatt_ref[:, lanes]
        gq = gk = gv = 0.0
        for half in range(2):
            mine = low_half if half == 0 else jnp.logical_not(low_half)
            mask = lambda a: jnp.where(mine, a, 0).astype(bf16)
            low = p_ref[0, 2 * pair + half]
            probs = low.astype(f32)
            inner = times_transpose(mask(g), v) * probs
            scores = (inner - probs * jnp.sum(inner, axis=-1, keepdims=True)).astype(bf16)
            gv += contract_rows(low, mask(g))
            gq += matmul(scores, mask(k))
            gk += contract_rows(scores, mask(q))
        gq_ref[:, lanes] = (gq * 0.125).astype(bf16)
        gk_ref[:, lanes] = gk.astype(bf16)
        gv_ref[:, lanes] = gv.astype(bf16)


def backward_scores(q, k, v, p, gatt):
    block = pl.BlockSpec((SEQ, D), lambda i: (i, 0))
    heads = pl.BlockSpec((1, HEADS, SEQ, SEQ), lambda i: (i, 0, 0, 0))
    return pl.pallas_call(
        scores_kernel,
        grid=(ITEMS,),
        out_shape=[jax.ShapeDtypeStruct((ROWS, D), bf16)] * 3,
        in_specs=[block] * 3 + [heads, block],
        out_specs=[block] * 3,
        cost_estimate=cost(25),
        compiler_params=params(20),
    )(q, k, v, p, gatt)


def shared_kernel(
    tok_ref, gain1, shift1, gq_ref, gk_ref, gv_ref, wq_ref, wk_ref, wv_ref, hidden_ref, dwo_ref, sums_two, grad_live, bias_rows,
    tok_out, keep_ref, away_ref,
):
    gain = vector(gain1)
    unit, hat, scaled = norm_forward(tok_ref[...].astype(f32), gain, vector(shift1))
    low = unit.astype(bf16)
    dwq = contract_rows(low, gq_ref[...]).astype(bf16)
    dwk = contract_rows(low, gk_ref[...]).astype(bf16)
    dwv = contract_rows(low, gv_ref[...]).astype(bf16)
    back = times_transpose(gq_ref[...], wq_ref[...]) + times_transpose(gk_ref[...], wk_ref[...]) + times_transpose(gv_ref[...], wv_ref[...])
    grad_norm, grad_gain, grad_shift = norm_backward(back, hat, scaled, gain)
    tok_out[...] = (hidden_ref[...] + grad_norm).astype(bf16)
    total = lambda ref: jnp.sum(ref[...].astype(f32), axis=0, keepdims=True)
    rows = [grad_gain, grad_shift, total(gq_ref), total(gv_ref), sums_two[...], grad_live[...], bias_rows[...]]
    vec = jnp.concatenate(rows + [jnp.zeros((VEC - 17, D), f32)], axis=0).astype(bf16)

    def put(mine, other):
        mine[:D] = dwq
        mine[D : 2 * D] = dwk
        other[:D] = dwv
        other[D : 2 * D] = dwo_ref[...]
        mine[2 * D :] = vec
        other[2 * D :] = vec

    @pl.when(core_index() == 0)
    def _():
        put(keep_ref, away_ref)

    @pl.when(core_index() == 1)
    def _():
        put(away_ref, keep_ref)


def mixed_kernel(own_ref, got_first, got_second, b_ref, modal_ref, hid_ref, b_out, near_small, out_ref):
    first = core_index() == 0
    mine, other = b_out[...].astype(f32), near_small[1:2].astype(f32)
    bias_vision, bias_text = jnp.where(first, mine, other), jnp.where(first, other, mine)
    for item in range(ITEMS):
        at = slice(item * SEQ, (item + 1) * SEQ)
        vis = slice(item * VIS, (item + 1) * VIS)
        vision = own_ref[vis] + (got_first, got_second)[item][:VIS].astype(f32) + bias_vision
        text = text_sum(own_ref, got_first, got_second, b_ref, item) + bias_text
        rows = unpack_item(vision, text, *slots_of(modal_ref[item : item + 1])).astype(bf16).astype(f32)
        out_ref[at] = (hid_ref[at] + rows).astype(bf16)


def split_kernel(count, size, axes, *refs):
    ins, outs, total = refs[:count], refs[count:-1], refs[-1]
    extra = total.shape[0] - 4 * size
    total[...] = sum(ref[: 4 * size + extra].astype(f32) for ref in ins).astype(bf16)
    me = place(axes)
    for step, out in zip((0, 1, 3, 2), outs):
        at = pl.multiple_of(lax.rem(me + step, 4) * size, 16)
        out[:size] = total[pl.ds(at, size)]
        if extra:
            out[size:] = total[4 * size :]


def split(pieces, size, extra, axes):
    outs = [((size + extra, D), bf16)] * 4
    scratch = [pltpu.VMEM((4 * size + extra, D), bf16)]
    return call(functools.partial(split_kernel, len(pieces), size, axes), outs, *pieces, scratch=scratch)


def block_steps(size):
    first = core_index() == 0
    return jnp.where(first, 4 * size, size), jnp.where(first, size, 4 * size)


def expert_split_kernel(size, near_keep, near_got, far_keep, far_got, *refs):
    outs, total = refs[:-1], refs[-1]
    near = (near_keep[...].astype(f32) + near_got[...].astype(f32)).astype(bf16)
    total[:D] = near[:D]
    total[D : 2 * D] = (far_keep[...].astype(f32) + far_got[...].astype(f32)).astype(bf16)
    total[2 * D :] = near[D:]
    me = place("xz")
    outer, inner = block_steps(size)
    half = 6 * size
    for step in (0, 1, 3, 2):
        base = lax.rem(me + step, 4) * outer
        for matrix in range(3):
            for block in range(4):
                rows = total[pl.ds(pl.multiple_of(base + matrix * D + block * inner, 16), size)]
                to = (matrix * 4 + block) * size
                if step == 2:
                    out, to = (outs[1], 2 * half + to) if to < half else (outs[2], half + to)
                else:
                    out = outs[{0: 0, 1: 1, 3: 2}[step]]
                out[to : to + size] = rows


EXP = D // 16


def expert_second_kernel(mine, below, above, below_half, above_half, *refs):
    outs, total = refs[:-1], refs[-1]
    size = mine.shape[0]
    for at, far in ((slice(0, size // 2), below_half), (slice(size // 2, size), above_half)):
        total[at] = (mine[at].astype(f32) + below[at].astype(f32) + above[at].astype(f32) + far[...].astype(f32)).astype(bf16)
    me = place("zx")
    for step, out in zip((0, 1, 3, 2), outs):
        index = lax.rem(me + step, 4)
        for matrix in range(3):
            at = pl.multiple_of((matrix * 4 + index) * EXP, 16)
            out[matrix * EXP : (matrix + 1) * EXP] = total[pl.ds(at, EXP)]


def expert_third_kernel(*refs):
    ins, outs = refs[:4], refs[4:]
    total = sum(ref[...].astype(f32) for ref in ins).astype(bf16)
    for matrix, out in enumerate(outs):
        out[...] = total[matrix * EXP : (matrix + 1) * EXP]


def expert_keep_kernel(near, far, text, keep, away):
    first = core_index() == 0
    vision, language = near[...].astype(f32) + far[...].astype(f32), text[...].astype(f32)
    keep[...] = jnp.where(first, vision, language).astype(bf16)
    away[...] = jnp.where(first, language, vision).astype(bf16)


def sum_kernel(*refs):
    ins, out = refs[:4], refs[4]
    out[...] = sum(ref[...].astype(f32) for ref in ins).astype(bf16)


def fourth_kernel(*refs):
    ins, (keep, got, out, vec) = refs[:4], refs[4:]
    total = sum(ref[...].astype(f32) for ref in ins)
    out[: 2 * EXP] = total[: 2 * EXP].astype(bf16)
    vec[...] = total[2 * EXP :]
    first = core_index() == 0
    k, g = keep[...].astype(f32), got[...].astype(f32)
    out[2 * EXP : 3 * EXP] = jnp.where(first, k, g).astype(bf16)
    out[3 * EXP :] = jnp.where(first, g, k).astype(bf16)


def fifth_kernel(mine, first, third, second, shared, expert):
    me = place("xz")
    for step, piece in zip((0, 1, 3, 2), (mine, first, third, second)):
        index = lax.rem(me + 4 - step, 4)
        shared[pl.ds(pl.multiple_of(index * 2 * EXP, 16), 2 * EXP)] = piece[: 2 * EXP]
        at = pl.multiple_of(index * EXP, 16)
        expert[pl.ds(at, EXP)] = piece[2 * EXP : 3 * EXP]
        expert[pl.ds(4 * EXP + at, EXP)] = piece[3 * EXP :]


def expert_finish_kernel(mine, first, third, second, w_in, w_out):
    outer, inner = block_steps(EXP)
    me = place("zx")
    for step, piece in zip((0, 1, 3, 2), (mine, first, third, second)):
        base = lax.rem(me + 4 - step, 4) * inner
        for block in range(4):
            at = pl.ds(pl.multiple_of(base + block * outer, 16), EXP)
            w_in[at] = piece[block * EXP : (block + 1) * EXP].astype(f32)
            w_out[at] = piece[(4 + block) * EXP : (5 + block) * EXP].astype(f32)


def join_kernel(axes, *refs):
    ins, out = refs[:4], refs[4]
    size = out.shape[0] // 4
    me = place(axes)
    for step, piece in zip((0, 1, 3, 2), ins):
        at = pl.multiple_of(lax.rem(me + 4 - step, 4) * size, 16)
        out[pl.ds(at, size)] = piece[:size]


def join(piece, got, axes, size=None):
    return call(functools.partial(join_kernel, axes), [((4 * (size or piece.shape[0]), D), bf16)], piece, *got)[0]


def finish_kernel(mine, other, vec, wq, wk, wv, wo, g1, s1, bq, bv, g2, s2, bo, b_in, b_out):
    first = core_index() == 0
    for low, high, at in ((wq, wv, 0), (wk, wo, 1)):
        m, o = mine[at].astype(f32), other[at].astype(f32)
        low[...] = jnp.where(first, m, o)
        high[...] = jnp.where(first, o, m)

    @pl.when(pl.program_id(0) == 0)
    def _():
        for ref, row in ((g1, 0), (s1, 1), (bq, 2), (bv, 3), (g2, 4), (s2, 5), (bo, 6)):
            ref[...] = vec[row]
        b_in[...] = vec[pl.ds(9 + 4 * core_index() + lax.axis_index("ffn"), 1)]
        b_out[...] = vec[pl.ds(7 + core_index(), 1)]


def finish(mine, other, vec):
    steps = 4
    size = D // steps
    pair = pl.BlockSpec((2, size, D), lambda i: (0, i, 0))
    block = pl.BlockSpec((size, D), lambda i: (i, 0))
    return pl.pallas_call(
        finish_kernel,
        grid=(steps,),
        out_shape=[jax.ShapeDtypeStruct((D, D), f32)] * 4
        + [jax.ShapeDtypeStruct((D,), f32)] * 7
        + [jax.ShapeDtypeStruct((1, D), f32)] * 2,
        in_specs=[pair, pair, VMEM],
        out_specs=[block] * 4 + [VMEM] * 9,
        cost_estimate=cost(5),
        compiler_params=params(12),
    )(mine.reshape(2, D, D), other.reshape(2, D, D), vec)


def body(
    tokens,
    cotangent,
    modality,
    ln1_gain,
    ln1_shift,
    w_query,
    b_query,
    w_key,
    w_value,
    b_value,
    w_attn_out,
    b_attn_out,
    ln2_gain,
    ln2_shift,
    w_in,
    b_in,
    w_out,
    b_out,
):
    flat_tokens = tokens.reshape(ROWS, D)
    flat_cot = cotangent.reshape(ROWS, D)
    w_in, w_out = w_in[0], w_out[0]

    part_in, part_out, cot_first, cot_second, small, grad_text = parts(w_in, w_out, flat_cot, b_in, b_out, modality)
    part_in = send(part_in, lambda x, z, c, y: (x, z, 0, (y + 2) % 4) if c == 0 else None)
    part_out = send(part_out, lambda x, z, c, y: (x, z, 1, (y + 2) % 4) if c == 0 else None)

    cot_first, cot_second = swap_pair(cot_first), swap_other(cot_second)

    vectors = (ln1_gain, ln1_shift, b_query, b_value, b_attn_out, ln2_gain, ln2_shift)
    query, key, value, probs, attended, hidden_one, own_first, own_second, text_own = forward_attention(
        flat_tokens, modality, vectors, (w_query, w_key, w_value, w_attn_out), grad_text
    )
    sent_first, sent_second, text_own = tie((own_first, own_second, text_own), cot_first, cot_second)
    got_first, got_second, got_b = swap_pair(sent_first), swap_other(sent_second), swap_far(text_own)
    near_in, near_out = swap_core(tie(w_in, own_first)), swap_core(tie(w_out, own_first))
    far_part = jnp.where(core_index() == 0, *tie((part_in, part_out), own_first))
    far_got = shifts([far_part] * 3, "xz")
    near_small = swap_core(tie(small, far_got[2]))
    grad_own, grad_live = call(pack_kernel, [((CUT, D), bf16), ((2, D), f32)], tie(flat_cot, own_first), modality, micros=2)
    grad_mate, text_mate = call(pack_mates_kernel, [((CUT, D), bf16), ((2 * CUT_TXT, D), bf16)], cot_first, tie(cot_second, own_first))
    far_got = tie(far_got, got_first, got_second, got_b, near_small, grad_own, grad_mate)
    far_mine = join(far_part, far_got, "xz", D // 4)
    far_other = swap_core(far_mine)

    text_weights = (w_in, w_out, near_in, near_out)
    vision_weights = text_weights + (far_mine, far_other)
    text_home, text_mates, text_back, text_out, units_text, grads_text, text_act, text_pre = text_rows(
        text_own, got_first, got_second, got_b, text_mate, b_in, near_small, *text_weights
    )
    got_text = swap_far(text_back)
    smalls = (b_in, far_part, near_small)
    back_first, back_second, out_first, out_second, mate_act, mate_pre = vision_rows(
        True, (got_first, got_second), grad_mate, text_mates, smalls, vision_weights
    )
    back_first, back_second = swap_pair(back_first), swap_other(back_second)
    own_back, own_out, own_act, own_pre = vision_rows(
        False, (own_first, own_second), tie(grad_own, grad_mate, mate_act), text_home, smalls, vision_weights
    )

    near_keep, near_away, units, grads, bias_rows = near_grads(
        own_first, own_second, got_first, got_second, grad_own, grad_mate, own_act, mate_act, own_pre, mate_pre,
        units_text, grads_text, text_act, text_pre,
    )
    far_keep, far_away, bias_rows = far_grads(units, grads, own_act, mate_act, own_pre, mate_pre, bias_rows)
    near_away_got = swap_core(tie(near_away, back_first, back_second, got_text))

    grad_hidden, grad_attended, grad_w_attn_out, sums_two = call(
        branch_kernel,
        [((ROWS, D), f32), ((ROWS, D), bf16), ((D, D), bf16), ((3, D), f32)],
        own_back, tie(back_first, far_keep), back_second, got_text, modality, flat_cot, hidden_one, attended, ln2_gain, w_attn_out,
        micros=100, mebibytes=20,
    )
    far_away_got = swap_core(tie(far_away, back_first, back_second, got_text))
    out_first, out_second = tie((out_first, out_second), back_first, back_second)
    out_first, out_second = swap_pair(out_first), swap_other(out_second)
    expert_pieces = call(
        functools.partial(expert_split_kernel, EXP),
        [((12 * EXP, D), bf16)] + [((18 * EXP, D), bf16)] * 2,
        near_keep, near_away_got, far_keep, tie(far_away_got, grad_attended),
        scratch=[pltpu.VMEM((3 * D, D), bf16)], micros=2, mebibytes=20,
    )
    expert_got = [shift(piece, "xz", step) for piece, step in zip(expert_pieces[1:], (1, 3))]
    grad_query, grad_key, grad_value = backward_scores(query, key, value, probs, tie(grad_attended, *expert_pieces))
    grad_tokens, shared_keep, shared_away = call(
        shared_kernel,
        [((ROWS, D), bf16)] + [((2 * D + VEC, D), bf16)] * 2,
        flat_tokens, ln1_gain, ln1_shift, grad_query, grad_key, grad_value, w_query, w_key, w_value,
        grad_hidden, grad_w_attn_out, sums_two, grad_live, bias_rows,
        micros=11, mebibytes=28,
    )

    expert_relay = [shift(piece[12 * EXP :], "xz", step) for piece, step in zip(expert_got, (1, 3))]
    shared_got = swap_core(tie(shared_away, *expert_got, out_first, out_second))
    shared_pieces = split([shared_keep, shared_got], 2 * D // 4, VEC, "yx")
    shared_got = shifts(shared_pieces[1:], "yx")
    expert_pieces = call(
        expert_second_kernel,
        [((3 * EXP, D), bf16)] * 4,
        expert_pieces[0], *tie(expert_got, *shared_pieces), *expert_relay,
        scratch=[pltpu.VMEM((12 * EXP, D), bf16)],
    )
    expert_got = shifts(expert_pieces[1:], "zx")
    shared_pieces = split([shared_pieces[0]] + tie(shared_got, *expert_got[:2]), 2 * EXP, VEC, "xz")
    shared_got = shifts(shared_pieces[1:], "xz")
    near, far, text = call(expert_third_kernel, [((EXP, D), bf16)] * 3, expert_pieces[0], *expert_got)
    far = swap_far(far)
    size = 2 * EXP + VEC
    (shared_total,) = call(sum_kernel, [((size, D), bf16)], shared_pieces[0], *tie(shared_got, far))
    shared_got = shifts([shared_total] * 3, "zy")
    expert_keep, expert_away = call(expert_keep_kernel, [((EXP, D), bf16)] * 2, near, far, text)
    low, vec = call(
        fourth_kernel,
        [((4 * EXP, D), bf16), ((VEC, D), f32)],
        shared_total, *shared_got, expert_keep, swap_core(expert_away),
    )
    got_text_out = swap_far(tie(text_out, low))
    shared_sum, expert_sum = call(
        fifth_kernel, [((8 * EXP, D), bf16)] * 2, low, *shifts([low] * 3, "xz")
    )
    shared_got = shifts([shared_sum] * 3, "yx")
    expert_got = shifts([expert_sum] * 3, "zx")
    shared_sum = join(shared_sum, shared_got, "yx")
    shared_sum = tie(shared_sum, expert_got[0], expert_got[1])
    outs = finish(shared_sum, swap_core(shared_sum), vec)
    d_query, d_key, d_value, d_out, d_gain1, d_shift1, d_bq, d_bv, d_gain2, d_shift2, d_bo, d_b_in, d_b_out = outs
    grad_w_in, grad_w_out = call(expert_finish_kernel, [((D, D), f32)] * 2, tie(expert_sum, d_query), *expert_got)
    (mixed,) = call(
        mixed_kernel,
        [((ROWS, D), bf16)],
        tie(own_out, d_query), out_first, out_second, got_text_out, modality, hidden_one, b_out, near_small,
        micros=4, mebibytes=16,
    )
    return (
        mixed.reshape(tokens.shape),
        grad_tokens.reshape(tokens.shape),
        d_gain1,
        d_shift1,
        d_query,
        d_bq,
        d_key,
        d_value,
        d_bv,
        d_out,
        d_bo,
        d_gain2,
        d_shift2,
        grad_w_in[None],
        d_b_in,
        grad_w_out[None],
        d_b_out,
    )


def solution(mesh):
    items = P(AXES, None, None)
    expert_specs = (P("expert", None, "ffn"), P("expert", "ffn"), P("expert", "ffn", None), P("expert", None))
    return jax.shard_map(
        body,
        mesh=mesh,
        in_specs=(items, items, P(AXES, None)) + (P(),) * 11 + expert_specs,
        out_specs=(items, items) + (P(),) * 11 + expert_specs,
        check_vma=False,
    )
```

```python
import functools

import jax
import jax.numpy as jnp
from jax import lax
from jax.experimental import pallas as pl
from jax.experimental.pallas import tpu as pltpu
from jax.sharding import PartitionSpec as P

D = 768
HEAD_DIM = 64
HEADS = D // HEAD_DIM
PATCHES = 197
SEQ = 256
ITEMS = 2
ROWS = ITEMS * SEQ
TEXT_AT = 192
VIS = 208
TXT = 48
CUT = ITEMS * VIS
CUT_TXT = ITEMS * TXT
BACK = VIS + CUT_TXT
COT = SEQ + TXT + 16
VEC = 24

epsilon = 1e-05
root_half = 0.7071067811865476
inv_root_tau = 0.3989422804014327
AXES = ("dp", "expert", "ffn")
bf16 = jnp.bfloat16
f32 = jnp.float32


def split_index(index):
    return index // 32, index // 8 % 4, index // 4 % 2, index % 4


def join_index(x, z, core, y):
    return ((x * 4 + z) * 2 + core) * 4 + y


def send(value, where):
    pairs = []
    for index in range(128):
        target = where(*split_index(index))
        if target is not None:
            pairs.append((index, join_index(*target)))
    return lax.ppermute(value, AXES, pairs)


def swap_core(value):
    return send(value, lambda x, z, c, y: (x, z, 1 - c, y))


def swap_pair(value):
    return send(value, lambda x, z, c, y: (x, z, c, y ^ 1))


def swap_other(value):
    return send(value, lambda x, z, c, y: (x, z, c, 3 - y))


def swap_far(value):
    return send(value, lambda x, z, c, y: (x, z, c, y ^ 2))


def shift(value, axes, step):
    def where(x, z, c, y):
        at = dict(x=x, z=z, y=y)
        at[axes[c]] = (at[axes[c]] + step) % 4
        return at["x"], at["z"], c, at["y"]

    return send(value, where)


def shifts(pieces, axes):
    return [shift(piece, axes, step) for piece, step in zip(pieces, (1, 3, 2))]


def tie(value, *others):
    return lax.optimization_barrier((value, others))[0]


def core_index():
    return lax.axis_index("expert")


def place(axes):
    dp = lax.axis_index("dp")
    at = dict(x=dp // 4, z=dp % 4, y=lax.axis_index("ffn"))
    return jnp.where(core_index() == 0, at[axes[0]], at[axes[1]])


def norm_forward(values, gain_vec, shift_vec):
    centre = values - jnp.mean(values, axis=-1, keepdims=True)
    scaled = lax.rsqrt(jnp.mean(centre * centre, axis=-1, keepdims=True) + epsilon)
    normal_hat = centre * scaled
    return (normal_hat * gain_vec + shift_vec, normal_hat, scaled)


def norm_backward(grad_result, normal_hat, scaled, gain_vec):
    grad_hat = grad_result * gain_vec
    inner_term = (
        grad_hat
        - jnp.mean(grad_hat, axis=-1, keepdims=True)
        - normal_hat * jnp.mean(grad_hat * normal_hat, axis=-1, keepdims=True)
    )
    return (
        scaled * inner_term,
        jnp.sum(grad_result * normal_hat, axis=0, keepdims=True),
        jnp.sum(grad_result, axis=0, keepdims=True),
    )


def matmul(first_op, second_op):
    return jnp.dot(first_op, second_op, preferred_element_type=f32)


def contract_rows(first_op, second_op):
    return lax.dot_general(first_op, second_op, (((0,), (0,)), ((), ())), preferred_element_type=f32)


def times_transpose(first_op, second_op):
    return lax.dot_general(first_op, second_op, (((1,), (1,)), ((), ())), preferred_element_type=f32)


def vector(ref):
    return ref[...].astype(f32).reshape(1, D)


def slots_of(row):
    has_image = jnp.max(jnp.where(row == 0, 1.0, 0.0), axis=1, keepdims=True)
    texts = jnp.sum(jnp.where(row == 1, 1.0, 0.0), axis=1, keepdims=True)
    start = has_image * PATCHES
    slot = lax.broadcasted_iota(jnp.int32, (SEQ, 1), 0).astype(f32)
    modal = jnp.where(slot < start, 0.0, jnp.where(slot < start + texts, 1.0, 2.0))
    return has_image > 0.5, modal


def text_of(rows, has_image, modal):
    at = slice(TEXT_AT, TEXT_AT + TXT)
    return jnp.where(has_image, jnp.where(modal[at] == 1, rows[at], 0.0), jnp.where(modal[:TXT] == 1, rows[:TXT], 0.0))


def unpack_item(vision, text, has_image, modal):
    whole = jnp.concatenate(
        [
            jnp.where(has_image, vision[:TXT], text),
            vision[TXT:TEXT_AT],
            jnp.where(modal[TEXT_AT:VIS] == 1, text[: VIS - TEXT_AT], vision[TEXT_AT:]),
            text[VIS - TEXT_AT :],
            jnp.zeros((SEQ - TEXT_AT - TXT, D), f32),
        ],
        axis=0,
    )
    return jnp.where(modal < 2, whole, 0.0)


VMEM = pl.BlockSpec(memory_space=pltpu.VMEM)
ANY = pl.BlockSpec(memory_space=pl.ANY)


def cost(micros):
    return pl.CostEstimate(flops=0, bytes_accessed=int(micros * 1e5), transcendentals=0)


def params(mebibytes):
    return pltpu.CompilerParams(vmem_limit_bytes=mebibytes * 1024 * 1024)


def call(kernel, outs, *args, scratch=(), any_from=None, micros=1.5, mebibytes=12):
    specs = [VMEM] * len(args) if any_from is None else [VMEM] * any_from + [ANY] * (len(args) - any_from)
    return pl.pallas_call(
        kernel,
        out_shape=[jax.ShapeDtypeStruct(shape, dtype) for shape, dtype in outs],
        in_specs=specs,
        out_specs=[VMEM] * len(outs),
        scratch_shapes=list(scratch),
        cost_estimate=cost(micros),
        compiler_params=params(mebibytes),
    )(*args)


def pack_kernel(grad_ref, modal_ref, out_ref, sum_ref):
    sums = [0.0, 0.0]
    for item in range(ITEMS):
        has_image, modal = slots_of(modal_ref[item : item + 1])
        grad = grad_ref[item * SEQ : (item + 1) * SEQ].astype(f32)
        vision = jnp.where(modal[:VIS] == 0, grad[:VIS], 0.0)
        out_ref[item * VIS : (item + 1) * VIS] = vision.astype(bf16)
        sums[0] += jnp.sum(vision, axis=0, keepdims=True)
        sums[1] += jnp.sum(text_of(grad, has_image, modal), axis=0, keepdims=True)
    sum_ref[...] = jnp.concatenate(sums, axis=0)


def part_kernel(w_in, w_out, grad, b_in, b_out, modal_ref, in_ref, out_ref, first_ref, second_ref, small_ref, text_ref, sems):
    dp, share = lax.axis_index("dp"), D // 4
    x, z = lax.div(dp, 4), lax.rem(dp, 4)
    copies = [
        pltpu.make_async_copy(w_in.at[pl.ds(pl.multiple_of(x * share, 16), share)], in_ref.at[:share], sems.at[0]),
        pltpu.make_async_copy(w_out.at[pl.ds(pl.multiple_of(z * share, 16), share)], out_ref.at[:share], sems.at[1]),
        pltpu.make_async_copy(grad.at[:SEQ], first_ref.at[:SEQ], sems.at[2]),
        pltpu.make_async_copy(grad.at[SEQ:], second_ref.at[:SEQ], sems.at[3]),
    ]
    for copy in copies:
        copy.start()
    small = [b_in[...].astype(f32), b_out[...].astype(f32), jnp.zeros((14, D), f32)]
    small = jnp.concatenate(small, axis=0).astype(bf16)
    small_ref[...] = small
    modal = jnp.concatenate([modal_ref[...].astype(f32), jnp.zeros((16 - ITEMS, SEQ), f32)], axis=0)
    modal = jnp.concatenate([modal, jnp.zeros((16, D - SEQ), f32)], axis=1).astype(bf16)
    first_ref[SEQ + TXT :] = modal
    second_ref[SEQ + TXT :] = modal
    in_ref[share:] = small
    out_ref[share:] = small
    for copy in copies:
        copy.wait()
    for item, source, target in ((0, first_ref, second_ref), (1, second_ref, first_ref)):
        text = text_of(source[:SEQ].astype(f32), *slots_of(modal_ref[item : item + 1]))
        target[SEQ : SEQ + TXT] = text.astype(bf16)
        text_ref[item * TXT : (item + 1) * TXT] = text.astype(bf16)


def parts(*args):
    return pl.pallas_call(
        part_kernel,
        out_shape=[jax.ShapeDtypeStruct((D // 4 + 16, D), bf16)] * 2 + [jax.ShapeDtypeStruct((COT, D), bf16)] * 2
        + [jax.ShapeDtypeStruct((16, D), bf16), jax.ShapeDtypeStruct((CUT_TXT, D), bf16)],
        in_specs=[ANY] * 3 + [VMEM] * 3,
        out_specs=[VMEM] * 6,
        scratch_shapes=[pltpu.SemaphoreType.DMA((4,))],
        cost_estimate=cost(1),
        compiler_params=params(60),
    )(*args)


def forward_kernel(
    tok_ref, modal_ref, gain1, shift1, b_query, b_value, b_out, gain2, shift2, wq_ref, wk_ref, wv_ref, wo_ref,
    grad_text, q_out, k_out, v_out, p_out, att_out, hid_out, first_out, second_out, text_out,
    held, sems, q_all, k_all, v_all, p_all, att_all, hid_all, out_sems, first_ref, second_ref, text_ref, sent_sems,
):
    item = pl.program_id(0)
    pieces = 4
    rows = D // pieces

    def weight_copy(i, piece):
        at = pl.ds(piece * rows, rows)
        return pltpu.make_async_copy((wq_ref, wk_ref, wv_ref, wo_ref)[i].at[at], held.at[i, at], sems.at[i, piece])

    def start_weight(i):
        @pl.when(item == 0)
        def _():
            for piece in range(pieces):
                weight_copy(i, piece).start()

    def wait_weight(i):
        @pl.when(item == 0)
        def _():
            for piece in range(pieces):
                weight_copy(i, piece).wait()

    start_weight(0)

    @pl.when(item == 0)
    def _():
        text_ref[CUT_TXT:] = grad_text[...]

    outs = [(q_all, q_out), (k_all, k_out), (v_all, v_out), (p_all, p_out), (att_all, att_out), (hid_all, hid_out)]

    def copy_out(i, at):
        return pltpu.make_async_copy(outs[i][0].at[at], outs[i][1].at[at], out_sems.at[at, i])

    sent = [
        (first_ref.at[:VIS], first_out.at[:VIS]),
        (second_ref.at[:VIS], second_out.at[:VIS]),
        (first_ref.at[VIS:], first_out.at[VIS:]),
        (second_ref.at[VIS:], second_out.at[VIS:]),
        (text_ref, text_out),
    ]
    sent = [pltpu.make_async_copy(source, target, sent_sems.at[i]) for i, (source, target) in enumerate(sent)]

    q_ref, k_ref, v_ref, p_ref, att_ref = (ref.at[item] for ref in (q_all, k_all, v_all, p_all, att_all))
    x = tok_ref[...].astype(f32)
    unit, _, _ = norm_forward(x, vector(gain1), vector(shift1))
    unit = unit.astype(bf16)
    start_weight(1)
    wait_weight(0)
    q_ref[...] = ((matmul(unit, held[0]) + vector(b_query)).astype(bf16) * 0.125).astype(bf16)
    copy_out(0, item).start()
    start_weight(2)
    wait_weight(1)
    k_ref[...] = matmul(unit, held[1]).astype(bf16)
    copy_out(1, item).start()
    start_weight(3)
    wait_weight(2)
    v_ref[...] = (matmul(unit, held[2]) + vector(b_value)).astype(bf16)
    copy_out(2, item).start()
    row = modal_ref[pl.ds(item, 1)]
    bias = jnp.where(row < 2, 0.0, -1e30)
    low_half = lax.broadcasted_iota(jnp.int32, (1, 128), 1) < HEAD_DIM
    ones = jnp.ones((SEQ, 128), bf16)
    for pair in range(HEADS // 2):
        lanes = slice(pair * 128, (pair + 1) * 128)
        q, k, v = q_ref[:, lanes], k_ref[:, lanes], v_ref[:, lanes]
        halves = []
        for half in range(2):
            mine = low_half if half == 0 else jnp.logical_not(low_half)
            scores = times_transpose(jnp.where(mine, q, 0).astype(bf16), k) + bias
            scores = jnp.exp(scores - jnp.max(scores, axis=-1, keepdims=True))
            both = matmul(scores.astype(bf16), jnp.concatenate([v, ones], axis=1))
            inverse = 1.0 / both[:, 128:]
            p_ref[2 * pair + half] = (scores * jnp.concatenate([inverse, inverse], axis=1)).astype(bf16)
            halves.append(both[:, :128] * inverse)
        att_ref[:, lanes] = jnp.where(low_half, halves[0], halves[1]).astype(bf16)
    copy_out(3, item).start()
    copy_out(4, item).start()
    wait_weight(3)
    hidden = x + matmul(att_ref[...], held[3]) + vector(b_out)
    hid_all[item] = hidden
    copy_out(5, item).start()
    unit, _, _ = norm_forward(hidden, vector(gain2), vector(shift2))
    has_image, _ = slots_of(row)
    vision = unit[:VIS].astype(bf16)
    text = jnp.where(has_image, unit[TEXT_AT : TEXT_AT + TXT], unit[:TXT]).astype(bf16)
    text_ref[pl.ds(pl.multiple_of(item * TXT, 16), TXT)] = text
    first_ref[pl.ds(pl.multiple_of(VIS + item * TXT, 16), TXT)] = text
    second_ref[pl.ds(pl.multiple_of(VIS + item * TXT, 16), TXT)] = text

    @pl.when(item == 0)
    def _():
        first_ref[:VIS] = vision
        sent[0].start()

    @pl.when(item == 1)
    def _():
        second_ref[:VIS] = vision
        for copy in sent[1:]:
            copy.start()
        for at in range(ITEMS):
            for i in range(len(outs)):
                copy_out(i, at).wait()
        for copy in sent:
            copy.wait()


def forward_attention(tokens, modality, vectors, weights, *rest):
    block = pl.BlockSpec((SEQ, D), lambda i: (i, 0))
    shapes = [((ITEMS, SEQ, D), bf16)] * 3 + [((ITEMS, HEADS, SEQ, SEQ), bf16), ((ITEMS, SEQ, D), bf16), ((ITEMS, SEQ, D), f32)]
    sent = [((BACK, D), bf16), ((BACK, D), bf16), ((2 * CUT_TXT, D), bf16)]
    outs = pl.pallas_call(
        forward_kernel,
        grid=(ITEMS,),
        out_shape=[jax.ShapeDtypeStruct(*s) for s in shapes + sent],
        in_specs=[block] + [VMEM] * 8 + [ANY] * 4 + [VMEM],
        out_specs=[ANY] * 9,
        scratch_shapes=[pltpu.VMEM((4, D, D), bf16), pltpu.SemaphoreType.DMA((4, 4))]
        + [pltpu.VMEM(*s) for s in shapes]
        + [pltpu.SemaphoreType.DMA((ITEMS, 6))]
        + [pltpu.VMEM(*s) for s in sent]
        + [pltpu.SemaphoreType.DMA((5,))],
        cost_estimate=cost(10),
        compiler_params=params(56),
    )(tokens, modality, *vectors, *weights, *rest)
    flat = [out.reshape(ROWS, D) for out in outs[:3]]
    return flat + [outs[3], outs[4].reshape(ROWS, D), outs[5].reshape(ROWS, D)] + list(outs[6:])


def fetch(first, second, buffer, sem):
    @pl.when(core_index() == 0)
    def _():
        pltpu.make_async_copy(first, buffer, sem).start()

    @pl.when(core_index() == 1)
    def _():
        pltpu.make_async_copy(second, buffer, sem).start()


def row_pass(unit, grad, first, bias, second, act_ref, pre_ref, base):
    for at in range(0, D, 256):
        cols = slice(at, at + 256)
        kept = slice(base + at, base + at + 256)
        pre_act = matmul(unit, first[:, cols]) + bias[:, cols]
        cdf = 0.5 + 0.5 * lax.erf(pre_act * root_half)
        act_ref[:, kept] = (pre_act * cdf).astype(bf16)
        slope = cdf + pre_act * (jnp.exp(-0.5 * pre_act * pre_act) * inv_root_tau)
        pre_ref[:, kept] = (times_transpose(grad, second[cols, :]) * slope).astype(bf16)


def vision_kernel(
    mates, first_unit, second_unit, grad_ref, text_ref, b_in, far_part, near_small,
    w_in, w_out, near_in, near_out, far_mine, far_other, *refs,
):
    outs, (act_ref, pre_ref, held, sems, units) = refs[:-5], refs[-5:]
    fetch(w_in, near_in, held.at[0], sems.at[0])
    fetch(w_out, near_out, held.at[1], sems.at[1])
    fetch(far_mine, far_other, held.at[2], sems.at[2])
    fetch(far_other, far_mine, held.at[3], sems.at[3])
    first = core_index() == 0
    biases = (
        jnp.where(first, b_in[...].astype(f32), near_small[0:1].astype(f32)),
        far_part[D // 4 : D // 4 + 1].astype(f32),
    )
    units[:VIS] = first_unit[:VIS]
    units[VIS:] = second_unit[:VIS]
    unit, grad = units[...], grad_ref[...]
    for part in range(2):
        for slot in (2 * part, 2 * part + 1):
            pltpu.make_async_copy(w_in, held.at[slot], sems.at[slot]).wait()
        row_pass(unit, grad, held.at[2 * part], biases[part], held.at[2 * part + 1], act_ref, pre_ref, part * D)
    back = times_transpose(pre_ref[:, :D], held[0]) + times_transpose(pre_ref[:, D:], held[2])
    out = matmul(act_ref[:, :D], held[1]) + matmul(act_ref[:, D:], held[3])
    if mates:
        for item in range(2):
            at = slice(item * VIS, (item + 1) * VIS)
            outs[item][:VIS] = back[at].astype(bf16)
            outs[item][VIS:] = text_ref[2 * item * CUT_TXT : (2 * item + 1) * CUT_TXT]
            outs[2 + item][:VIS] = out[at].astype(bf16)
            outs[2 + item][VIS:] = text_ref[(2 * item + 1) * CUT_TXT : (2 * item + 2) * CUT_TXT]
    else:
        outs[0][:CUT] = back
        outs[0][CUT:] = text_ref[:CUT_TXT]
        outs[1][:CUT] = out
        outs[1][CUT:] = text_ref[CUT_TXT:]


def vision_rows(mates, units, grad, text, smalls, weights):
    outs = [((BACK, D), bf16)] * 4 if mates else [((ROWS, D), f32)] * 2
    outs += [((CUT, 2 * D), bf16)] * 2
    scratch = [pltpu.VMEM((4, D, D), bf16), pltpu.SemaphoreType.DMA((4,)), pltpu.VMEM((CUT, D), bf16)]
    kernel = functools.partial(vision_kernel, mates)
    return call(kernel, outs, *units, grad, text, *smalls, *weights, scratch=scratch, any_from=7, micros=3, mebibytes=28)


def pack_mates_kernel(cot_first, cot_second, grad_ref, text_ref):
    for item, cot in ((0, cot_first), (1, cot_second)):
        modality = cot[SEQ + TXT :, :SEQ].astype(f32)
        has_image, modal = slots_of(modality[item : item + 1])
        grad = cot[:SEQ].astype(f32)
        grad_ref[item * VIS : (item + 1) * VIS] = jnp.where(modal[:VIS] == 0, grad[:VIS], 0.0).astype(bf16)
        at = item * CUT_TXT
        here, there = at + item * TXT, at + (1 - item) * TXT
        text_ref[here : here + TXT] = text_of(grad, has_image, modal).astype(bf16)
        text_ref[there : there + TXT] = cot[SEQ : SEQ + TXT]


def text_kernel(
    own_text, got_first, got_second, got_b, mates_grad, b_in, near_small, w_in, w_out, near_in, near_out,
    home_ref, mates_ref, b_back, b_out, unit_ref, grad_ref, act_ref, pre_ref, held, sems,
):
    fetch(near_in, w_in, held.at[0], sems.at[0])
    fetch(near_out, w_out, held.at[1], sems.at[1])
    unit_ref[:CUT_TXT] = own_text[:CUT_TXT]
    unit_ref[CUT_TXT : 2 * CUT_TXT] = got_first[VIS:]
    unit_ref[2 * CUT_TXT : 3 * CUT_TXT] = got_second[VIS:]
    unit_ref[3 * CUT_TXT :] = got_b[:CUT_TXT]
    grad_ref[:CUT_TXT] = own_text[CUT_TXT:]
    grad_ref[CUT_TXT : 3 * CUT_TXT] = mates_grad[...]
    grad_ref[3 * CUT_TXT :] = got_b[CUT_TXT:]
    bias = jnp.where(core_index() == 0, near_small[0:1].astype(f32), b_in[...].astype(f32))
    for slot in range(2):
        pltpu.make_async_copy(w_in, held.at[slot], sems.at[slot]).wait()
    row_pass(unit_ref[...], grad_ref[...], held.at[0], bias, held.at[1], act_ref, pre_ref, 0)
    back = times_transpose(pre_ref[...], held[0])
    out = matmul(act_ref[...], held[1])
    for piece, (target, base) in enumerate(((home_ref, 0), (mates_ref, 0), (mates_ref, 2 * CUT_TXT))):
        at = slice(piece * CUT_TXT, (piece + 1) * CUT_TXT)
        target[base : base + CUT_TXT] = back[at].astype(target.dtype)
        target[base + CUT_TXT : base + 2 * CUT_TXT] = out[at].astype(target.dtype)
    b_back[...] = back[3 * CUT_TXT :].astype(bf16)
    b_out[...] = out[3 * CUT_TXT :].astype(bf16)


def text_rows(*args):
    outs = [((2 * CUT_TXT, D), f32), ((4 * CUT_TXT, D), bf16)] + [((CUT_TXT, D), bf16)] * 2
    outs += [((4 * CUT_TXT, D), bf16)] * 4
    scratch = [pltpu.VMEM((2, D, D), bf16), pltpu.SemaphoreType.DMA((2,))]
    return call(text_kernel, outs, *args, scratch=scratch, any_from=7, micros=5, mebibytes=20)


class Outputs:
    def __init__(self, keep, away, blocks, sems):
        self.keep, self.away, self.blocks, self.sems, self.pending = keep, away, blocks, sems, []

    def put(self, index, value, kind):
        slot = len(self.pending) % 2
        if len(self.pending) >= 2:
            self.pending[-2].wait()
        self.blocks[slot] = value.astype(bf16)
        rows = pl.ds(index * D, D)
        kept = core_index() == kind

        @pl.when(kept)
        def _():
            pltpu.make_async_copy(self.blocks.at[slot], self.keep.at[rows], self.sems.at[slot]).start()

        @pl.when(jnp.logical_not(kept))
        def _():
            pltpu.make_async_copy(self.blocks.at[slot], self.away.at[rows], self.sems.at[slot]).start()

        self.pending.append(pltpu.make_async_copy(self.blocks.at[slot], self.keep.at[rows], self.sems.at[slot]))

    def finish(self):
        for copy in self.pending[-2:]:
            copy.wait()


def column_sum(value):
    return jnp.sum(value.astype(f32), axis=0, keepdims=True)


def near_grads_kernel(
    own_first, own_second, got_first, got_second, grad_own, grad_mate, act_own, act_mate, pre_own, pre_mate,
    unit_text, grad_text, act_text, pre_text, keep_ref, away_ref, units, grads, bias_ref, blocks, sems, acts, pres, in_sems,
):
    near = slice(0, D)
    loads = []

    def load(source, target):
        loads.append(pltpu.make_async_copy(source, target, in_sems.at[len(loads)]))
        loads[-1].start()

    for piece, source in enumerate((own_first, own_second, got_first, got_second)):
        load(source.at[:VIS], units.at[piece * VIS : (piece + 1) * VIS])
    for own, mate, total in ((pre_own, pre_mate, pres), (act_own, act_mate, acts)):
        load(own.at[:, near], total.at[:CUT])
        load(mate.at[:, near], total.at[CUT:])
    load(grad_own, grads.at[:CUT])
    load(grad_mate, grads.at[CUT:])
    outputs = Outputs(keep_ref, away_ref, blocks, sems)
    outputs.put(1, contract_rows(unit_text[...], pre_text[...]), 0)
    outputs.put(1, contract_rows(act_text[...], grad_text[...]), 1)
    for copy in loads[:6]:
        copy.wait()
    outputs.put(0, contract_rows(units[...], pres[...]), 0)
    for copy in loads[6:]:
        copy.wait()
    outputs.put(0, contract_rows(acts[...], grads[...]), 1)
    at_y = lax.axis_index("ffn")
    bias_ref[...] = jnp.zeros_like(bias_ref)
    bias_ref[pl.ds(at_y, 1)] = column_sum(pres[...])
    bias_ref[pl.ds(4 + at_y, 1)] = column_sum(pre_text[...])
    outputs.finish()


def far_grads_kernel(
    units, grads, act_own, act_mate, pre_own, pre_mate, bias_in, keep_ref, away_ref, bias_ref, blocks, sems, acts, pres, in_sems
):
    far = slice(D, 2 * D)
    loads = []
    for own, mate, total in ((pre_own, pre_mate, pres), (act_own, act_mate, acts)):
        for source, target in ((own, total.at[:CUT]), (mate, total.at[CUT:])):
            loads.append(pltpu.make_async_copy(source.at[:, far], target, in_sems.at[len(loads)]))
            loads[-1].start()
    outputs = Outputs(keep_ref, away_ref, blocks, sems)
    for copy in loads[:2]:
        copy.wait()
    outputs.put(0, contract_rows(units[...], pres[...]), 0)
    for copy in loads[2:]:
        copy.wait()
    outputs.put(0, contract_rows(acts[...], grads[...]), 1)
    bias_ref[...] = bias_in[...]
    bias_ref[pl.ds(lax.rem(lax.axis_index("ffn") + 2, 4), 1)] = column_sum(pres[...])
    outputs.finish()


def near_grads(*args):
    rows = jax.ShapeDtypeStruct((2 * CUT, D), bf16)
    return pl.pallas_call(
        near_grads_kernel,
        out_shape=[jax.ShapeDtypeStruct((2 * D, D), bf16)] * 2 + [rows, rows, jax.ShapeDtypeStruct((8, D), f32)],
        in_specs=[ANY] * 10 + [VMEM] * 4,
        out_specs=[ANY, ANY] + [VMEM] * 3,
        scratch_shapes=[pltpu.VMEM((2, D, D), bf16), pltpu.SemaphoreType.DMA((2,))]
        + [pltpu.VMEM((2 * CUT, D), bf16)] * 2
        + [pltpu.SemaphoreType.DMA((10,))],
        cost_estimate=cost(1),
        compiler_params=params(24),
    )(*args)


def far_grads(*args):
    return pl.pallas_call(
        far_grads_kernel,
        out_shape=[jax.ShapeDtypeStruct((D, D), bf16)] * 2 + [jax.ShapeDtypeStruct((8, D), f32)],
        in_specs=[VMEM] * 2 + [ANY] * 4 + [VMEM],
        out_specs=[ANY, ANY, VMEM],
        scratch_shapes=[pltpu.VMEM((2, D, D), bf16), pltpu.SemaphoreType.DMA((2,))]
        + [pltpu.VMEM((2 * CUT, D), bf16)] * 2
        + [pltpu.SemaphoreType.DMA((4,))],
        cost_estimate=cost(1),
        compiler_params=params(24),
    )(*args)


def text_sum(own_ref, got_first, got_second, b_ref, item):
    txt = slice(VIS + item * TXT, VIS + (item + 1) * TXT)
    total = own_ref[CUT + item * TXT : CUT + (item + 1) * TXT] + b_ref[item * TXT : (item + 1) * TXT].astype(f32)
    return total + got_first[txt].astype(f32) + got_second[txt].astype(f32)


def branch_kernel(
    own_ref, got_first, got_second, b_ref, modal_ref, cot_ref, hid_ref, att_ref, gain_ref, wo_ref,
    hidden_ref, gatt_ref, dwo_ref, sum_ref,
):
    gain = vector(gain_ref)
    sums = [0.0, 0.0, 0.0]
    for item in range(ITEMS):
        at = slice(item * SEQ, (item + 1) * SEQ)
        vis = slice(item * VIS, (item + 1) * VIS)
        vision = own_ref[vis] + (got_first, got_second)[item][:VIS].astype(f32)
        text = text_sum(own_ref, got_first, got_second, b_ref, item)
        grad_unit = unpack_item(vision, text, *slots_of(modal_ref[item : item + 1])).astype(bf16).astype(f32)
        _, hat, scaled = norm_forward(hid_ref[at], 1.0, 0.0)
        grad_norm, grad_gain, grad_shift = norm_backward(grad_unit, hat, scaled, gain)
        grad_hidden = cot_ref[at].astype(f32) + grad_norm
        hidden_ref[at] = grad_hidden
        branch = grad_hidden.astype(bf16)
        gatt_ref[at] = branch
        sums[0] += grad_gain
        sums[1] += grad_shift
        sums[2] += jnp.sum(branch.astype(f32), axis=0, keepdims=True)
    dwo_ref[...] = contract_rows(att_ref[...], gatt_ref[...]).astype(bf16)
    gatt_ref[...] = times_transpose(gatt_ref[...], wo_ref[...]).astype(bf16)
    sum_ref[...] = jnp.concatenate(sums, axis=0)


def scores_kernel(q_ref, k_ref, v_ref, p_ref, gatt_ref, gq_ref, gk_ref, gv_ref):
    low_half = lax.broadcasted_iota(jnp.int32, (1, 128), 1) < HEAD_DIM
    for pair in range(HEADS // 2):
        lanes = slice(pair * 128, (pair + 1) * 128)
        q, k, v, g = q_ref[:, lanes], k_ref[:, lanes], v_ref[:, lanes], gatt_ref[:, lanes]
        gq = gk = gv = 0.0
        for half in range(2):
            mine = low_half if half == 0 else jnp.logical_not(low_half)
            mask = lambda a: jnp.where(mine, a, 0).astype(bf16)
            low = p_ref[0, 2 * pair + half]
            probs = low.astype(f32)
            inner = times_transpose(mask(g), v) * probs
            scores = (inner - probs * jnp.sum(inner, axis=-1, keepdims=True)).astype(bf16)
            gv += contract_rows(low, mask(g))
            gq += matmul(scores, mask(k))
            gk += contract_rows(scores, mask(q))
        gq_ref[:, lanes] = (gq * 0.125).astype(bf16)
        gk_ref[:, lanes] = gk.astype(bf16)
        gv_ref[:, lanes] = gv.astype(bf16)


def backward_scores(q, k, v, p, gatt):
    block = pl.BlockSpec((SEQ, D), lambda i: (i, 0))
    heads = pl.BlockSpec((1, HEADS, SEQ, SEQ), lambda i: (i, 0, 0, 0))
    return pl.pallas_call(
        scores_kernel,
        grid=(ITEMS,),
        out_shape=[jax.ShapeDtypeStruct((ROWS, D), bf16)] * 3,
        in_specs=[block] * 3 + [heads, block],
        out_specs=[block] * 3,
        cost_estimate=cost(25),
        compiler_params=params(20),
    )(q, k, v, p, gatt)


def shared_kernel(
    tok_ref, gain1, shift1, gq_ref, gk_ref, gv_ref, wq_ref, wk_ref, wv_ref, hidden_ref, dwo_ref, sums_two, grad_live, bias_rows,
    tok_out, keep_ref, away_ref,
):
    gain = vector(gain1)
    unit, hat, scaled = norm_forward(tok_ref[...].astype(f32), gain, vector(shift1))
    low = unit.astype(bf16)
    dwq = contract_rows(low, gq_ref[...]).astype(bf16)
    dwk = contract_rows(low, gk_ref[...]).astype(bf16)
    dwv = contract_rows(low, gv_ref[...]).astype(bf16)
    back = times_transpose(gq_ref[...], wq_ref[...]) + times_transpose(gk_ref[...], wk_ref[...]) + times_transpose(gv_ref[...], wv_ref[...])
    grad_norm, grad_gain, grad_shift = norm_backward(back, hat, scaled, gain)
    tok_out[...] = (hidden_ref[...] + grad_norm).astype(bf16)
    total = lambda ref: jnp.sum(ref[...].astype(f32), axis=0, keepdims=True)
    rows = [grad_gain, grad_shift, total(gq_ref), total(gv_ref), sums_two[...], grad_live[...], bias_rows[...]]
    vec = jnp.concatenate(rows + [jnp.zeros((VEC - 17, D), f32)], axis=0).astype(bf16)

    def put(mine, other):
        mine[:D] = dwq
        mine[D : 2 * D] = dwk
        other[:D] = dwv
        other[D : 2 * D] = dwo_ref[...]
        mine[2 * D :] = vec
        other[2 * D :] = vec

    @pl.when(core_index() == 0)
    def _():
        put(keep_ref, away_ref)

    @pl.when(core_index() == 1)
    def _():
        put(away_ref, keep_ref)


def mixed_kernel(own_ref, got_first, got_second, b_ref, modal_ref, hid_ref, b_out, near_small, out_ref):
    first = core_index() == 0
    mine, other = b_out[...].astype(f32), near_small[1:2].astype(f32)
    bias_vision, bias_text = jnp.where(first, mine, other), jnp.where(first, other, mine)
    for item in range(ITEMS):
        at = slice(item * SEQ, (item + 1) * SEQ)
        vis = slice(item * VIS, (item + 1) * VIS)
        vision = own_ref[vis] + (got_first, got_second)[item][:VIS].astype(f32) + bias_vision
        text = text_sum(own_ref, got_first, got_second, b_ref, item) + bias_text
        rows = unpack_item(vision, text, *slots_of(modal_ref[item : item + 1])).astype(bf16).astype(f32)
        out_ref[at] = (hid_ref[at] + rows).astype(bf16)


def split_kernel(count, size, axes, *refs):
    ins, outs, total = refs[:count], refs[count:-1], refs[-1]
    extra = total.shape[0] - 4 * size
    total[...] = sum(ref[: 4 * size + extra].astype(f32) for ref in ins).astype(bf16)
    me = place(axes)
    for step, out in zip((0, 1, 3, 2), outs):
        at = pl.multiple_of(lax.rem(me + step, 4) * size, 16)
        out[:size] = total[pl.ds(at, size)]
        if extra:
            out[size:] = total[4 * size :]


def split(pieces, size, extra, axes):
    outs = [((size + extra, D), bf16)] * 4
    scratch = [pltpu.VMEM((4 * size + extra, D), bf16)]
    return call(functools.partial(split_kernel, len(pieces), size, axes), outs, *pieces, scratch=scratch)


def block_steps(size):
    first = core_index() == 0
    return jnp.where(first, 4 * size, size), jnp.where(first, size, 4 * size)


def expert_split_kernel(size, near_keep, near_got, far_keep, far_got, *refs):
    outs, total = refs[:-1], refs[-1]
    near = (near_keep[...].astype(f32) + near_got[...].astype(f32)).astype(bf16)
    total[:D] = near[:D]
    total[D : 2 * D] = (far_keep[...].astype(f32) + far_got[...].astype(f32)).astype(bf16)
    total[2 * D :] = near[D:]
    me = place("xz")
    outer, inner = block_steps(size)
    half = 6 * size
    for step in (0, 1, 3, 2):
        base = lax.rem(me + step, 4) * outer
        for matrix in range(3):
            for block in range(4):
                rows = total[pl.ds(pl.multiple_of(base + matrix * D + block * inner, 16), size)]
                to = (matrix * 4 + block) * size
                if step == 2:
                    out, to = (outs[1], 2 * half + to) if to < half else (outs[2], half + to)
                else:
                    out = outs[{0: 0, 1: 1, 3: 2}[step]]
                out[to : to + size] = rows


EXP = D // 16


def expert_second_kernel(mine, below, above, below_half, above_half, *refs):
    outs, total = refs[:-1], refs[-1]
    size = mine.shape[0]
    for at, far in ((slice(0, size // 2), below_half), (slice(size // 2, size), above_half)):
        total[at] = (mine[at].astype(f32) + below[at].astype(f32) + above[at].astype(f32) + far[...].astype(f32)).astype(bf16)
    me = place("zx")
    for step, out in zip((0, 1, 3, 2), outs):
        index = lax.rem(me + step, 4)
        for matrix in range(3):
            at = pl.multiple_of((matrix * 4 + index) * EXP, 16)
            out[matrix * EXP : (matrix + 1) * EXP] = total[pl.ds(at, EXP)]


def expert_third_kernel(*refs):
    ins, outs = refs[:4], refs[4:]
    total = sum(ref[...].astype(f32) for ref in ins).astype(bf16)
    for matrix, out in enumerate(outs):
        out[...] = total[matrix * EXP : (matrix + 1) * EXP]


def expert_keep_kernel(near, far, text, keep, away):
    first = core_index() == 0
    vision, language = near[...].astype(f32) + far[...].astype(f32), text[...].astype(f32)
    keep[...] = jnp.where(first, vision, language).astype(bf16)
    away[...] = jnp.where(first, language, vision).astype(bf16)


def sum_kernel(*refs):
    ins, out = refs[:4], refs[4]
    out[...] = sum(ref[...].astype(f32) for ref in ins).astype(bf16)


def fourth_kernel(*refs):
    ins, (keep, got, out, vec) = refs[:4], refs[4:]
    total = sum(ref[...].astype(f32) for ref in ins)
    out[: 2 * EXP] = total[: 2 * EXP].astype(bf16)
    vec[...] = total[2 * EXP :]
    first = core_index() == 0
    k, g = keep[...].astype(f32), got[...].astype(f32)
    out[2 * EXP : 3 * EXP] = jnp.where(first, k, g).astype(bf16)
    out[3 * EXP :] = jnp.where(first, g, k).astype(bf16)


def fifth_kernel(mine, first, third, second, shared, expert):
    me = place("xz")
    for step, piece in zip((0, 1, 3, 2), (mine, first, third, second)):
        index = lax.rem(me + 4 - step, 4)
        shared[pl.ds(pl.multiple_of(index * 2 * EXP, 16), 2 * EXP)] = piece[: 2 * EXP]
        at = pl.multiple_of(index * EXP, 16)
        expert[pl.ds(at, EXP)] = piece[2 * EXP : 3 * EXP]
        expert[pl.ds(4 * EXP + at, EXP)] = piece[3 * EXP :]


def expert_finish_kernel(mine, first, third, second_in, second_out, w_in, w_out):
    outer, inner = block_steps(EXP)
    me = place("zx")
    half = 4 * EXP
    pieces = [(0, mine[:half], mine[half:]), (1, first[:half], first[half:]), (3, third[:half], third[half:])]
    for step, low_in, low_out in pieces + [(2, second_in[...], second_out[...])]:
        base = lax.rem(me + 4 - step, 4) * inner
        for block in range(4):
            at = pl.ds(pl.multiple_of(base + block * outer, 16), EXP)
            w_in[at] = low_in[block * EXP : (block + 1) * EXP].astype(f32)
            w_out[at] = low_out[block * EXP : (block + 1) * EXP].astype(f32)


def join_kernel(axes, *refs):
    ins, out = refs[:4], refs[4]
    size = out.shape[0] // 4
    me = place(axes)
    for step, piece in zip((0, 1, 3, 2), ins):
        at = pl.multiple_of(lax.rem(me + 4 - step, 4) * size, 16)
        out[pl.ds(at, size)] = piece[:size]


def join(piece, got, axes, size=None):
    return call(functools.partial(join_kernel, axes), [((4 * (size or piece.shape[0]), D), bf16)], piece, *got)[0]


def finish_kernel(mine, other, vec, wq, wk, wv, wo, g1, s1, bq, bv, g2, s2, bo, b_in, b_out):
    first = core_index() == 0
    for low, high, at in ((wq, wv, 0), (wk, wo, 1)):
        m, o = mine[at].astype(f32), other[at].astype(f32)
        low[...] = jnp.where(first, m, o)
        high[...] = jnp.where(first, o, m)

    @pl.when(pl.program_id(0) == 0)
    def _():
        for ref, row in ((g1, 0), (s1, 1), (bq, 2), (bv, 3), (g2, 4), (s2, 5), (bo, 6)):
            ref[...] = vec[row]
        b_in[...] = vec[pl.ds(9 + 4 * core_index() + lax.axis_index("ffn"), 1)]
        b_out[...] = vec[pl.ds(7 + core_index(), 1)]


def finish(mine, other, vec):
    steps = 4
    size = D // steps
    pair = pl.BlockSpec((2, size, D), lambda i: (0, i, 0))
    block = pl.BlockSpec((size, D), lambda i: (i, 0))
    return pl.pallas_call(
        finish_kernel,
        grid=(steps,),
        out_shape=[jax.ShapeDtypeStruct((D, D), f32)] * 4
        + [jax.ShapeDtypeStruct((D,), f32)] * 7
        + [jax.ShapeDtypeStruct((1, D), f32)] * 2,
        in_specs=[pair, pair, VMEM],
        out_specs=[block] * 4 + [VMEM] * 9,
        cost_estimate=cost(5),
        compiler_params=params(12),
    )(mine.reshape(2, D, D), other.reshape(2, D, D), vec)


def body(
    tokens,
    cotangent,
    modality,
    ln1_gain,
    ln1_shift,
    w_query,
    b_query,
    w_key,
    w_value,
    b_value,
    w_attn_out,
    b_attn_out,
    ln2_gain,
    ln2_shift,
    w_in,
    b_in,
    w_out,
    b_out,
):
    flat_tokens = tokens.reshape(ROWS, D)
    flat_cot = cotangent.reshape(ROWS, D)
    w_in, w_out = w_in[0], w_out[0]

    part_in, part_out, cot_first, cot_second, small, grad_text = parts(w_in, w_out, flat_cot, b_in, b_out, modality)
    part_in = send(part_in, lambda x, z, c, y: (x, z, 0, (y + 2) % 4) if c == 0 else None)
    part_out = send(part_out, lambda x, z, c, y: (x, z, 1, (y + 2) % 4) if c == 0 else None)

    cot_first, cot_second = swap_pair(cot_first), swap_other(cot_second)

    vectors = (ln1_gain, ln1_shift, b_query, b_value, b_attn_out, ln2_gain, ln2_shift)
    query, key, value, probs, attended, hidden_one, own_first, own_second, text_own = forward_attention(
        flat_tokens, modality, vectors, (w_query, w_key, w_value, w_attn_out), grad_text
    )
    sent_first, sent_second, text_own = tie((own_first, own_second, text_own), cot_first, cot_second)
    got_first, got_second, got_b = swap_pair(sent_first), swap_other(sent_second), swap_far(text_own)
    near_in, near_out = swap_core(tie(w_in, own_first)), swap_core(tie(w_out, own_first))
    far_part = jnp.where(core_index() == 0, *tie((part_in, part_out), own_first))
    far_got = shifts([far_part] * 3, "xz")
    near_small = swap_core(tie(small, far_got[2]))
    grad_own, grad_live = call(pack_kernel, [((CUT, D), bf16), ((2, D), f32)], tie(flat_cot, own_first), modality, micros=2)
    grad_mate, text_mate = call(pack_mates_kernel, [((CUT, D), bf16), ((2 * CUT_TXT, D), bf16)], cot_first, tie(cot_second, own_first))
    far_got = tie(far_got, got_first, got_second, got_b, near_small, grad_own, grad_mate)
    far_mine = join(far_part, far_got, "xz", D // 4)
    far_other = swap_core(far_mine)

    text_weights = (w_in, w_out, near_in, near_out)
    vision_weights = text_weights + (far_mine, far_other)
    text_home, text_mates, text_back, text_out, units_text, grads_text, text_act, text_pre = text_rows(
        text_own, got_first, got_second, got_b, text_mate, b_in, near_small, *text_weights
    )
    got_text = swap_far(text_back)
    smalls = (b_in, far_part, near_small)
    back_first, back_second, out_first, out_second, mate_act, mate_pre = vision_rows(
        True, (got_first, got_second), grad_mate, text_mates, smalls, vision_weights
    )
    back_first, back_second = swap_pair(back_first), swap_other(back_second)
    own_back, own_out, own_act, own_pre = vision_rows(
        False, (own_first, own_second), tie(grad_own, grad_mate, mate_act), text_home, smalls, vision_weights
    )

    near_keep, near_away, units, grads, bias_rows = near_grads(
        own_first, own_second, got_first, got_second, grad_own, grad_mate, own_act, mate_act, own_pre, mate_pre,
        units_text, grads_text, text_act, text_pre,
    )
    far_keep, far_away, bias_rows = far_grads(units, grads, own_act, mate_act, own_pre, mate_pre, bias_rows)
    near_away_got = swap_core(tie(near_away, back_first, back_second, got_text))

    grad_hidden, grad_attended, grad_w_attn_out, sums_two = call(
        branch_kernel,
        [((ROWS, D), f32), ((ROWS, D), bf16), ((D, D), bf16), ((3, D), f32)],
        own_back, tie(back_first, far_keep), back_second, got_text, modality, flat_cot, hidden_one, attended, ln2_gain, w_attn_out,
        micros=100, mebibytes=20,
    )
    far_away_got = swap_core(tie(far_away, back_first, back_second, got_text))
    out_first, out_second = tie((out_first, out_second), back_first, back_second)
    out_first, out_second = swap_pair(out_first), swap_other(out_second)
    got_text_out = swap_far(tie(text_out, back_first, back_second))
    expert_pieces = call(
        functools.partial(expert_split_kernel, EXP),
        [((12 * EXP, D), bf16)] + [((18 * EXP, D), bf16)] * 2,
        near_keep, near_away_got, far_keep, tie(far_away_got, grad_attended),
        scratch=[pltpu.VMEM((3 * D, D), bf16)], micros=2, mebibytes=20,
    )
    expert_got = [shift(piece, "xz", step) for piece, step in zip(expert_pieces[1:], (1, 3))]
    grad_query, grad_key, grad_value = backward_scores(query, key, value, probs, tie(grad_attended, *expert_pieces))
    grad_tokens, shared_keep, shared_away = call(
        shared_kernel,
        [((ROWS, D), bf16)] + [((2 * D + VEC, D), bf16)] * 2,
        flat_tokens, ln1_gain, ln1_shift, grad_query, grad_key, grad_value, w_query, w_key, w_value,
        grad_hidden, grad_w_attn_out, sums_two, grad_live, bias_rows,
        micros=11, mebibytes=28,
    )

    expert_relay = [shift(piece[12 * EXP :], "xz", step) for piece, step in zip(expert_got, (1, 3))]
    shared_got = swap_core(tie(shared_away, *expert_got, out_first, out_second, got_text_out))
    shared_pieces = split([shared_keep, shared_got], 2 * D // 4, VEC, "yx")
    shared_got = shifts(shared_pieces[1:], "yx")
    expert_pieces = call(
        expert_second_kernel,
        [((3 * EXP, D), bf16)] * 4,
        expert_pieces[0], *tie(expert_got, *shared_pieces), *expert_relay,
        scratch=[pltpu.VMEM((12 * EXP, D), bf16)],
    )
    expert_got = shifts(expert_pieces[1:], "zx")
    shared_pieces = split([shared_pieces[0]] + tie(shared_got, *expert_got[:2]), 2 * EXP, VEC, "xz")
    shared_got = shifts(shared_pieces[1:], "xz")
    near, far, text = call(expert_third_kernel, [((EXP, D), bf16)] * 3, expert_pieces[0], *expert_got)
    far = swap_far(far)
    size = 2 * EXP + VEC
    (shared_total,) = call(sum_kernel, [((size, D), bf16)], shared_pieces[0], *tie(shared_got, far))
    shared_got = shifts([shared_total] * 3, "zy")
    expert_keep, expert_away = call(expert_keep_kernel, [((EXP, D), bf16)] * 2, near, far, text)
    low, vec = call(
        fourth_kernel,
        [((4 * EXP, D), bf16), ((VEC, D), f32)],
        shared_total, *shared_got, expert_keep, swap_core(expert_away),
    )
    shared_sum, expert_sum = call(
        fifth_kernel, [((8 * EXP, D), bf16)] * 2, low, *shifts([low] * 3, "xz")
    )
    shared_got = shifts([shared_sum] * 3, "yx")
    expert_got = [shift(expert_sum, "zx", step) for step in (1, 3)]
    expert_relay = [shift(expert_got[0][: 4 * EXP], "zx", 1), shift(expert_got[1][4 * EXP :], "zx", 3)]
    shared_sum = join(shared_sum, shared_got, "yx")
    shared_sum = tie(shared_sum, *expert_got)
    outs = finish(shared_sum, swap_core(shared_sum), vec)
    d_query, d_key, d_value, d_out, d_gain1, d_shift1, d_bq, d_bv, d_gain2, d_shift2, d_bo, d_b_in, d_b_out = outs
    grad_w_in, grad_w_out = call(expert_finish_kernel, [((D, D), f32)] * 2, tie(expert_sum, d_query), *expert_got, *expert_relay)
    (mixed,) = call(
        mixed_kernel,
        [((ROWS, D), bf16)],
        own_out, out_first, out_second, got_text_out, modality, hidden_one, b_out, near_small,
        micros=4, mebibytes=16,
    )
    return (
        mixed.reshape(tokens.shape),
        grad_tokens.reshape(tokens.shape),
        d_gain1,
        d_shift1,
        d_query,
        d_bq,
        d_key,
        d_value,
        d_bv,
        d_out,
        d_bo,
        d_gain2,
        d_shift2,
        grad_w_in[None],
        d_b_in,
        grad_w_out[None],
        d_b_out,
    )


def solution(mesh):
    items = P(AXES, None, None)
    expert_specs = (P("expert", None, "ffn"), P("expert", "ffn"), P("expert", "ffn", None), P("expert", None))
    return jax.shard_map(
        body,
        mesh=mesh,
        in_specs=(items, items, P(AXES, None)) + (P(),) * 11 + expert_specs,
        out_specs=(items, items) + (P(),) * 11 + expert_specs,
        check_vma=False,
    )
```
